32 devices in a mesh: dp: 4 (over x, core), tensor: 8 (over z, y).
Axes of the slice: x: 2, y: 2, z: 4, core: 2. Of those that a mesh axis runs over, the one named last changes fastest.
Arguments:
- words: bfloat16 [12, 768, 4096], P('dp', 'tensor'), may hold values from -6 to 6
- w_in: bfloat16 [3072, 768], P('tensor'), may hold values from -0.21875 to 0.21875
- b_in: float32 [3072], P('tensor'), may hold values from -3 to 3
- w_out: bfloat16 [3072, 768], P('tensor'), may hold values from -0.109375 to 0.109375
- b_out: float32 [768], P('tensor'), may hold values from -3 to 3
- gain_one: float32 [768], P('tensor'), may hold values from 0.5 to 1.5
- shift_one: float32 [768], P('tensor'), may hold values from -2 to 2
- gain_two: float32 [768], P('tensor'), may hold values from 0.5 to 1.5
- shift_two: float32 [768], P('tensor'), may hold values from -2 to 2
- cotangent: bfloat16 [12, 768, 4096], P('dp', 'tensor'), may hold values from -6 to 6
- valid: int32 [12], P('dp'), may hold values 0 or 1
Outputs:
- activations: bfloat16 [12, 768, 4096], P('dp', 'tensor')
- grad_words: float32 [12, 768, 4096], P('dp', 'tensor')
- grad_w_in: float32 [3072, 768], P('tensor')
- grad_b_in: float32 [3072], P('tensor')
- grad_w_out: float32 [3072, 768], P('tensor')
- grad_b_out: float32 [768], P('tensor')
- grad_gain_one: float32 [768], P('tensor')
- grad_shift_one: float32 [768], P('tensor')
- grad_gain_two: float32 [768], P('tensor')
- grad_shift_two: float32 [768], P('tensor')
The draws below stay inside these ranges and needn't reach their ends.
Inputs may be any that keep to these rules, and one draw needn't show every extreme that they name: `valid`: 1 marks a real sequence, 0 a padding sequence whose output gradient is ignored.
All inputs are finite; a program needn't handle non-finite values. No bound on the sum of `valid` on one device may be relied on, other than what follows from the above.
Results may differ from the reference program's by a relative error of at most 0.018.
Values may be sent and summed in bfloat16 or wider, within the bound.
A program may use at most 128 MiB of HBM per device.

```python
import math
import jax
import jax.numpy as jnp
from jax import lax

D = 768
FF = 3072
ROOT = 64
SEQ = 4096
SEQS = 12


def touch_ends(array, own_key, least, top_value):
    shape = array.shape
    place = [jax.random.randint(jax.random.fold_in(own_key, axis), (), 0, shape[axis]) for axis in range(len(shape))]
    array = array.at[tuple(place)].set(least)
    longest = shape.index(max(shape))
    place[longest] = (place[longest] + 1) % shape[longest]
    return array.at[tuple(place)].set(top_value)


def steps_of(stream_key, extent, pieces, low, largest):
    level, own = 1.0, jax.random.fold_in(stream_key, 6)
    for axis_at, parts in pieces:
        draws = jnp.exp(jax.random.uniform(jax.random.fold_in(own, axis_at), (parts,), jnp.float32, low / len(pieces), largest / len(pieces)))
        level = level * jnp.repeat(draws, extent[axis_at] // parts).reshape([-1 if axis == axis_at else 1 for axis in range(len(extent))])
    return level


def noise(rng, shape, scale, most, shards=(), held_as=jnp.bfloat16):
    values = jax.random.normal(rng, shape, jnp.float32) * scale
    if len(shards) > 0:
        values = steps_of(rng, shape, shards, -0.22, 0.18) * values
    return jnp.clip(values, min=-most, max=most).astype(held_as)


def setup_inputs(seed: int = 0) -> dict:
    seeds = jax.random.split(jax.random.key(seed), 12)
    words = noise(seeds[0], (SEQS, D, SEQ), 1.0, 6.0, ((0, 4), (1, 8)))
    w_in = noise(seeds[1], (FF, D), D ** -0.5, 0.21875, ((0, 8),))
    b_in = noise(seeds[2], (FF,), 0.5, 3.0, ((0, 8),), jnp.float32)
    w_out = noise(seeds[3], (FF, D), FF ** -0.5, 0.109375, ((0, 8),))
    b_out = noise(seeds[4], (D,), 0.5, 3.0, ((0, 8),), jnp.float32)
    gain_one = jnp.clip(1.0 + 0.1 * jax.random.normal(seeds[5], (D,), jnp.float32), 0.5, 1.5)
    shift_one = noise(seeds[6], (D,), 0.3, 2.0, ((0, 8),), jnp.float32)
    gain_two = jnp.clip(1.0 + 0.1 * jax.random.normal(seeds[7], (D,), jnp.float32), 0.5, 1.5)
    shift_two = noise(seeds[8], (D,), 0.3, 2.0, ((0, 8),), jnp.float32)
    cotangent = noise(seeds[9], (SEQS, D, SEQ), 1.0, 6.0, ((0, 4), (1, 8)))
    valid = touch_ends((jax.random.randint(seeds[10], (SEQS,), 0, 16) < 15).astype(jnp.int32), jax.random.fold_in(seeds[10], 1), 0, 1)
    return dict(words=words, w_in=w_in, b_in=b_in, w_out=w_out, b_out=b_out, gain_one=gain_one, shift_one=shift_one, gain_two=gain_two, shift_two=shift_two, cotangent=cotangent, valid=valid)


@jax.custom_vjp
def low(v):
    return lax.optimization_barrier(v.astype(jnp.bfloat16)).astype(jnp.float32)

@jax.custom_vjp
def low_back(v):
    return v

def low_keep(v):
    return (low(v), None)

def low_pass(kept, grad):
    return (grad,)

def back_keep(v):
    return (v, None)

def back_low(kept, grad):
    return (low(grad),)
low.defvjp(low_keep, low_pass)
low_back.defvjp(back_keep, back_low)
EPSILON = 1e-12
HIGHEST_PRECISION = lax.Precision.HIGHEST

def angles(left_ids, right_ids, period):
    product_index = left_ids[:, None] * right_ids[None, :] % period
    return product_index.astype(jnp.float32) * (2.0 * math.pi / period)

def layer_norm(values, gain, shift):
    center = lax.optimization_barrier(jnp.mean(values, axis=-1, keepdims=True))
    offsets = values - center
    spread = lax.optimization_barrier(jnp.mean(offsets * offsets, axis=-1, keepdims=True))
    return offsets * lax.rsqrt(spread + EPSILON) * gain + shift

def forward(tokens, w_in, b_in, w_out, b_out, gain_one, shift_one, gain_two, shift_two):
    length = tokens.shape[0]
    model_width = tokens.shape[1]
    hidden_ids = jnp.arange(model_width, dtype=jnp.int32)
    hidden_angle = angles(hidden_ids, hidden_ids, model_width)
    cos_hidden = low(jnp.cos(hidden_angle))
    sin_hidden = low(-jnp.sin(hidden_angle))
    real_part = jnp.dot(tokens, cos_hidden, precision=HIGHEST_PRECISION)
    imag_part = jnp.dot(tokens, sin_hidden, precision=HIGHEST_PRECISION)
    spectrum = low(low_back(jnp.stack([real_part, imag_part], axis=1)))
    spectrum = spectrum.reshape(ROOT, ROOT, 2, model_width)
    root_ids = jnp.arange(ROOT, dtype=jnp.int32)
    root_angle = angles(root_ids, root_ids, ROOT)
    cosine = low(jnp.cos(root_angle))
    sine_table = low(jnp.sin(root_angle))
    table_a = jnp.stack([jnp.stack([cosine, sine_table], axis=-1), jnp.stack([-sine_table, cosine], axis=-1)], axis=1)
    table_b = jnp.stack([cosine, sine_table], axis=-1)
    section_one = jnp.einsum('kpnq,nmqd->kmpd', table_a, spectrum, precision=HIGHEST_PRECISION)
    section_one = low_back(section_one)
    turn_angle = angles(root_ids, root_ids, length)
    turn_cos = jnp.cos(turn_angle)[:, :, None]
    turn_sin = jnp.sin(turn_angle)[:, :, None]
    real_turn = section_one[:, :, 0] * turn_cos + section_one[:, :, 1] * turn_sin
    imag_turn = section_one[:, :, 1] * turn_cos - section_one[:, :, 0] * turn_sin
    turned = low(jnp.stack([real_turn, imag_turn], axis=2))
    mixed_rows = jnp.einsum('anq,knqd->akd', table_b, turned, precision=HIGHEST_PRECISION)
    mixed_rows = low_back(mixed_rows).reshape(length, model_width)
    first_sum = tokens + mixed_rows * (1.0 / math.sqrt(length * model_width))
    normed = layer_norm(first_sum, gain_one, shift_one)
    inner_sum = low_back(jnp.dot(low(normed), w_in.T, precision=HIGHEST_PRECISION)) + b_in
    active = low(jax.nn.gelu(inner_sum, approximate=True))
    outer_sum = low_back(jnp.dot(active, w_out, precision=HIGHEST_PRECISION)) + b_out
    return layer_norm(normed + outer_sum, gain_two, shift_two)

def forward_columns(columns_first, *weights):
    return forward(columns_first.T, *weights).T

def reference(words, w_in, b_in, w_out, b_out, gain_one, shift_one, gain_two, shift_two, cotangent, valid):
    weights = (w_in.astype(jnp.float32), b_in, w_out.astype(jnp.float32), b_out, gain_one, shift_one, gain_two, shift_two)
    empty_sums = tuple((jnp.zeros_like(weight) for weight in weights))

    def sequence_step(totals, inputs_now):
        tokens, grad_out, keep_flag = inputs_now
        outputs, pullback = jax.vjp(forward_columns, tokens.astype(jnp.float32), *weights)
        grads = pullback(grad_out.astype(jnp.float32) * keep_flag.astype(jnp.float32))
        totals = tuple((total + grad for total, grad in zip(totals, grads[1:])))
        return (totals, (outputs.astype(jnp.bfloat16), grads[0]))
    totals, (activations, grad_words) = lax.scan(sequence_step, empty_sums, (words, cotangent, valid))
    return (activations, grad_words, totals[0], totals[1], totals[2], totals[3], totals[4], totals[5], totals[6], totals[7])
```

```python
import math

import jax
import jax.numpy as jnp
import numpy as np
from jax import lax
from jax.experimental import pallas as pl
from jax.experimental.pallas import tpu as pltpu
from jax.sharding import PartitionSpec as P

EPSILON = 1e-12
MESH = pl.DeviceIdType.MESH
BF = jnp.bfloat16
F32 = jnp.float32


def token_tables(length, group):
    half = length // (2 * group)
    n = np.arange(length, dtype=np.int64)

    def wave(k):
        angle = (n[:, None] * k[None, :] % length) * (2.0 * math.pi / length)
        return np.cos(angle), np.sin(angle)

    cos, sin = wave(np.arange(length // 2))
    main = np.stack(
        [cos.reshape(length, group, half), sin.reshape(length, group, half)], axis=2
    ).reshape(length, length)
    edge_cos, edge_sin = wave(half * (np.arange(group) + 1))
    edge = np.zeros((length, 128))
    edge[:, 0 : 2 * group : 2] = edge_cos
    edge[:, 1 : 2 * group : 2] = np.where(np.abs(edge_sin) < 1e-9, 0.0, edge_sin)
    return main.astype(BF), edge.astype(BF)


def hidden_tables(width):
    ids = np.arange(width, dtype=np.int64)
    angle = (ids[:, None] * ids[None, :] % width) * (2.0 * math.pi / width)
    return np.cos(angle).astype(BF), np.sin(angle).astype(BF)


class Place:
    def __init__(self, n_dp, n_tensor):
        self.n_dp, self.n_tensor = n_dp, n_tensor
        self.slices = n_tensor // 2
        self.group = 2 * n_dp
        self.dp = lax.axis_index("dp")
        self.tensor = lax.axis_index("tensor")
        self.z = self.tensor // 2
        self.y = self.tensor % 2
        self.g = self.dp * 2 + self.y
        self.block = self.block_of(self.dp, self.y)

    def block_of(self, dp, y):
        return ((dp % (self.n_dp // 2)) * 2 + dp // (self.n_dp // 2)) * 2 + y

    def dp_of(self, z):
        return (z % 2) * (self.n_dp // 2) + z // 2

    def peer(self, offset):
        g = self.g ^ offset
        return (g // 2, self.z * 2 + g % 2), g


def start_all(moves):
    for src, dst, send, recv, device, own in moves:
        if device is None:
            pltpu.make_async_copy(src, dst, recv).start()
        elif own is None:
            pltpu.make_async_remote_copy(src, dst, send, recv, device, MESH).start()
        else:
            @pl.when(own)
            def _():
                pltpu.make_async_copy(src, dst, recv).start()

            @pl.when(jnp.logical_not(own))
            def _():
                pltpu.make_async_remote_copy(src, dst, send, recv, device, MESH).start()


def wait_sent(moves):
    for src, dst, send, recv, device, own in moves:
        if device is None:
            continue
        if own is None:
            pltpu.make_async_copy(src, src, send).wait()
        else:
            @pl.when(jnp.logical_not(own))
            def _():
                pltpu.make_async_copy(src, src, send).wait()


def wait_arrived(arrivals):
    for ref, recv in arrivals:
        pltpu.make_async_copy(ref, ref, recv).wait()


def greet(sources, n_targets):
    barrier = pltpu.get_barrier_semaphore()
    count = 0
    for device, own in sources:
        if own is None:
            pl.semaphore_signal(barrier, inc=1, device_id=device, device_id_type=MESH)
        else:
            @pl.when(jnp.logical_not(own))
            def _():
                pl.semaphore_signal(barrier, inc=1, device_id=device, device_id_type=MESH)
    total = 0
    for own in n_targets:
        total = total + (1 if own is None else jnp.where(own, 0, 1))
    pl.semaphore_wait(barrier, total)


ANY = pl.BlockSpec(memory_space=pl.ANY)


def exchange(body, ins, outs, n_sems, collective_id):
    return pl.pallas_call(
        body,
        out_shape=outs,
        in_specs=[ANY] * len(ins),
        out_specs=[ANY] * len(outs),
        scratch_shapes=[pltpu.SemaphoreType.DMA((n_sems,)), pltpu.SemaphoreType.DMA((n_sems,))],
        compiler_params=pltpu.CompilerParams(collective_id=collective_id, has_side_effects=True),
    )(*ins)


def on_device(
    words, w_in, b_in, w_out, b_out, gain_one, shift_one, gain_two, shift_two, cotangent, valid
):
    seqs, columns, length = words.shape
    width = w_in.shape[1]
    n_dp, n_tensor = lax.axis_size("dp"), lax.axis_size("tensor")
    assert n_tensor == 2 * n_dp
    group = 2 * n_dp
    half = length // (2 * group)
    mix_scale = 1.0 / math.sqrt(length * width)
    table, edge_table = token_tables(length, group)
    hid_cos, hid_sin = hidden_tables(width)

    def to_slice_body(x_ref, o_ref, send, recv):
        at = Place(n_dp, n_tensor)
        moves, sources = [], []
        target_dp = at.dp_of(at.z)
        for j in range(seqs):
            z = (at.dp + j) % at.slices
            own = jnp.logical_and(target_dp == at.dp, z == at.z)
            moves.append((x_ref.at[j], o_ref.at[j], send.at[j], recv.at[j], (target_dp, z * 2 + at.y), own))
            sources.append((((at.z - j + at.n_dp) % at.n_dp, at.block), own))
        greet(sources, [m[5] for m in moves])
        start_all(moves)
        wait_sent(moves)
        wait_arrived([(m[1], m[3]) for m in moves])

    (x_col,) = exchange(
        to_slice_body, [words], [jax.ShapeDtypeStruct(words.shape, BF)], seqs, 1
    )

    spectrum = jnp.einsum("jcl,lk->jck", x_col, table, preferred_element_type=F32).astype(BF)
    edges = jnp.einsum("jcl,lk->jck", x_col, edge_table, preferred_element_type=F32).astype(BF)

    def to_tokens_body(x_ref, u_ref, e_ref, xo_ref, uo_ref, eo_ref, send, recv):
        at = Place(n_dp, n_tensor)
        rows = pl.ds(pl.multiple_of(at.block * columns, 16), columns)
        moves, sources = [], []
        k = 0
        for offset in range(group):
            device, g = at.peer(offset)
            if offset == 0:
                device = None
            else:
                sources.append((device, None))
            first = pl.ds(pl.multiple_of(g * half, 128), half)
            last = pl.ds(pl.multiple_of(length - (g + 1) * half, 128), half)
            mine = pl.ds(pl.multiple_of(g * 2 * half, 128), 2 * half)
            for j in range(seqs):
                for src, dst in (
                    (x_ref.at[j, :, first], xo_ref.at[j, rows, pl.ds(0, half)]),
                    (x_ref.at[j, :, last], xo_ref.at[j, rows, pl.ds(half, half)]),
                    (u_ref.at[j, :, mine], uo_ref.at[j, rows]),
                    (e_ref.at[j], eo_ref.at[j, rows]),
                ):
                    moves.append((src, dst, send.at[k], recv.at[k], device, None))
                    k += 1
        greet(sources, [None] * len(sources))
        start_all(moves)
        wait_sent(moves)
        wait_arrived([(m[1], m[3]) for m in moves])

    x_tok, u_tok, e_tok = exchange(
        to_tokens_body,
        [x_col, spectrum, edges],
        [
            jax.ShapeDtypeStruct((seqs, width, 2 * half), BF),
            jax.ShapeDtypeStruct((seqs, width, 2 * half), BF),
            jax.ShapeDtypeStruct((seqs, width, 128), BF),
        ],
        group * seqs * 4,
        2,
    )

    def cot_body(c_ref, o_ref, send, recv):
        at = Place(n_dp, n_tensor)
        rows = pl.ds(pl.multiple_of(at.tensor * columns, 16), columns)
        moves, sources, owns, arrivals = [], [], [], []
        k = 0
        for offset in range(group):
            g = at.g ^ offset
            first = pl.ds(pl.multiple_of(g * half, 128), half)
            last = pl.ds(pl.multiple_of(length - (g + 1) * half, 128), half)
            for j in range(seqs):
                z = (at.dp + j) % at.slices
                device = (g // 2, z * 2 + g % 2)
                own = (z == at.z) if offset == 0 else None
                key = (j * n_tensor + at.tensor) * 2
                moves.append((c_ref.at[j, :, first], o_ref.at[j, rows, pl.ds(0, half)], send.at[k], recv.at[key], device, own))
                moves.append((c_ref.at[j, :, last], o_ref.at[j, rows, pl.ds(half, half)], send.at[k + 1], recv.at[key + 1], device, own))
                k += 2
                owns.append(own)
        for j in range(seqs):
            src_dp = (at.z - j + at.n_dp) % at.n_dp
            for b in range(n_tensor):
                own = jnp.logical_and(src_dp == at.dp, at.tensor == b)
                sources.append(((src_dp, b), own))
                their = pl.ds(b * columns, columns)
                key = (j * n_tensor + b) * 2
                arrivals.append((o_ref.at[j, their, pl.ds(0, half)], recv.at[key]))
                arrivals.append((o_ref.at[j, their, pl.ds(half, half)], recv.at[key + 1]))
        greet(sources, owns)
        start_all(moves)
        wait_sent(moves)
        wait_arrived(arrivals)

    (cot_tok,) = exchange(
        cot_body, [cotangent], [jax.ShapeDtypeStruct((seqs, width, 2 * half), BF)], group * seqs * 2, 3
    )

    w_in_all = lax.all_gather(w_in, "tensor", axis=0, tiled=True)
    w_out_all = lax.all_gather(w_out, "tensor", axis=0, tiled=True)
    b_in_all = lax.all_gather(b_in, "tensor", axis=0, tiled=True)
    small = lax.all_gather(
        jnp.stack([b_out, gain_one, shift_one, gain_two, shift_two], 0), "tensor", axis=1, tiled=True
    )
    b_out_all, g1, s1, g2, s2 = [small[i][:, None] for i in range(5)]
    g = lax.axis_index("dp") * 2 + lax.axis_index("tensor") % 2
    z = lax.axis_index("tensor") // 2
    keep_all = lax.all_gather(valid.astype(F32), "dp", axis=0, tiled=False)

    lane = jnp.arange(half)
    turn = ((lane[:, None] + lane[None, :]) == half).astype(BF)
    edge_lane = jnp.arange(128)
    pick_u = ((edge_lane[:, None] == 2 * g) & (lane[None, :] == 0)).astype(BF)
    pick_v = ((edge_lane[:, None] == 2 * g + 1) & (lane[None, :] == 0)).astype(BF)

    def dot(a, b, da, db):
        return lax.dot_general(a, b, (((da,), (db,)), ((), ())), preferred_element_type=F32)

    def norm(v):
        center = jnp.mean(v, axis=0, keepdims=True)
        off = v - center
        inverse = lax.rsqrt(jnp.mean(off * off, axis=0, keepdims=True) + EPSILON)
        return off * inverse, inverse

    def norm_back(gh, h, inverse):
        return inverse * (
            gh - jnp.mean(gh, axis=0, keepdims=True) - h * jnp.mean(gh * h, axis=0, keepdims=True)
        )

    acts, gus, ges, gfs = [], [], [], []
    totals = None
    for j in range(seqs):
        u, v = u_tok[j, :, :half], u_tok[j, :, half:]
        u_turned = (dot(u, turn, 1, 0) + dot(e_tok[j], pick_u, 1, 0)).astype(BF)
        v_turned = (dot(v, turn, 1, 0) + dot(e_tok[j], pick_v, 1, 0)).astype(BF)
        mixed_a = dot(hid_cos, u, 1, 0) - dot(hid_sin, v, 1, 0)
        mixed_b = dot(hid_cos, u_turned, 1, 0) + dot(hid_sin, v_turned, 1, 0)
        mixed = jnp.concatenate([mixed_a, mixed_b], axis=1)
        first = x_tok[j].astype(F32) + mixed * mix_scale
        h1, inv1 = norm(first)
        normed = h1 * g1 + s1
        normed_low = normed.astype(BF)
        inner = dot(w_in_all, normed_low, 1, 0) + b_in_all[:, None]
        active, gelu_back = jax.vjp(lambda q: jax.nn.gelu(q, approximate=True), inner)
        active_low = active.astype(BF)
        outer = dot(w_out_all, active_low, 0, 0) + b_out_all
        h2, inv2 = norm(normed + outer)
        acts.append((h2 * g2 + s2).astype(BF))
        src_dp = (z - j + n_dp) % n_dp
        go = cot_tok[j].astype(F32) * keep_all[src_dp, j]
        g_second = norm_back(go * g2, h2, inv2)
        g_low = g_second.astype(BF)
        g_w_out = dot(active_low, g_low, 1, 1)
        (g_inner,) = gelu_back(dot(w_out_all, g_low, 1, 0))
        inner_low = g_inner.astype(BF)
        g_w_in = dot(inner_low, normed_low, 1, 1)
        g_normed = g_second + dot(w_in_all, inner_low, 0, 0)
        g_first = norm_back(g_normed * g1, h1, inv1)
        gm = (g_first * mix_scale).astype(BF)
        gm_a, gm_b = gm[:, :half], gm[:, half:]
        gm_t = dot(gm_b, turn, 1, 0)
        even = (gm_t + gm_a.astype(F32)).astype(BF)
        odd = (gm_t - gm_a.astype(F32)).astype(BF)
        gu = dot(hid_cos, even, 1, 0)
        gv = dot(hid_sin, odd, 1, 0)
        ge = dot(hid_cos, dot(gm_b, pick_u, 1, 1).astype(BF), 1, 0) + dot(
            hid_sin, dot(gm_b, pick_v, 1, 1).astype(BF), 1, 0
        )
        gus.append(jnp.concatenate([gu, gv], axis=1).astype(BF))
        ges.append(ge.astype(BF))
        gfs.append(g_first.astype(BF))
        updates = (
            g_w_in,
            jnp.sum(g_inner, axis=1),
            g_w_out,
            jnp.sum(g_second, axis=1),
            jnp.sum(g_normed * h1, axis=1),
            jnp.sum(g_normed, axis=1),
            jnp.sum(go * h2, axis=1),
            jnp.sum(go, axis=1),
        )
        totals = updates if totals is None else tuple(a + b for a, b in zip(totals, updates))
    act_tok, gu_tok, ge_tok, gf_tok = [jnp.stack(q) for q in (acts, gus, ges, gfs)]

    def act_body(a_ref, o_ref, send, recv):
        at = Place(n_dp, n_tensor)
        first = pl.ds(pl.multiple_of(at.g * half, 128), half)
        last = pl.ds(pl.multiple_of(length - (at.g + 1) * half, 128), half)
        moves, sources, owns, arrivals = [], [], [], []
        k = 0
        for offset in range(n_tensor):
            b = at.tensor ^ offset
            rows = pl.ds(pl.multiple_of(b * columns, 16), columns)
            for j in range(seqs):
                dp = (at.z - j + at.n_dp) % at.n_dp
                own = (dp == at.dp) if offset == 0 else None
                key = (j * group + at.g) * 2
                moves.append((a_ref.at[j, rows, pl.ds(0, half)], o_ref.at[j, :, first], send.at[k], recv.at[key], (dp, b), own))
                moves.append((a_ref.at[j, rows, pl.ds(half, half)], o_ref.at[j, :, last], send.at[k + 1], recv.at[key + 1], (dp, b), own))
                k += 2
                owns.append(own)
        for j in range(seqs):
            src_z = (at.dp + j) % at.slices
            for g_ in range(group):
                own = jnp.logical_and(src_z == at.z, at.g == g_)
                sources.append(((g_ // 2, src_z * 2 + g_ % 2), own))
                their_first = pl.ds(g_ * half, half)
                their_last = pl.ds(length - (g_ + 1) * half, half)
                key = (j * group + g_) * 2
                arrivals.append((o_ref.at[j, :, their_first], recv.at[key]))
                arrivals.append((o_ref.at[j, :, their_last], recv.at[key + 1]))
        greet(sources, owns)
        start_all(moves)
        wait_sent(moves)
        wait_arrived(arrivals)

    (activations,) = exchange(
        act_body, [act_tok], [jax.ShapeDtypeStruct(words.shape, BF)], n_tensor * seqs * 2, 4
    )

    def to_columns_body(u_ref, e_ref, f_ref, uo_ref, eo_ref, fo_ref, send, recv):
        at = Place(n_dp, n_tensor)
        first = pl.ds(pl.multiple_of(at.g * half, 128), half)
        last = pl.ds(pl.multiple_of(length - (at.g + 1) * half, 128), half)
        mine = pl.ds(pl.multiple_of(at.g * 2 * half, 128), 2 * half)
        moves, sources = [], []
        k = 0
        for offset in range(group):
            device, g_ = at.peer(offset)
            rows = pl.ds(pl.multiple_of(at.block_of(g_ // 2, g_ % 2) * columns, 16), columns)
            if offset == 0:
                device = None
            else:
                sources.append((device, None))
            for j in range(seqs):
                for src, dst in (
                    (u_ref.at[j, rows], uo_ref.at[j, :, mine]),
                    (e_ref.at[j, rows], eo_ref.at[at.g, j]),
                    (f_ref.at[j, rows, pl.ds(0, half)], fo_ref.at[j, :, first]),
                    (f_ref.at[j, rows, pl.ds(half, half)], fo_ref.at[j, :, last]),
                ):
                    moves.append((src, dst, send.at[k], recv.at[k], device, None))
                    k += 1
        greet(sources, [None] * len(sources))
        start_all(moves)
        wait_sent(moves)
        wait_arrived([(m[1], m[3]) for m in moves])

    gu_col, ge_col, gf_col = exchange(
        to_columns_body,
        [gu_tok, ge_tok, gf_tok],
        [
            jax.ShapeDtypeStruct((seqs, columns, length), BF),
            jax.ShapeDtypeStruct((group, seqs, columns, 128), BF),
            jax.ShapeDtypeStruct((seqs, columns, length), BF),
        ],
        group * seqs * 4,
        5,
    )
    ge_sum = jnp.sum(ge_col.astype(F32), axis=0).astype(BF)
    gw_col = (
        gf_col.astype(F32)
        + jnp.einsum("jck,lk->jcl", gu_col, table, preferred_element_type=F32)
        + jnp.einsum("jck,lk->jcl", ge_sum, edge_table, preferred_element_type=F32)
    ).astype(BF)

    def home_body(x_ref, o_ref, send, recv):
        at = Place(n_dp, n_tensor)
        moves, sources = [], []
        target_dp = at.dp_of(at.z)
        for j in range(seqs):
            z_ = (at.dp + j) % at.slices
            own = jnp.logical_and(target_dp == at.dp, z_ == at.z)
            moves.append((x_ref.at[j], o_ref.at[j], send.at[j], recv.at[j], ((at.z - j + at.n_dp) % at.n_dp, at.block), own))
            sources.append(((target_dp, z_ * 2 + at.y), own))
        greet(sources, [m[5] for m in moves])
        start_all(moves)
        wait_sent(moves)
        wait_arrived([(m[1], m[3]) for m in moves])

    (gw,) = exchange(home_body, [gw_col], [jax.ShapeDtypeStruct(words.shape, BF)], seqs, 6)
    grad_words = gw.astype(F32)

    def reduce_weight(v):
        part = lax.psum_scatter(v.astype(BF), "tensor", scatter_dimension=0, tiled=True)
        return lax.psum(part, "dp").astype(F32)

    grad_w_in = reduce_weight(totals[0])
    grad_w_out = reduce_weight(totals[2])
    grad_b_in = lax.psum(lax.psum_scatter(totals[1], "tensor", scatter_dimension=0, tiled=True), "dp")
    rest = jnp.stack(totals[3:], 0)
    rest = lax.psum(lax.psum_scatter(rest, "tensor", scatter_dimension=1, tiled=True), "dp")
    return (
        activations,
        grad_words,
        grad_w_in,
        grad_b_in,
        grad_w_out,
        rest[0],
        rest[1],
        rest[2],
        rest[3],
        rest[4],
    )


def solution(mesh):
    spec = (
        P("dp", "tensor", None),
        P("tensor", None),
        P("tensor"),
        P("tensor", None),
        P("tensor"),
        P("tensor"),
        P("tensor"),
        P("tensor"),
        P("tensor"),
        P("dp", "tensor", None),
        P("dp"),
    )
    out = (
        P("dp", "tensor", None),
        P("dp", "tensor", None),
        P("tensor", None),
        P("tensor"),
        P("tensor", None),
        P("tensor"),
        P("tensor"),
        P("tensor"),
        P("tensor"),
        P("tensor"),
    )
    return jax.shard_map(on_device, mesh=mesh, in_specs=spec, out_specs=out, check_vma=False)
```

```python
import math

import jax
import jax.numpy as jnp
import numpy as np
from jax import lax
from jax.experimental import pallas as pl
from jax.experimental.pallas import tpu as pltpu
from jax.sharding import PartitionSpec as P

EPSILON = 1e-12
MESH = pl.DeviceIdType.MESH
BF = jnp.bfloat16
F32 = jnp.float32


def token_tables(length, group):
    half = length // (2 * group)
    n = np.arange(length, dtype=np.int64)

    def wave(k):
        angle = (n[:, None] * k[None, :] % length) * (2.0 * math.pi / length)
        return np.cos(angle), np.sin(angle)

    cos, sin = wave(np.arange(length // 2))
    main = np.stack(
        [cos.reshape(length, group, half), sin.reshape(length, group, half)], axis=2
    ).reshape(length, length)
    edge_cos, edge_sin = wave(half * (np.arange(group) + 1))
    edge = np.zeros((length, 128))
    edge[:, 0 : 2 * group : 2] = edge_cos
    edge[:, 1 : 2 * group : 2] = np.where(np.abs(edge_sin) < 1e-9, 0.0, edge_sin)
    return main.astype(BF), edge.astype(BF)


def hidden_tables(width):
    ids = np.arange(width, dtype=np.int64)
    angle = (ids[:, None] * ids[None, :] % width) * (2.0 * math.pi / width)
    return np.cos(angle).astype(BF), np.sin(angle).astype(BF)


class Place:
    def __init__(self, n_dp, n_tensor):
        self.n_dp, self.n_tensor = n_dp, n_tensor
        self.slices = n_tensor // 2
        self.group = 2 * n_dp
        self.dp = lax.axis_index("dp")
        self.tensor = lax.axis_index("tensor")
        self.z = self.tensor // 2
        self.y = self.tensor % 2
        self.g = self.dp * 2 + self.y
        self.block = self.block_of(self.dp, self.y)

    def block_of(self, dp, y):
        return ((dp % (self.n_dp // 2)) * 2 + dp // (self.n_dp // 2)) * 2 + y

    def dp_of(self, z):
        return (z % 2) * (self.n_dp // 2) + z // 2

    def peer(self, offset):
        g = self.g ^ offset
        return (g // 2, self.z * 2 + g % 2), g


def start_all(moves):
    for src, dst, send, recv, device, own in moves:
        if device is None:
            pltpu.make_async_copy(src, dst, recv).start()
        elif own is None:
            pltpu.make_async_remote_copy(src, dst, send, recv, device, MESH).start()
        else:
            @pl.when(own)
            def _():
                pltpu.make_async_copy(src, dst, recv).start()

            @pl.when(jnp.logical_not(own))
            def _():
                pltpu.make_async_remote_copy(src, dst, send, recv, device, MESH).start()


def wait_sent(moves):
    for src, dst, send, recv, device, own in moves:
        if device is None:
            continue
        if own is None:
            pltpu.make_async_copy(src, src, send).wait()
        else:
            @pl.when(jnp.logical_not(own))
            def _():
                pltpu.make_async_copy(src, src, send).wait()


def wait_arrived(arrivals):
    for ref, recv in arrivals:
        pltpu.make_async_copy(ref, ref, recv).wait()


def greet(sources, n_targets):
    barrier = pltpu.get_barrier_semaphore()
    count = 0
    for device, own in sources:
        if own is None:
            pl.semaphore_signal(barrier, inc=1, device_id=device, device_id_type=MESH)
        else:
            @pl.when(jnp.logical_not(own))
            def _():
                pl.semaphore_signal(barrier, inc=1, device_id=device, device_id_type=MESH)
    total = 0
    for own in n_targets:
        total = total + (1 if own is None else jnp.where(own, 0, 1))
    pl.semaphore_wait(barrier, total)


ANY = pl.BlockSpec(memory_space=pl.ANY)


def exchange(body, ins, outs, n_sems, collective_id):
    return pl.pallas_call(
        body,
        out_shape=outs,
        in_specs=[ANY] * len(ins),
        out_specs=[ANY] * len(outs),
        scratch_shapes=[pltpu.SemaphoreType.DMA((n_sems,)), pltpu.SemaphoreType.DMA((n_sems,))],
        compiler_params=pltpu.CompilerParams(collective_id=collective_id, has_side_effects=True),
    )(*ins)


def on_device(
    words, w_in, b_in, w_out, b_out, gain_one, shift_one, gain_two, shift_two, cotangent, valid
):
    seqs, columns, length = words.shape
    width = w_in.shape[1]
    n_dp, n_tensor = lax.axis_size("dp"), lax.axis_size("tensor")
    assert n_tensor == 2 * n_dp
    group = 2 * n_dp
    half = length // (2 * group)
    mix_scale = 1.0 / math.sqrt(length * width)
    table, edge_table = token_tables(length, group)
    hid_cos, hid_sin = hidden_tables(width)

    def to_slice_body(x_ref, o_ref, send, recv):
        at = Place(n_dp, n_tensor)
        moves, sources = [], []
        target_dp = at.dp_of(at.z)
        for j in range(seqs):
            z = (at.dp + j) % at.slices
            own = jnp.logical_and(target_dp == at.dp, z == at.z)
            moves.append((x_ref.at[j], o_ref.at[j], send.at[j], recv.at[j], (target_dp, z * 2 + at.y), own))
            sources.append((((at.z - j + at.n_dp) % at.n_dp, at.block), own))
        greet(sources, [m[5] for m in moves])
        start_all(moves)
        wait_sent(moves)
        wait_arrived([(m[1], m[3]) for m in moves])

    (x_col,) = exchange(
        to_slice_body, [words], [jax.ShapeDtypeStruct(words.shape, BF)], seqs, 1
    )

    spectrum = jnp.einsum("jcl,lk->jck", x_col, table, preferred_element_type=F32).astype(BF)
    edges = jnp.einsum("jcl,lk->jck", x_col, edge_table, preferred_element_type=F32).astype(BF)

    def to_tokens_body(x_ref, u_ref, e_ref, xo_ref, uo_ref, eo_ref, send, recv):
        at = Place(n_dp, n_tensor)
        rows = pl.ds(pl.multiple_of(at.block * columns, 16), columns)
        moves, sources = [], []
        k = 0
        for offset in range(group):
            device, g = at.peer(offset)
            if offset == 0:
                device = None
            else:
                sources.append((device, None))
            first = pl.ds(pl.multiple_of(g * half, 128), half)
            last = pl.ds(pl.multiple_of(length - (g + 1) * half, 128), half)
            mine = pl.ds(pl.multiple_of(g * 2 * half, 128), 2 * half)
            for j in range(seqs):
                for src, dst in (
                    (x_ref.at[j, :, first], xo_ref.at[j, rows, pl.ds(0, half)]),
                    (x_ref.at[j, :, last], xo_ref.at[j, rows, pl.ds(half, half)]),
                    (u_ref.at[j, :, mine], uo_ref.at[j, rows]),
                    (e_ref.at[j], eo_ref.at[j, rows]),
                ):
                    moves.append((src, dst, send.at[k], recv.at[k], device, None))
                    k += 1
        greet(sources, [None] * len(sources))
        start_all(moves)
        wait_sent(moves)
        wait_arrived([(m[1], m[3]) for m in moves])

    x_tok, u_tok, e_tok = exchange(
        to_tokens_body,
        [x_col, spectrum, edges],
        [
            jax.ShapeDtypeStruct((seqs, width, 2 * half), BF),
            jax.ShapeDtypeStruct((seqs, width, 2 * half), BF),
            jax.ShapeDtypeStruct((seqs, width, 128), BF),
        ],
        group * seqs * 4,
        2,
    )

    w_in_all = lax.all_gather(w_in, "tensor", axis=0, tiled=True)
    w_out_all = lax.all_gather(w_out, "tensor", axis=0, tiled=True)
    b_in_all = lax.all_gather(b_in, "tensor", axis=0, tiled=True)
    small = lax.all_gather(
        jnp.stack([b_out, gain_one, shift_one, gain_two, shift_two], 0), "tensor", axis=1, tiled=True
    )
    vectors = jnp.pad(small.T, ((0, 0), (0, 3)))
    keep_all = lax.all_gather(valid.astype(F32), "dp", axis=0, tiled=True)
    units = w_in_all.shape[0]
    tokens = 2 * half

    def dot(a, b, da, db):
        return lax.dot_general(a, b, (((da,), (db,)), ((), ())), preferred_element_type=F32)

    def layer_body(
        x_ref, u_ref, e_ref, c_ref, win_ref, wout_ref, cos_ref, sin_ref, vec, b_in_v, keep,
        act_o, gu_o, ge_o, gf_o, gin_o, gout_o, gb_o, gv_o,
        win, wout, cos, sin, xb, ub, eb, cb, ab, a_all, m_all, nl, gl, f1, f2, f3, tile, bacc, vacc, gtile,
        load, cot_send, cot_own, cot_recv, act_send, act_own, act_recv, col_send, col_recv, out_sem,
    ):
        at = Place(n_dp, n_tensor)
        tokens = 2 * half
        barrier = pltpu.get_barrier_semaphore()
        count = 0
        for j in range(seqs):
            src_dp = (at.z - j + at.n_dp) % at.n_dp
            for b in range(n_tensor):
                own = jnp.logical_and(src_dp == at.dp, at.tensor == b)

                @pl.when(jnp.logical_not(own))
                def _():
                    pl.semaphore_signal(barrier, inc=1, device_id=(src_dp, b), device_id_type=MESH)

                count = count + jnp.where(own, 0, 1)
        for j in range(seqs):
            z = (at.dp + j) % at.slices
            for g_ in range(group):
                own = jnp.logical_and(z == at.z, at.g == g_)

                @pl.when(jnp.logical_not(own))
                def _():
                    pl.semaphore_signal(barrier, inc=1, device_id=(g_ // 2, z * 2 + g_ % 2), device_id_type=MESH)

                count = count + jnp.where(own, 0, 1)
        for offset in range(1, group):
            device, _ = at.peer(offset)
            pl.semaphore_signal(barrier, inc=1, device_id=device, device_id_type=MESH)
            count = count + 1
        pl.semaphore_wait(barrier, count)

        def wait(ref, sem):
            pltpu.make_async_copy(ref, ref, sem).wait()

        def lanes(g):
            return (
                pl.ds(pl.multiple_of(g * half, 128), half),
                pl.ds(pl.multiple_of(length - (g + 1) * half, 128), half),
            )

        parts = (pl.ds(0, half), pl.ds(half, half))
        rows_of = lambda b: pl.ds(pl.multiple_of(b * columns, 16), columns)

        def cot_start(j):
            z = (at.dp + j) % at.slices
            for offset in range(group):
                g = at.g ^ offset
                for p in range(2):
                    src = c_ref.at[j, :, lanes(g)[p]]
                    dst = cb.at[j, rows_of(at.tensor), parts[p]]
                    device = (g // 2, z * 2 + g % 2)
                    if offset:
                        pltpu.make_async_remote_copy(src, dst, cot_send.at[j], cot_recv.at[j], device, MESH).start()
                    else:
                        @pl.when(z == at.z)
                        def _():
                            pltpu.make_async_copy(src, dst, cot_recv.at[j]).start()

                        @pl.when(z != at.z)
                        def _():
                            pltpu.make_async_remote_copy(src, dst, cot_own.at[j], cot_recv.at[j], device, MESH).start()

        def cot_finish(j):
            z = (at.dp + j) % at.slices
            wait(c_ref.at[j, :, pl.ds(0, length - 2 * half)], cot_send.at[j])

            @pl.when(z != at.z)
            def _():
                wait(c_ref.at[j, :, pl.ds(0, 2 * half)], cot_own.at[j])

        def act_start(j):
            dp = (at.z - j + at.n_dp) % at.n_dp
            for offset in range(n_tensor):
                b = at.tensor ^ offset
                for p in range(2):
                    src = ab.at[j, rows_of(b), parts[p]]
                    dst = act_o.at[j, :, lanes(at.g)[p]]
                    if offset:
                        pltpu.make_async_remote_copy(src, dst, act_send.at[j], act_recv.at[j], (dp, b), MESH).start()
                    else:
                        @pl.when(dp == at.dp)
                        def _():
                            pltpu.make_async_copy(src, dst, act_recv.at[j]).start()

                        @pl.when(dp != at.dp)
                        def _():
                            pltpu.make_async_remote_copy(src, dst, act_own.at[j], act_recv.at[j], (dp, b), MESH).start()

        def act_finish(j):
            dp = (at.z - j + at.n_dp) % at.n_dp
            wait(ab.at[j, pl.ds(0, width - columns)], act_send.at[j])

            @pl.when(dp != at.dp)
            def _():
                wait(ab.at[j, pl.ds(0, columns)], act_own.at[j])

            wait(act_o.at[j], act_recv.at[j])

        def col_moves(j):
            for offset in range(group):
                device, g_ = at.peer(offset)
                rows = rows_of(at.block_of(g_ // 2, g_ % 2))
                for i, (src, dst) in enumerate((
                    (ub.at[j, rows], gu_o.at[j, :, pl.ds(pl.multiple_of(at.g * tokens, 128), tokens)]),
                    (eb.at[j, rows], ge_o.at[at.g, j]),
                    (xb.at[j, rows, parts[0]], gf_o.at[j, :, lanes(at.g)[0]]),
                    (xb.at[j, rows, parts[1]], gf_o.at[j, :, lanes(at.g)[1]]),
                )):
                    kind = min(i, 2)
                    if offset:
                        yield pltpu.make_async_remote_copy(
                            src, dst, col_send.at[j, kind], col_recv.at[j, kind], device, MESH)
                    else:
                        yield pltpu.make_async_copy(src, dst, col_recv.at[j, kind])

        def col_finish(j):
            rest = pl.ds(0, width - columns)
            wait(ub.at[j, rest], col_send.at[j, 0])
            wait(eb.at[j, rest], col_send.at[j, 1])
            wait(xb.at[j, rest], col_send.at[j, 2])
            wait(gu_o.at[j], col_recv.at[j, 0])
            wait(ge_o.at[:, j], col_recv.at[j, 1])
            wait(gf_o.at[j], col_recv.at[j, 2])

        loads = {}
        def load_start(key, src, dst):
            loads[key] = pltpu.make_async_copy(src, dst, load.at[len(loads)])
            loads[key].start()

        for j in range(seqs):
            load_start(("u", j), u_ref.at[j], ub.at[j])
            load_start(("e", j), e_ref.at[j], eb.at[j])
            load_start(("x", j), x_ref.at[j], xb.at[j])
            if j == 0:
                load_start("cos", cos_ref, cos)
                load_start("sin", sin_ref, sin)
                load_start("win", win_ref, win)
                load_start("wout", wout_ref, wout)

        for j in range(seqs):
            cot_start(j)

        lane0 = lax.broadcasted_iota(jnp.int32, (half, half), 0)
        lane1 = lax.broadcasted_iota(jnp.int32, (half, half), 1)
        turn = jnp.where(lane0 + lane1 == half, 1.0, 0.0).astype(BF)
        edge0 = lax.broadcasted_iota(jnp.int32, (128, half), 0)
        edge1 = lax.broadcasted_iota(jnp.int32, (128, half), 1)
        pick_u = jnp.where((edge0 == 2 * at.g) & (edge1 == 0), 1.0, 0.0).astype(BF)
        pick_v = jnp.where((edge0 == 2 * at.g + 1) & (edge1 == 0), 1.0, 0.0).astype(BF)
        A, B = parts
        block = 256
        step = 32

        def over(rows, size, body, carry=None, unroll=2):
            def inner(i, c):
                r = pl.ds(pl.multiple_of(i * size, size), size)
                return body(r, c)
            return lax.fori_loop(0, rows // size, inner, carry, unroll=unroll)

        def fold(v):
            return jnp.sum(v.reshape(v.shape[0] // 8, 8, v.shape[1]), axis=0)

        def lane_fold(v):
            return sum(v[:, k * 128 : (k + 1) * 128] for k in range(v.shape[1] // 128))

        zeros8 = jnp.zeros((8, tokens), F32)

        def mean_of(total):
            return jnp.sum(total, axis=0, keepdims=True) / width

        def statistics(ref):
            total = over(width, step, lambda r, c: c + fold(ref[r, :]), zeros8)
            center = mean_of(total)
            def spread(r, c):
                off = ref[r, :] - center
                return c + fold(off * off)
            var = mean_of(over(width, step, spread, zeros8))
            return center, lax.rsqrt(var + EPSILON)

        bacc[...] = jnp.zeros_like(bacc)
        vacc[...] = jnp.zeros_like(vacc)

        def forward_mix(j):
            for key in ("u", "e", "x"):
                loads[(key, j)].wait()
            if j == 0:
                loads["cos"].wait()
                loads["sin"].wait()
            def turned(r, c):
                e = eb[j, r, :]
                tile[r, A] = (dot(ub[j, r, A], turn, 1, 0) + dot(e, pick_u, 1, 0)).astype(BF)
                tile[r, B] = (dot(ub[j, r, B], turn, 1, 0) + dot(e, pick_v, 1, 0)).astype(BF)
                return c
            over(width, block, turned, 0, unroll=1)
            def mixed(r, c):
                f1[r, A] = xb[j, r, A].astype(F32) + mix_scale * (
                    dot(cos[r, :], ub[j, :, A], 1, 0) - dot(sin[r, :], ub[j, :, B], 1, 0))
                f1[r, B] = xb[j, r, B].astype(F32) + mix_scale * (
                    dot(cos[r, :], tile[:, A], 1, 0) + dot(sin[r, :], tile[:, B], 1, 0))
                return c
            over(width, block, mixed, 0, unroll=1)
            center, inverse = statistics(f1)
            def scale(r, c):
                h = (f1[r, :] - center) * inverse
                f1[r, :] = h
                n = h * vec[r, 1:2] + vec[r, 2:3]
                f2[r, :] = n
                nl[j, r, :] = n.astype(BF)
                return c
            over(width, step, scale, 0)
            return inverse

        c0 = math.sqrt(2.0 / math.pi)
        c1 = c0 * 0.044715

        def forward_mlp(j):
            if j == 0:
                loads["win"].wait()
                loads["wout"].wait()
            def inner(r, c):
                v = dot(win[r, :], nl[j], 1, 0) + b_in_v[r, :]
                v2 = v * v
                p = 0.5 + 0.5 * jnp.tanh(v * (c0 + c1 * v2))
                a = v * p
                a_all[j, r, :] = a.astype(BF)
                m_all[j, r, :] = (p + a * (1.0 - p) * (2.0 * c0 + 6.0 * c1 * v2)).astype(BF)
                return c
            over(units, block, inner, 0, unroll=1)
            def outer(r, c):
                f2[r, :] = f2[r, :] + dot(wout[:, r], a_all[j], 0, 0) + vec[r, 0:1]
                return c
            for k in range(width // block):
                outer(pl.ds(k * block, block), 0)

        def second_norm(j):
            center, inverse = statistics(f2)
            flag = keep[((at.z - j + at.n_dp) % at.n_dp) * seqs + j]
            def result(r, c):
                h = (f2[r, :] - center) * inverse
                f2[r, :] = h
                ab[j, r, :] = (h * vec[r, 3:4] + vec[r, 4:5]).astype(BF)
                return c
            over(width, step, result, 0)
            act_start(j)
            wait(cb.at[j], cot_recv.at[j])
            def sums(r, c):
                go = cb[j, r, :].astype(F32) * flag
                h = f2[r, :]
                goh = go * h
                vacc[3, r, :] += lane_fold(goh)
                vacc[4, r, :] += lane_fold(go)
                gh = go * vec[r, 3:4]
                return c[0] + fold(gh), c[1] + fold(gh * h)
            m1, m2 = over(width, step, sums, (zeros8, zeros8))
            m1, m2 = mean_of(m1), mean_of(m2)
            def back(r, c):
                gh = cb[j, r, :].astype(F32) * flag * vec[r, 3:4]
                gs = inverse * (gh - m1 - f2[r, :] * m2)
                vacc[0, r, :] += lane_fold(gs)
                f3[r, :] = gs
                gl[j, r, :] = gs.astype(BF)
                return c
            over(width, step, back, 0)

        def backward_mlp(j):
            def inner(r, c):
                gi = dot(wout[r, :], gl[j], 1, 0) * m_all[j, r, :].astype(F32)
                bacc[r, :] += lane_fold(gi)
                m_all[j, r, :] = gi.astype(BF)
                return c
            over(units, block, inner, 0, unroll=1)
            for k in range(width // block):
                r = pl.ds(k * block, block)
                f3[r, :] = f3[r, :] + dot(win[:, r], m_all[j], 0, 0)

        def first_back(j, inverse):
            def sums(r, c):
                gn = f3[r, :]
                h = f1[r, :]
                gnh = gn * h
                vacc[1, r, :] += lane_fold(gnh)
                vacc[2, r, :] += lane_fold(gn)
                gh = gn * vec[r, 1:2]
                return c[0] + fold(gh), c[1] + fold(gh * h)
            m1, m2 = over(width, step, sums, (zeros8, zeros8))
            m1, m2 = mean_of(m1), mean_of(m2)
            def back(r, c):
                gf = inverse * (f3[r, :] * vec[r, 1:2] - m1 - f1[r, :] * m2)
                xb[j, r, :] = gf.astype(BF)
                tile[r, :] = (gf * mix_scale).astype(BF)
                return c
            over(width, step, back, 0)
            def fold_pairs(r, c):
                a = tile[r, A].astype(F32)
                b = tile[r, B]
                t = dot(b, turn, 1, 0)
                ub[j, r, A] = (t + a).astype(BF)
                ub[j, r, B] = (t - a).astype(BF)
                eb[j, r, :] = dot(b, pick_u + pick_v, 1, 1).astype(BF)
                return c
            over(width, block, fold_pairs, 0, unroll=1)
            even, odd, edge = ub[j, :, A], ub[j, :, B], eb[j]
            is_cos = lax.broadcasted_iota(jnp.int32, (block, 128), 1) % 2 == 0
            for k in range(width // block):
                r = pl.ds(k * block, block)
                f1[r, A] = dot(cos[r, :], even, 1, 0)
                f1[r, B] = dot(sin[r, :], odd, 1, 0)
                f2[r, 0:128] = jnp.where(is_cos, dot(cos[r, :], edge, 1, 0), dot(sin[r, :], edge, 1, 0))
            def pack(r, c):
                ub[j, r, :] = f1[r, :].astype(BF)
                eb[j, r, :] = f2[r, 0:128].astype(BF)
                return c
            over(width, step, pack, 0)
            for move in col_moves(j):
                move.start()

        for j in range(seqs):
            inverse = forward_mix(j)
            forward_mlp(j)
            second_norm(j)
            backward_mlp(j)
            first_back(j, inverse)

        n_tiles = units // block
        def weight_step(i, c):
            r = pl.ds(pl.multiple_of(i * block, block), block)
            slot = i % 2
            @pl.when(i >= 2)
            def _():
                wait(gin_o.at[pl.ds(0, block)], out_sem.at[slot, 0])
                wait(gin_o.at[pl.ds(0, block)], out_sem.at[slot, 1])
            tin = gtile.at[slot, 0]
            tout = gtile.at[slot, 1]
            s_in = jnp.zeros((block, width), F32)
            s_out = jnp.zeros((block, width), F32)
            for j in range(seqs):
                s_in = s_in + dot(m_all[j, r, :], nl[j], 1, 1)
                s_out = s_out + dot(a_all[j, r, :], gl[j], 1, 1)
            tin[...] = s_in.astype(BF)
            tout[...] = s_out.astype(BF)
            pltpu.make_async_copy(tin, gin_o.at[r], out_sem.at[slot, 0]).start()
            pltpu.make_async_copy(tout, gout_o.at[r], out_sem.at[slot, 1]).start()
            return c
        lax.fori_loop(0, n_tiles, weight_step, 0)
        for slot in range(2):
            wait(gin_o.at[pl.ds(0, block)], out_sem.at[slot, 0])
            wait(gin_o.at[pl.ds(0, block)], out_sem.at[slot, 1])
        gb_o[...] = bacc[...]
        gv_o[...] = vacc[...]
        for j in range(seqs):
            cot_finish(j)
            act_finish(j)
            col_finish(j)

    shape = jax.ShapeDtypeStruct
    dma = pltpu.SemaphoreType.DMA
    whole_vmem = pl.BlockSpec(memory_space=pltpu.VMEM)
    activations, gu_col, ge_col, gf_col, g_in, g_out, g_b, g_v = pl.pallas_call(
        layer_body,
        out_shape=[
            shape(words.shape, BF),
            shape((seqs, columns, length), BF),
            shape((group, seqs, columns, 128), BF),
            shape((seqs, columns, length), BF),
            shape((units, width), BF),
            shape((units, width), BF),
            shape((units, 128), F32),
            shape((5, width, 128), F32),
        ],
        in_specs=[ANY] * 8 + [whole_vmem, whole_vmem, pl.BlockSpec(memory_space=pltpu.SMEM)],
        out_specs=[ANY] * 6 + [whole_vmem, whole_vmem],
        scratch_shapes=[
            pltpu.VMEM((units, width), BF),
            pltpu.VMEM((units, width), BF),
            pltpu.VMEM((width, width), BF),
            pltpu.VMEM((width, width), BF),
            pltpu.VMEM((seqs, width, tokens), BF),
            pltpu.VMEM((seqs, width, tokens), BF),
            pltpu.VMEM((seqs, width, 128), BF),
            pltpu.VMEM((seqs, width, tokens), BF),
            pltpu.VMEM((seqs, width, tokens), BF),
            pltpu.VMEM((seqs, units, tokens), BF),
            pltpu.VMEM((seqs, units, tokens), BF),
            pltpu.VMEM((seqs, width, tokens), BF),
            pltpu.VMEM((seqs, width, tokens), BF),
            pltpu.VMEM((width, tokens), F32),
            pltpu.VMEM((width, tokens), F32),
            pltpu.VMEM((width, tokens), F32),
            pltpu.VMEM((width, tokens), BF),
            pltpu.VMEM((units, 128), F32),
            pltpu.VMEM((5, width, 128), F32),
            pltpu.VMEM((2, 2, 256, width), BF),
            dma((3 * seqs + 4,)),
            dma((seqs,)),
            dma((seqs,)),
            dma((seqs,)),
            dma((seqs,)),
            dma((seqs,)),
            dma((seqs,)),
            dma((seqs, 3)),
            dma((seqs, 3)),
            dma((2, 2)),
        ],
        compiler_params=pltpu.CompilerParams(
            collective_id=3, has_side_effects=True, vmem_limit_bytes=64 * 1024 * 1024
        ),
    )(
        x_tok, u_tok, e_tok, cotangent, w_in_all, w_out_all,
        jnp.asarray(hid_cos), jnp.asarray(hid_sin), vectors, b_in_all[:, None], keep_all,
    )
    ge_sum = jnp.sum(ge_col.astype(F32), axis=0).astype(BF)
    gw_col = (
        gf_col.astype(F32)
        + jnp.einsum("jck,lk->jcl", gu_col, table, preferred_element_type=F32)
        + jnp.einsum("jck,lk->jcl", ge_sum, edge_table, preferred_element_type=F32)
    ).astype(BF)

    def home_body(x_ref, o_ref, send, recv):
        at = Place(n_dp, n_tensor)
        moves, sources = [], []
        target_dp = at.dp_of(at.z)
        for j in range(seqs):
            z_ = (at.dp + j) % at.slices
            own = jnp.logical_and(target_dp == at.dp, z_ == at.z)
            moves.append((x_ref.at[j], o_ref.at[j], send.at[j], recv.at[j], ((at.z - j + at.n_dp) % at.n_dp, at.block), own))
            sources.append(((target_dp, z_ * 2 + at.y), own))
        greet(sources, [m[5] for m in moves])
        start_all(moves)
        wait_sent(moves)
        wait_arrived([(m[1], m[3]) for m in moves])

    (gw,) = exchange(home_body, [gw_col], [jax.ShapeDtypeStruct(words.shape, BF)], seqs, 6)
    grad_words = gw.astype(F32)

    def reduce_weight(v):
        part = lax.psum_scatter(v.astype(BF), "tensor", scatter_dimension=0, tiled=True)
        return lax.psum(part, "dp").astype(F32)

    grad_w_in = reduce_weight(g_in)
    grad_w_out = reduce_weight(g_out)
    g_b = jnp.sum(g_b, axis=1)
    rest = jnp.sum(g_v, axis=2)
    grad_b_in = lax.psum(lax.psum_scatter(g_b, "tensor", scatter_dimension=0, tiled=True), "dp")
    rest = lax.psum(lax.psum_scatter(rest, "tensor", scatter_dimension=1, tiled=True), "dp")
    return (
        activations,
        grad_words,
        grad_w_in,
        grad_b_in,
        grad_w_out,
        rest[0],
        rest[1],
        rest[2],
        rest[3],
        rest[4],
    )


def solution(mesh):
    spec = (
        P("dp", "tensor", None),
        P("tensor", None),
        P("tensor"),
        P("tensor", None),
        P("tensor"),
        P("tensor"),
        P("tensor"),
        P("tensor"),
        P("tensor"),
        P("dp", "tensor", None),
        P("dp"),
    )
    out = (
        P("dp", "tensor", None),
        P("dp", "tensor", None),
        P("tensor", None),
        P("tensor"),
        P("tensor", None),
        P("tensor"),
        P("tensor"),
        P("tensor"),
        P("tensor"),
        P("tensor"),
    )
    return jax.shard_map(on_device, mesh=mesh, in_specs=spec, out_specs=out, check_vma=False)
```

```python
import math

import jax
import jax.numpy as jnp
import numpy as np
from jax import lax
from jax.experimental import pallas as pl
from jax.experimental.pallas import tpu as pltpu
from jax.sharding import PartitionSpec as P

EPSILON = 1e-12
MESH = pl.DeviceIdType.MESH
BF = jnp.bfloat16
F32 = jnp.float32


def token_tables(length, group):
    half = length // (2 * group)
    n = np.arange(length, dtype=np.int64)

    def wave(k):
        angle = (n[:, None] * k[None, :] % length) * (2.0 * math.pi / length)
        return np.cos(angle), np.sin(angle)

    cos, sin = wave(np.arange(length // 2))
    main = np.stack(
        [cos.reshape(length, group, half), sin.reshape(length, group, half)], axis=2
    ).reshape(length, group, 2 * half)
    main = main.transpose(1, 0, 2).reshape(group * length, 2 * half)
    edge_cos, edge_sin = wave(half * (np.arange(group) + 1))
    edge = np.zeros((length, 128))
    edge[:, 0 : 2 * group : 2] = edge_cos
    edge[:, 1 : 2 * group : 2] = np.where(np.abs(edge_sin) < 1e-9, 0.0, edge_sin)
    return main.astype(BF), edge.astype(BF)


def hidden_tables(width):
    ids = np.arange(width, dtype=np.int64)
    angle = (ids[:, None] * ids[None, :] % width) * (2.0 * math.pi / width)
    return np.cos(angle).astype(BF), np.sin(angle).astype(BF)


class Place:
    def __init__(self, n_dp, n_tensor):
        self.n_dp, self.n_tensor = n_dp, n_tensor
        self.slices = n_tensor // 2
        self.group = 2 * n_dp
        self.dp = lax.axis_index("dp")
        self.tensor = lax.axis_index("tensor")
        self.z = self.tensor // 2
        self.y = self.tensor % 2
        self.g = self.dp * 2 + self.y
        self.block = self.block_of(self.dp, self.y)

    def block_of(self, dp, y):
        return ((dp % (self.n_dp // 2)) * 2 + dp // (self.n_dp // 2)) * 2 + y

    def dp_of(self, z):
        return (z % 2) * (self.n_dp // 2) + z // 2

    def peer(self, offset):
        g = self.g ^ offset
        return (g // 2, self.z * 2 + g % 2), g


ANY = pl.BlockSpec(memory_space=pl.ANY)


def on_device(
    words, w_in, b_in, w_out, b_out, gain_one, shift_one, gain_two, shift_two, cotangent, valid
):
    seqs, columns, length = words.shape
    width = w_in.shape[1]
    n_dp, n_tensor = lax.axis_size("dp"), lax.axis_size("tensor")
    assert n_tensor == 2 * n_dp
    group = 2 * n_dp
    half = length // (2 * group)
    mix_scale = 1.0 / math.sqrt(length * width)
    table, edge_table = token_tables(length, group)
    hid_cos, hid_sin = hidden_tables(width)

    table = jnp.asarray(table)
    edge_table = jnp.asarray(edge_table)
    units = w_in.shape[0] * n_tensor
    tokens = 2 * half

    def dot(a, b, da, db):
        return lax.dot_general(a, b, (((da,), (db,)), ((), ())), preferred_element_type=F32)

    wide = 512
    pad = lambda v: jnp.pad(v, (0, wide - v.shape[0]))
    rows_in = jnp.stack(
        [pad(v) for v in (b_in, b_out, gain_one, shift_one, gain_two, shift_two, valid.astype(F32))]
        + [jnp.zeros((wide,), F32)]
    )

    def layer_body(
        x_ref, c_ref, win_ref, wout_ref, cos_ref, sin_ref, table_ref, edge_ref, rows_ref,
        act_o, gu_o, ge_o, gf_o, gw_o, gin_o, gout_o, vec_o,
        win, wout, cos, sin, xb, ub, eb, cb, ab, a_all, m_all, nl, gl, f, tile, edge_v,
        bacc, vacc, b_in_v, vec, vrows, drows, grows, drows2, spare,
        load, slice_send, slice_recv, tok_send, tok_recv, vec_send, vec_recv, gather_send, gather_recv,
        cot_send, cot_own, cot_recv, act_send, act_own, act_recv, col_send, col_recv,
        ready, rs_send, rs_recv, table_sem, home_send, home_recv, more_send, more_recv, more_free,
        vg_send, vg_recv,
    ):
        at = Place(n_dp, n_tensor)
        barrier = pltpu.get_barrier_semaphore()
        count = 0
        for j in range(seqs):
            src_dp = (at.z - j + at.n_dp) % at.n_dp
            for b in range(n_tensor):
                mine_ = jnp.logical_and(src_dp == at.dp, at.tensor == b)

                @pl.when(jnp.logical_not(mine_))
                def _():
                    pl.semaphore_signal(barrier, inc=1, device_id=(src_dp, b), device_id_type=MESH)

                count = count + jnp.where(mine_, 0, 1)
        for j in range(seqs):
            z = (at.dp + j) % at.slices
            for g_ in range(group):
                mine_ = jnp.logical_and(z == at.z, at.g == g_)

                @pl.when(jnp.logical_not(mine_))
                def _():
                    pl.semaphore_signal(barrier, inc=1, device_id=(g_ // 2, z * 2 + g_ % 2), device_id_type=MESH)

                count = count + jnp.where(mine_, 0, 1)
        for offset in range(1, group):
            device, _ = at.peer(offset)
            pl.semaphore_signal(barrier, inc=1, device_id=device, device_id_type=MESH)
            count = count + 1
        for offset in range(1, n_tensor):
            pl.semaphore_signal(
                barrier, inc=1, device_id=(at.dp, at.tensor ^ offset), device_id_type=MESH)
            count = count + 1
        pl.semaphore_wait(barrier, count)

        def wait(ref, sem):
            pltpu.make_async_copy(ref, ref, sem).wait()

        def lanes(g):
            return (
                pl.ds(pl.multiple_of(g * half, 128), half),
                pl.ds(pl.multiple_of(length - (g + 1) * half, 128), half),
            )

        parts = (pl.ds(0, half), pl.ds(half, half))
        own = lambda j: pl.ds(j * tokens, tokens)
        f1, f2, f3 = [f.at[pl.ds(k * width, width)] for k in range(3)]
        rows_of = lambda b: pl.ds(pl.multiple_of(b * columns, 16), columns)

        def cot_start(j):
            z = (at.dp + j) % at.slices
            for offset in range(group):
                g = at.g ^ offset
                for p in range(2):
                    src = c_ref.at[j, :, lanes(g)[p]]
                    dst = cb.at[pl.ds(pl.multiple_of(j * width + at.tensor * columns, 16), columns), parts[p]]
                    device = (g // 2, z * 2 + g % 2)
                    if offset:
                        pltpu.make_async_remote_copy(src, dst, cot_send.at[j], cot_recv.at[j], device, MESH).start()
                    else:
                        @pl.when(z == at.z)
                        def _():
                            pltpu.make_async_copy(src, dst, cot_recv.at[j]).start()

                        @pl.when(z != at.z)
                        def _():
                            pltpu.make_async_remote_copy(src, dst, cot_own.at[j], cot_recv.at[j], device, MESH).start()

        def cot_finish(j):
            z = (at.dp + j) % at.slices
            wait(c_ref.at[j, :, pl.ds(0, length - 2 * half)], cot_send.at[j])

            @pl.when(z != at.z)
            def _():
                wait(c_ref.at[j, :, pl.ds(0, 2 * half)], cot_own.at[j])

        def act_start(j):
            dp = (at.z - j + at.n_dp) % at.n_dp
            for offset in range(n_tensor):
                b = at.tensor ^ offset
                for p in range(2):
                    src = ab.at[j, rows_of(b), parts[p]]
                    dst = act_o.at[j, :, lanes(at.g)[p]]
                    if offset:
                        pltpu.make_async_remote_copy(src, dst, act_send.at[j], act_recv.at[j], (dp, b), MESH).start()
                    else:
                        @pl.when(dp == at.dp)
                        def _():
                            pltpu.make_async_copy(src, dst, act_recv.at[j]).start()

                        @pl.when(dp != at.dp)
                        def _():
                            pltpu.make_async_remote_copy(src, dst, act_own.at[j], act_recv.at[j], (dp, b), MESH).start()

        def act_finish(j):
            dp = (at.z - j + at.n_dp) % at.n_dp
            wait(ab.at[j, pl.ds(0, width - columns)], act_send.at[j])

            @pl.when(dp != at.dp)
            def _():
                wait(ab.at[j, pl.ds(0, columns)], act_own.at[j])

            wait(act_o.at[j], act_recv.at[j])

        def col_moves(j):
            for offset in range(group):
                device, g_ = at.peer(offset)
                rows = rows_of(at.block_of(g_ // 2, g_ % 2))
                for i, (src, dst) in enumerate((
                    (ub.at[j, rows], gu_o.at[at.g, pl.ds(j * columns, columns)]),
                    (eb.at[j, rows], ge_o.at[at.g, pl.ds(j * columns, columns)]),
                    (xb.at[j, rows, parts[0]], gf_o.at[j, :, lanes(at.g)[0]]),
                    (xb.at[j, rows, parts[1]], gf_o.at[j, :, lanes(at.g)[1]]),
                )):
                    kind = min(i, 2)
                    if offset:
                        yield pltpu.make_async_remote_copy(
                            src, dst, col_send.at[j, kind], col_recv.at[j, kind], device, MESH)
                    else:
                        yield pltpu.make_async_copy(src, dst, col_recv.at[j, kind])

        def col_finish(j):
            rest = pl.ds(0, width - columns)
            wait(ub.at[j, rest], col_send.at[j, 0])
            wait(eb.at[j, rest], col_send.at[j, 1])
            wait(xb.at[j, rest], col_send.at[j, 2])

        def col_arrived(j):
            wait(gu_o.at[:, pl.ds(j * columns, columns)], col_recv.at[j, 0])
            wait(ge_o.at[:, pl.ds(j * columns, columns)], col_recv.at[j, 1])
            wait(gf_o.at[j], col_recv.at[j, 2])

        two = own(2)
        n_pieces = length // tokens

        def slice_at(j):
            z = (at.dp + j) % at.slices
            dp = at.dp_of(at.z)
            return (dp, z * 2 + at.y), jnp.logical_and(dp == at.dp, z == at.z)

        def slice_start(j):
            device, here = slice_at(j)
            for k in range(n_pieces):
                src = x_ref.at[j, :, pl.ds(k * tokens, tokens)]
                dst = a_all.at[pl.ds(j * width + k * columns, columns), two]

                @pl.when(here)
                def _():
                    pltpu.make_async_copy(src, dst, slice_recv.at[j]).start()

                @pl.when(jnp.logical_not(here))
                def _():
                    pltpu.make_async_remote_copy(src, dst, slice_send.at[j], slice_recv.at[j], device, MESH).start()

        def slice_finish(j):
            _, here = slice_at(j)

            @pl.when(jnp.logical_not(here))
            def _():
                wait(x_ref.at[j], slice_send.at[j])

        depth = min(1024, length // 2)
        n_chunks = length // depth
        per = depth // tokens
        def front_slot(i):
            ref = (a_all, m_all)[i % 2]
            return ref.at[pl.ds(i // 2 * depth, depth), own(1)]

        def table_rows(c, g):
            return table_ref.at[pl.ds(pl.multiple_of(g * length + c * depth, 16), depth)]

        order = [(offset, c) for offset in reversed(range(group)) for c in range(n_chunks)]
        def front_load(i):
            offset, c = order[i]
            return pltpu.make_async_copy(table_rows(c, at.g ^ offset), front_slot(i % 6), table_sem.at[i % 6])

        def to_tokens(js, offset, kinds):
            device, g = at.peer(offset)
            rows = rows_of(at.block)
            for j in js:
                moves = []
                if "u" in kinds:
                    moves.append((m_all.at[pl.ds(j * width + offset * columns, columns), two], ub.at[j, rows], 0))
                if "e" in kinds:
                    moves.append((m_all.at[pl.ds(seqs * width + j * columns, columns), pl.ds(2 * tokens, 128)], eb.at[j, rows], 1))
                if "x" in kinds:
                    for p, i in ((0, g), (1, 2 * group - 1 - g)):
                        moves.append((
                            a_all.at[pl.ds(pl.multiple_of(j * width + i // 2 * columns, 16), columns),
                                     pl.ds(pl.multiple_of(2 * tokens + i % 2 * half, 128), half)],
                            xb.at[j, rows, parts[p]], 2))
                for src, dst, kind in moves:
                    if offset:
                        pltpu.make_async_remote_copy(
                            src, dst, tok_send.at[j, kind], tok_recv.at[j, kind], device, MESH).start()
                    else:
                        pltpu.make_async_copy(src, dst, tok_recv.at[j, kind]).start()

        def front_prefetch():
            for i in range(6):
                front_load(i).start()

        def front_pass(js):
            m = len(js) * columns
            def piece(k):
                vals = [a_all[j * width + k * columns : j * width + (k + 1) * columns, 2 * tokens : 3 * tokens] for j in js]
                return vals[0] if len(vals) == 1 else jnp.concatenate(vals, axis=0)
            for offset in range(1, group):
                to_tokens(js, offset, "x")
            edge = jnp.zeros((m, 128), F32)
            for k in range(n_pieces):
                edge = edge + dot(piece(k), edge_v[k * tokens : (k + 1) * tokens, :], 1, 0)
            for i, j in enumerate(js):
                m_all[seqs * width + j * columns : seqs * width + (j + 1) * columns, 2 * tokens : 2 * tokens + 128] = (
                    edge[i * columns : (i + 1) * columns].astype(BF))
            for n, (offset, c) in enumerate(order):
                if c == 0:
                    total = jnp.zeros((m, tokens), F32)
                front_load(n).wait()
                slot = front_slot(n % 6)
                for s_ in range(per):
                    total = total + dot(piece(c * per + s_), slot[pl.ds(s_ * tokens, tokens), :], 1, 0)
                if n + 6 < len(order):
                    front_load(n + 6).start()
                if c == n_chunks - 1:
                    for i, j in enumerate(js):
                        m_all[j * width + offset * columns : j * width + (offset + 1) * columns, 2 * tokens : 3 * tokens] = (
                            total[i * columns : (i + 1) * columns].astype(BF))
                    to_tokens(js, offset, "ue" if offset else "uex")

        def tokens_arrived(j):
            wait(ub.at[j], tok_recv.at[j, 0])
            wait(eb.at[j], tok_recv.at[j, 1])
            wait(xb.at[j], tok_recv.at[j, 2])

        def tokens_sent(j):
            rest = pl.ds(0, width - columns)
            wait(ub.at[j, rest], tok_send.at[j, 0])
            wait(eb.at[j, rest], tok_send.at[j, 1])
            wait(xb.at[j, rest], tok_send.at[j, 2])

        bt = units // n_tensor
        hb, qb = bt // 2, bt // 4
        slices = at.slices
        core, x = at.dp % 2, at.dp // 2 % 2
        flip = lambda bit: (at.dp ^ bit, at.tensor)
        core_peer, x_peer, y_peer = flip(1), flip(2), (at.dp, at.tensor ^ 1)
        z_peer = lambda offset: (at.dp, (at.z ^ offset) * 2 + at.y)
        w_refs, w_bufs = (win_ref, wout_ref), (win, wout)
        n_far = slices - 1

        def piece_rows(o, y, n_quarters, xx):
            start = ((at.z ^ o) * 2 + y) * bt + core * hb + xx * qb
            return pl.ds(pl.multiple_of(start, 16), n_quarters * qb)

        def pass_on(level, arr, rows, key, device):
            ref = w_bufs[arr].at[rows]
            pltpu.make_async_remote_copy(
                ref, ref, gather_send.at[level, arr], gather_recv.at[level, arr, key], device, MESH).start()

        def arrive(level, arr, rows, key):
            wait(w_bufs[arr].at[rows], gather_recv.at[level, arr, key])

        def gather_start():
            mine = pl.ds(pl.multiple_of(core * hb + x * qb, 16), qb)
            half_rows = pl.ds(pl.multiple_of(core * hb, 16), hb)
            for arr in range(2):
                for o in range(1, slices):
                    pltpu.make_async_remote_copy(
                        w_refs[arr].at[mine], w_bufs[arr].at[piece_rows(0, at.y, 1, x)],
                        gather_send.at[0, arr], gather_recv.at[0, arr, o - 1], z_peer(o), MESH).start()
            for arr in range(2):
                pltpu.make_async_remote_copy(
                    w_refs[arr].at[half_rows], w_bufs[arr].at[piece_rows(0, at.y, 2, 0)],
                    gather_send.at[2, arr], gather_recv.at[2, arr, 0], y_peer, MESH).start()
                pltpu.make_async_copy(
                    w_refs[arr], w_bufs[arr].at[pl.ds(pl.multiple_of(at.tensor * bt, 16), bt)], load.at[arr]).start()

        def gather_two():
            for arr in range(2):
                for o in range(1, slices):
                    rows = piece_rows(o, at.y, 1, x)
                    arrive(0, arr, rows, o - 1)
                    pass_on(1, arr, rows, o - 1, x_peer)
                    pass_on(2, arr, rows, 2 * o - 1, y_peer)
                    pass_on(3, arr, rows, 2 * o - 2, core_peer)

        def gather_three():
            for arr in range(2):
                for o in range(1, slices):
                    rows = piece_rows(o, at.y, 1, 1 - x)
                    arrive(1, arr, rows, o - 1)
                    pass_on(2, arr, rows, 2 * o, y_peer)
                    pass_on(3, arr, rows, 2 * o - 1, core_peer)

        def gather_four(arr):
            other = 1 - at.y
            keys = [(0, 2, 0, 0)] + [(o, 1, q, 2 * o - 1 + q) for o in range(1, slices) for q in range(2)]
            for o, n, q, key in keys:
                xx = 0 if n == 2 else (1 - x if q else x)
                rows = piece_rows(o, other, n, xx)
                arrive(2, arr, rows, key)
                pass_on(3, arr, rows, 2 * n_far + key, core_peer)

        def gather_last(arr):
            def theirs(o, y, n, xx):
                start = ((at.z ^ o) * 2 + y) * bt + (1 - core) * hb + xx * qb
                return pl.ds(pl.multiple_of(start, 16), n * qb)
            pltpu.make_async_copy(
                w_refs[arr], w_bufs[arr].at[pl.ds(pl.multiple_of(at.tensor * bt, 16), bt)], load.at[arr]).wait()
            for o in range(1, slices):
                for q in range(2):
                    arrive(3, arr, theirs(o, at.y, 1, 1 - x if q else x), 2 * o - 2 + q)
            arrive(3, arr, theirs(0, 1 - at.y, 2, 0), 2 * n_far)
            for o in range(1, slices):
                for q in range(2):
                    arrive(3, arr, theirs(o, 1 - at.y, 1, 1 - x if q else x), 2 * n_far + 2 * o - 1 + q)

        def gather_sent():
            for arr in range(2):
                g = w_bufs[arr]
                for level, quarters in enumerate((n_far, n_far, 2 + 2 * n_far, 2 * n_far + 2 + 2 * n_far)):
                    wait(g.at[pl.ds(0, quarters * qb)], gather_send.at[level, arr])

        def vectors_start():
            pltpu.make_async_copy(rows_ref, vrows.at[pl.ds(pl.multiple_of(at.tensor * 8, 8), 8)], vec_recv.at[0]).start()
            pltpu.make_async_copy(rows_ref, drows.at[pl.ds(pl.multiple_of(at.dp * 8, 8), 8)], vec_recv.at[1]).start()
            for offset in range(1, n_tensor):
                pltpu.make_async_remote_copy(
                    rows_ref, vrows.at[pl.ds(pl.multiple_of(at.tensor * 8, 8), 8)],
                    vec_send.at[0], vec_recv.at[0], (at.dp, at.tensor ^ offset), MESH).start()
            for offset in range(1, n_dp):
                pltpu.make_async_remote_copy(
                    rows_ref, drows.at[pl.ds(pl.multiple_of(at.dp * 8, 8), 8)],
                    vec_send.at[1], vec_recv.at[1], (at.dp ^ offset, at.tensor), MESH).start()

        def vectors_arrived():
            wait(vrows.at[pl.ds(0, 8 * n_tensor)], vec_recv.at[0])
            wait(drows, vec_recv.at[1])
            wait(vrows.at[pl.ds(0, 8 * (n_tensor - 1))], vec_send.at[0])
            wait(drows.at[pl.ds(0, 8 * (n_dp - 1))], vec_send.at[1])
            turned = vrows[...].T
            for t in range(n_tensor):
                b_in_v[t * bt : (t + 1) * bt, :] = turned[0:bt, 8 * t : 8 * t + 1]
                vec[t * columns : (t + 1) * columns, :] = turned[0:columns, 8 * t + 1 : 8 * t + 6]

        lane0 = lax.broadcasted_iota(jnp.int32, (half, half), 0)
        lane1 = lax.broadcasted_iota(jnp.int32, (half, half), 1)
        turn = jnp.where(lane0 + lane1 == half, 1.0, 0.0).astype(BF)
        edge0 = lax.broadcasted_iota(jnp.int32, (128, half), 0)
        edge1 = lax.broadcasted_iota(jnp.int32, (128, half), 1)
        pick_u = jnp.where((edge0 == 2 * at.g) & (edge1 == 0), 1.0, 0.0).astype(BF)
        pick_v = jnp.where((edge0 == 2 * at.g + 1) & (edge1 == 0), 1.0, 0.0).astype(BF)
        A, B = parts
        block = 256
        step = 32

        def over(rows, size, body, carry=None, unroll=2):
            def inner(i, c):
                r = pl.ds(pl.multiple_of(i * size, size), size)
                return body(r, c)
            return lax.fori_loop(0, rows // size, inner, carry, unroll=unroll)

        def fold(v):
            return jnp.sum(v.reshape(v.shape[0] // 8, 8, v.shape[1]), axis=0)

        def lane_fold(v):
            return sum(v[:, k * 128 : (k + 1) * 128] for k in range(v.shape[1] // 128))

        zeros8 = jnp.zeros((8, tokens), F32)

        def mean_of(total):
            return jnp.sum(total, axis=0, keepdims=True) / width

        def statistics(ref):
            total = over(width, step, lambda r, c: c + fold(ref[r, :]), zeros8)
            center = mean_of(total)
            def spread(r, c):
                off = ref[r, :] - center
                return c + fold(off * off)
            var = mean_of(over(width, step, spread, zeros8))
            return center, lax.rsqrt(var + EPSILON)

        bacc[...] = jnp.zeros_like(bacc)
        vacc[...] = jnp.zeros_like(vacc)

        def forward_mix(j):
            tokens_arrived(j)
            def turned(r, c):
                e = eb[j, r, :]
                tile[r, A] = (dot(ub[j, r, A], turn, 1, 0) + dot(e, pick_u, 1, 0)).astype(BF)
                tile[r, B] = (dot(ub[j, r, B], turn, 1, 0) + dot(e, pick_v, 1, 0)).astype(BF)
                return c
            over(width, block, turned, 0, unroll=1)
            def mixed(r, c):
                f1[r, A] = xb[j, r, A].astype(F32) + mix_scale * (
                    dot(cos[r, :], ub[j, :, A], 1, 0) - dot(sin[r, :], ub[j, :, B], 1, 0))
                f1[r, B] = xb[j, r, B].astype(F32) + mix_scale * (
                    dot(cos[r, :], tile[:, A], 1, 0) + dot(sin[r, :], tile[:, B], 1, 0))
                return c
            over(width, block, mixed, 0, unroll=1)
            center, inverse = statistics(f1)
            def scale(r, c):
                h = (f1[r, :] - center) * inverse
                f1[r, :] = h
                n = h * vec[r, 1:2] + vec[r, 2:3]
                f2[r, :] = n
                nl[r, own(j)] = n.astype(BF)
                return c
            over(width, step, scale, 0)
            return inverse

        c0 = math.sqrt(2.0 / math.pi)
        c1 = c0 * 0.044715

        def forward_mlp(j):
            def inner(r, c):
                v = dot(win[r, :], nl[:, own(j)], 1, 0) + b_in_v[r, :]
                v2 = v * v
                p = 0.5 + 0.5 * jnp.tanh(v * (c0 + c1 * v2))
                a = v * p
                a_all[r, own(j)] = a.astype(BF)
                m_all[r, own(j)] = (p + a * (1.0 - p) * (2.0 * c0 + 6.0 * c1 * v2)).astype(BF)
                return c
            over(units, block, inner, 0, unroll=1)
            def outer(r, c):
                f2[r, :] = f2[r, :] + dot(wout[:, r], a_all[:, own(j)], 0, 0) + vec[r, 0:1]
                return c
            for k in range(width // block):
                outer(pl.ds(k * block, block), 0)

        def second_norm(j):
            center, inverse = statistics(f2)
            flag = drows[pl.ds(pl.multiple_of((at.z - j + at.n_dp) % at.n_dp * 8, 8), 8), 0:128][6:7, j : j + 1]
            def result(r, c):
                h = (f2[r, :] - center) * inverse
                f2[r, :] = h
                ab[j, r, :] = (h * vec[r, 3:4] + vec[r, 4:5]).astype(BF)
                return c
            over(width, step, result, 0)
            act_start(j)
            wait(cb.at[pl.ds(j * width, width)], cot_recv.at[j])
            def sums(r, c):
                go = cb[pl.ds(pl.multiple_of(j * width + r.start, 16), r.size), :].astype(F32) * flag
                h = f2[r, :]
                goh = go * h
                vacc[3, r, :] += lane_fold(goh)
                vacc[4, r, :] += lane_fold(go)
                gh = go * vec[r, 3:4]
                return c[0] + fold(gh), c[1] + fold(gh * h)
            m1, m2 = over(width, step, sums, (zeros8, zeros8))
            m1, m2 = mean_of(m1), mean_of(m2)
            def back(r, c):
                gh = cb[pl.ds(pl.multiple_of(j * width + r.start, 16), r.size), :].astype(F32) * flag * vec[r, 3:4]
                gs = inverse * (gh - m1 - f2[r, :] * m2)
                vacc[0, r, :] += lane_fold(gs)
                f3[r, :] = gs
                gl[r, own(j)] = gs.astype(BF)
                return c
            over(width, step, back, 0)

        def backward_inner(j):
            def inner(r, c):
                gi = dot(wout[r, :], gl[:, own(j)], 1, 0) * m_all[r, own(j)].astype(F32)
                bacc[r, :] += lane_fold(gi)
                m_all[r, own(j)] = gi.astype(BF)
                return c
            over(units, block, inner, 0, unroll=1)

        def backward_outer(j):
            for k in range(width // block):
                r = pl.ds(k * block, block)
                f3[r, :] = f3[r, :] + dot(win[:, r], m_all[:, own(j)], 0, 0)

        def first_back(j, inverse):
            def sums(r, c):
                gn = f3[r, :]
                h = f1[r, :]
                gnh = gn * h
                vacc[1, r, :] += lane_fold(gnh)
                vacc[2, r, :] += lane_fold(gn)
                gh = gn * vec[r, 1:2]
                return c[0] + fold(gh), c[1] + fold(gh * h)
            m1, m2 = over(width, step, sums, (zeros8, zeros8))
            m1, m2 = mean_of(m1), mean_of(m2)
            def back(r, c):
                gf = inverse * (f3[r, :] * vec[r, 1:2] - m1 - f1[r, :] * m2)
                xb[j, r, :] = gf.astype(BF)
                tile[r, :] = (gf * mix_scale).astype(BF)
                return c
            over(width, step, back, 0)
            def fold_pairs(r, c):
                a = tile[r, A].astype(F32)
                b = tile[r, B]
                t = dot(b, turn, 1, 0)
                ub[j, r, A] = (t + a).astype(BF)
                ub[j, r, B] = (t - a).astype(BF)
                eb[j, r, :] = dot(b, pick_u + pick_v, 1, 1).astype(BF)
                return c
            over(width, block, fold_pairs, 0, unroll=1)
            even, odd, edge = ub[j, :, A], ub[j, :, B], eb[j]
            is_cos = lax.broadcasted_iota(jnp.int32, (block, 128), 1) % 2 == 0
            for k in range(width // block):
                r = pl.ds(k * block, block)
                f1[r, A] = dot(cos[r, :], even, 1, 0)
                f1[r, B] = dot(sin[r, :], odd, 1, 0)
                f2[r, 0:128] = jnp.where(is_cos, dot(cos[r, :], edge, 1, 0), dot(sin[r, :], edge, 1, 0))
            def pack(r, c):
                ub[j, r, :] = f1[r, :].astype(BF)
                eb[j, r, :] = f2[r, 0:128].astype(BF)
                return c
            over(width, step, pack, 0)
            for move in col_moves(j):
                move.start()

        grads = (wout, win)
        if seqs * tokens >= 2 * width:
            land = lambda rows, arr: a_all.at[rows, pl.ds(arr * width, width)]
        else:
            land = lambda rows, arr: spare.at[rows, pl.ds(arr * width, width)]
        at2 = n_tensor * hb
        at3 = at2 + slices * hb
        at4 = at3 + slices * qb
        at5 = at4 + (slices - 1) * qb
        land1 = lambda arr, k: land(pl.ds(pl.multiple_of(k * hb, 16), hb), arr)
        land2 = lambda arr, k, n: land(pl.ds(at2 + k * n, n), arr)
        land3 = lambda arr, k: land(pl.ds(at3 + k * qb, qb), arr)
        land4 = lambda arr, k: land(pl.ds(at4 + k * qb, qb), arr)
        land5 = lambda arr: land(pl.ds(at5, qb), arr)
        def block_at(k):
            y = jnp.where(k < slices, 1 - at.y, at.y)
            return (k % slices) * 2 + y
        def rows_half(k, c):
            return pl.ds(pl.multiple_of(block_at(k) * bt + c * hb, 16), hb)
        def rows_quarter(k, xx):
            return pl.ds(pl.multiple_of(block_at(k) * bt + core * hb + xx * qb, 16), qb)

        def send(src, dst, level, arr, k, device):
            pltpu.make_async_remote_copy(
                src, dst, rs_send.at[level, arr], rs_recv.at[level, arr, k], device, MESH).start()

        def ready_signal():
            for i, device in enumerate([core_peer, x_peer, y_peer] + [z_peer(o) for o in range(1, slices)]
                                       + [flip(1 << b) for b in range(2, n_dp.bit_length() - 1)]):
                pl.semaphore_signal(ready.at[i], inc=1, device_id=device, device_id_type=MESH)

        def weight_grads(arr, left, right):
            def tile_step(k, c):
                r = pl.ds(pl.multiple_of(block_at(k) * bt, 16), bt)
                grads[arr][r, :] = dot(left[r, :], right[...], 1, 1).astype(BF)
                return c
            lax.fori_loop(0, n_tensor, tile_step, 0)

        def level1(arr):
            def go(k, c):
                send(grads[arr].at[rows_half(k, 1 - core)], land1(arr, k), 0, arr, k, core_peer)
                return c
            lax.fori_loop(0, n_tensor, go, 0)

        def add(arr, rows, landed, level, k):
            wait(landed, rs_recv.at[level, arr, k])
            ref = grads[arr].at[rows]
            n = ref.shape[0]
            def go(i, c):
                r = pl.ds(pl.multiple_of(i * 16, 16), 16)
                ref[r, :] = (ref[r, :].astype(F32) + landed[r, :].astype(F32)).astype(BF)
                return c
            lax.fori_loop(0, n // 16, go, 0, unroll=2)

        def after1(arr):
            def go(k, c):
                add(arr, rows_half(k, core), land1(arr, k), 0, k)
                if arr == 0:
                    @pl.when(k < slices)
                    def _():
                        send(grads[arr].at[rows_half(k, core)], land2(arr, k, hb), 1, arr, k, y_peer)
                else:
                    send(grads[arr].at[rows_quarter(k, 1 - x)], land2(arr, k, qb), 1, arr, k, x_peer)
                return c
            lax.fori_loop(0, n_tensor, go, 0)

        def after2(arr):
            if arr == 0:
                def go(k, c):
                    add(arr, rows_half(slices + k, core), land2(arr, k, hb), 1, k)
                    send(grads[arr].at[rows_quarter(slices + k, 1 - x)], land3(arr, k), 2, arr, k, x_peer)
                    return c
                lax.fori_loop(0, slices, go, 0)
            else:
                def go(k, c):
                    add(arr, rows_quarter(k, x), land2(arr, k, qb), 1, k)
                    @pl.when(k < slices)
                    def _():
                        send(grads[arr].at[rows_quarter(k, x)], land3(arr, k), 2, arr, k, y_peer)
                    return c
                lax.fori_loop(0, n_tensor, go, 0)

        def after3(arr):
            for offset in range(slices):
                k = at.z ^ offset
                add(arr, rows_quarter(slices + k, x), land3(arr, k), 2, k)
                if offset:
                    send(grads[arr].at[rows_quarter(slices + k, x)], land4(arr, offset - 1), 3, arr, offset - 1, z_peer(offset))

        def after4(arr):
            mine = rows_quarter(slices + at.z, x)
            for offset in range(1, slices):
                add(arr, mine, land4(arr, offset - 1), 3, offset - 1)
            for b in range(2, n_dp.bit_length() - 1):
                k = b - 2
                peer_ = flip(1 << b)
                pltpu.make_async_remote_copy(
                    grads[arr].at[mine], land5(arr), more_send.at[arr, k], more_recv.at[arr, k], peer_, MESH).start()
                wait(grads[arr].at[mine], more_send.at[arr, k])
                wait(land5(arr), more_recv.at[arr, k])
                ref = grads[arr].at[mine]
                ref[...] = (ref[...].astype(F32) + land5(arr)[...].astype(F32)).astype(BF)
                if b + 1 < n_dp.bit_length() - 1:
                    pl.semaphore_signal(more_free, inc=1, device_id=peer_, device_id_type=MESH)
                    pl.semaphore_wait(more_free, 1)
            home = pl.ds(pl.multiple_of(core * hb + x * qb, 16), qb)
            out = (gout_o, gin_o)[arr]
            pltpu.make_async_copy(grads[arr].at[mine], out.at[home], rs_recv.at[4, arr, 0]).start()
            for q in range(1, 4):
                pltpu.make_async_remote_copy(
                    grads[arr].at[mine], out.at[home], rs_send.at[4, arr], rs_recv.at[4, arr, q], flip(q), MESH).start()

        def rs_finish(arr):
            g = grads[arr]
            n = n_tensor * hb
            wait(g.at[pl.ds(0, n)], rs_send.at[0, arr])
            wait(g.at[pl.ds(0, slices * hb)], rs_send.at[1, arr])
            wait(g.at[pl.ds(0, slices * qb)], rs_send.at[2, arr])
            wait(g.at[pl.ds(0, (slices - 1) * qb)], rs_send.at[3, arr])
            wait(g.at[pl.ds(0, 3 * qb)], rs_send.at[4, arr])
            for q in range(4):
                wait((gout_o, gin_o)[arr].at[pl.ds(0, qb)], rs_recv.at[4, arr, q])

        every = seqs * columns
        n_slots = 6
        slot_ref = lambda i: m_all.at[pl.ds(i // 2 * depth, depth), pl.ds((1 + i % 2) * tokens, tokens)]
        def table_start(i):
            c, g = i // group, i % group
            rows = pl.ds(g * length + c * depth, depth)
            return pltpu.make_async_copy(table_ref.at[rows], slot_ref(i % n_slots), table_sem.at[i % n_slots])

        def words_back():
            steps = [(c, g) for c in range(n_chunks) for g in range(group)]
            for i in range(n_slots):
                table_start(i).start()
            for j in range(seqs):
                col_arrived(j)
            for g in range(group):
                pltpu.make_async_copy(gu_o.at[g], cb.at[pl.ds(g * every, every)], table_sem.at[n_slots + 1]).start()
            for g in range(group):
                pltpu.make_async_copy(ge_o.at[g], m_all.at[pl.ds(g * every, every), pl.ds(0, 128)], table_sem.at[n_slots + 2]).start()
            for j in range(seqs):
                for k in range(length // tokens):
                    pltpu.make_async_copy(
                        gf_o.at[j, :, pl.ds(k * tokens, tokens)], nl.at[pl.ds(k * columns, columns), own(j)],
                        table_sem.at[n_slots + 3]).start()
            wait(cb, table_sem.at[n_slots + 1])
            wait(m_all.at[pl.ds(0, group * every), pl.ds(0, 128)], table_sem.at[n_slots + 2])
            wait(nl, table_sem.at[n_slots + 3])
            edge = m_all[0:every, 0:128].astype(F32)
            for g in range(1, group):
                edge = edge + m_all[g * every : (g + 1) * every, 0:128].astype(F32)
            edge = edge.astype(BF)
            for c in range(n_chunks):
                for s_ in range(per):
                    k = c * per + s_
                    acc = pl.ds(k * every, every)
                    f[acc, :] = dot(edge, edge_v[k * tokens : (k + 1) * tokens, :], 1, 1)
                for g in range(group):
                    i = c * group + g
                    table_start(i).wait()
                    for s_ in range(per):
                        acc = pl.ds((c * per + s_) * every, every)
                        f[acc, :] += dot(cb[pl.ds(g * every, every), :], slot_ref(i % n_slots)[pl.ds(s_ * tokens, tokens), :], 1, 1)
                    if i + n_slots < n_chunks * group:
                        table_start(i + n_slots).start()
                for s_ in range(per):
                    k = c * per + s_
                    for j in range(seqs):
                        rows = pl.ds(k * columns, columns)
                        gl[rows, own(j)] = (
                            f[pl.ds(k * every + j * columns, columns), :] + nl[rows, own(j)].astype(F32)).astype(BF)
                        home_start(j, k)

        def home_at(j):
            dp = (at.z - j + at.n_dp) % at.n_dp
            return dp, jnp.logical_and(dp == at.dp, at.block == at.tensor)

        def home_start(j, k):
            dp, here = home_at(j)
            src = gl.at[pl.ds(k * columns, columns), own(j)]
            dst = gw_o.at[j, :, pl.ds(k * tokens, tokens)]

            @pl.when(here)
            def _():
                pltpu.make_async_copy(src, dst, home_recv.at[j]).start()

            @pl.when(jnp.logical_not(here))
            def _():
                pltpu.make_async_remote_copy(src, dst, home_send.at[j], home_recv.at[j], (dp, at.block), MESH).start()

        def home_finish(j):
            dp, here = home_at(j)

            @pl.when(jnp.logical_not(here))
            def _():
                wait(gw_o.at[j], home_send.at[j])

            wait(gw_o.at[j], home_recv.at[j])

        def vector_grads():
            cols = pl.ds(0, 128)
            vrows[...] = jnp.zeros_like(vrows)
            turned = jnp.zeros((wide, 128), F32)
            scratch = f1.at[pl.ds(0, wide), cols]
            scratch[...] = turned
            for t in range(n_tensor):
                scratch[0:bt, 8 * t : 8 * t + 1] = jnp.sum(bacc[t * bt : (t + 1) * bt, :], axis=1, keepdims=True)
                for i in range(5):
                    scratch[0:columns, 8 * t + 1 + i : 8 * t + 2 + i] = jnp.sum(
                        vacc[i, t * columns : (t + 1) * columns, :], axis=1, keepdims=True)
            vrows[...] = scratch[...].T
            n = 8 * n_tensor
            for offset in range(1, n_dp):
                pltpu.make_async_remote_copy(
                    vrows.at[pl.ds(0, n)], grows.at[pl.ds((offset - 1) * n, n)],
                    vg_send.at[0], vg_recv.at[0], (at.dp ^ offset, at.tensor), MESH).start()

        def vector_grads_two():
            n = 8 * n_tensor
            wait(grows.at[pl.ds(0, (n_dp - 1) * n)], vg_recv.at[0])
            wait(grows.at[pl.ds(0, (n_dp - 1) * n)], vg_send.at[0])
            total = vrows[0:n, :]
            for offset in range(1, n_dp):
                total = total + grows[(offset - 1) * n : offset * n, :]
            vrows[0:n, :] = total
            for offset in range(1, n_tensor):
                t = at.tensor ^ offset
                pltpu.make_async_remote_copy(
                    vrows.at[pl.ds(pl.multiple_of(t * 8, 8), 8)], drows2.at[pl.ds((offset - 1) * 8, 8)],
                    vg_send.at[1], vg_recv.at[1], (at.dp, t), MESH).start()

        def vector_grads_three():
            n = 8 * (n_tensor - 1)
            wait(drows2.at[pl.ds(0, n)], vg_recv.at[1])
            wait(drows2.at[pl.ds(0, n)], vg_send.at[1])
            total = vrows[pl.ds(pl.multiple_of(at.tensor * 8, 8), 8), :]
            for offset in range(1, n_tensor):
                total = total + drows2[(offset - 1) * 8 : offset * 8, :]
            vec_o[...] = total

        tables = [
            pltpu.make_async_copy(src, dst, load.at[2 + i])
            for i, (src, dst) in enumerate(((edge_ref, edge_v), (cos_ref, cos), (sin_ref, sin)))
        ]
        slice_start(0)
        vectors_start()
        gather_start()
        for move in tables:
            move.start()
        front_prefetch()
        wait(a_all.at[pl.ds(0, width), two], slice_recv.at[0])
        for j in range(1, seqs):
            slice_start(j)
        tables[0].wait()
        front_pass([0])
        front_prefetch()
        gather_two()
        for j in range(seqs):
            cot_start(j)
        gather_three()
        tables[1].wait()
        tables[2].wait()
        vectors_arrived()
        for j in range(seqs):
            if j == 0:
                inverse = forward_mix(0)
                for arr in range(2):
                    gather_four(arr)
                for arr in range(2):
                    gather_last(arr)
            else:
                inverse = forward_mix(j)
            if j == 2:
                for i in range(seqs):
                    tokens_sent(i)
            forward_mlp(j)
            if j == 0:
                for i in range(1, seqs):
                    wait(a_all.at[pl.ds(i * width, width), two], slice_recv.at[i])
                front_pass(list(range(1, seqs)))
            second_norm(j)
            backward_inner(j)
            if j == seqs - 1:
                gather_sent()
                weight_grads(0, a_all, gl)
                ready_signal()
                pl.semaphore_wait(ready.at[0], 1)
                level1(0)
            backward_outer(j)
            if j == seqs - 1:
                weight_grads(1, m_all, nl)
                level1(1)
            first_back(j, inverse)
        vector_grads()
        for i in range(1, 3 + slices - 1 + max(0, n_dp.bit_length() - 3)):
            pl.semaphore_wait(ready.at[i], 1)
        after1(0)
        after1(1)
        vector_grads_two()
        words_back()
        after2(0)
        after2(1)
        after3(0)
        after3(1)
        after4(0)
        after4(1)
        for j in range(seqs):
            slice_finish(j)
            cot_finish(j)
            act_finish(j)
            col_finish(j)
            home_finish(j)
        vector_grads_three()
        rs_finish(0)
        rs_finish(1)

    shape = jax.ShapeDtypeStruct
    dma = pltpu.SemaphoreType.DMA
    whole_vmem = pl.BlockSpec(memory_space=pltpu.VMEM)
    need_spare = seqs * tokens < 2 * width
    regular = pltpu.SemaphoreType.REGULAR
    activations, _, _, _, gw, g_in, g_out, vec_g = pl.pallas_call(
        layer_body,
        out_shape=[
            shape(words.shape, BF),
            shape((group, seqs * columns, tokens), BF),
            shape((group, seqs * columns, 128), BF),
            shape((seqs, columns, length), BF),
            shape((seqs, columns, length), BF),
            shape(w_in.shape, BF),
            shape(w_in.shape, BF),
            shape((8, wide), F32),
        ],
        in_specs=[ANY] * 9,
        out_specs=[ANY] * 7 + [whole_vmem],
        scratch_shapes=[
            pltpu.VMEM((units, width), BF),
            pltpu.VMEM((units, width), BF),
            pltpu.VMEM((width, width), BF),
            pltpu.VMEM((width, width), BF),
            pltpu.VMEM((seqs, width, tokens), BF),
            pltpu.VMEM((seqs, width, tokens), BF),
            pltpu.VMEM((seqs, width, 128), BF),
            pltpu.VMEM((group * seqs * columns, tokens), BF),
            pltpu.VMEM((seqs, width, tokens), BF),
            pltpu.VMEM((units, seqs * tokens), BF),
            pltpu.VMEM((units, seqs * tokens), BF),
            pltpu.VMEM((width, seqs * tokens), BF),
            pltpu.VMEM((width, seqs * tokens), BF),
            pltpu.VMEM((3 * width, tokens), F32),
            pltpu.VMEM((width, tokens), BF),
            pltpu.VMEM((length, 128), BF),
            pltpu.VMEM((units, 128), F32),
            pltpu.VMEM((5, width, 128), F32),
            pltpu.VMEM((units, 1), F32),
            pltpu.VMEM((width, 5), F32),
            pltpu.VMEM((128, wide), F32),
            pltpu.VMEM((8 * n_dp, wide), F32),
            pltpu.VMEM((8 * n_tensor * (n_dp - 1), wide), F32),
            pltpu.VMEM((8 * (n_tensor - 1), wide), F32),
            pltpu.VMEM((units, 2 * width) if need_spare else (16, 128), BF),
            dma((5,)),
            dma((seqs,)),
            dma((seqs,)),
            dma((seqs, 3)),
            dma((seqs, 3)),
            dma((2,)),
            dma((2,)),
            dma((4, 2)),
            dma((4, 2, 2 * n_tensor)),
            dma((seqs,)),
            dma((seqs,)),
            dma((seqs,)),
            dma((seqs,)),
            dma((seqs,)),
            dma((seqs,)),
            dma((seqs, 3)),
            dma((seqs, 3)),
            regular((3 + n_tensor // 2 + n_dp,)),
            dma((5, 2)),
            dma((5, 2, n_tensor)),
            dma((10,)),
            dma((seqs,)),
            dma((seqs,)),
            dma((2, n_dp)),
            dma((2, n_dp)),
            regular,
            dma((2,)),
            dma((2,)),
        ],
        compiler_params=pltpu.CompilerParams(
            collective_id=1, has_side_effects=True, vmem_limit_bytes=64 * 1024 * 1024
        ),
    )(
        words, cotangent, w_in, w_out, jnp.asarray(hid_cos), jnp.asarray(hid_sin), table, edge_table, rows_in
    )
    grad_words = gw.astype(F32)

    grad_w_in = g_in.astype(F32)
    grad_w_out = g_out.astype(F32)
    return (
        activations,
        grad_words,
        grad_w_in,
        vec_g[0, : w_in.shape[0]],
        grad_w_out,
        vec_g[1, :columns],
        vec_g[2, :columns],
        vec_g[3, :columns],
        vec_g[4, :columns],
        vec_g[5, :columns],
    )


def solution(mesh):
    spec = (
        P("dp", "tensor", None),
        P("tensor", None),
        P("tensor"),
        P("tensor", None),
        P("tensor"),
        P("tensor"),
        P("tensor"),
        P("tensor"),
        P("tensor"),
        P("dp", "tensor", None),
        P("dp"),
    )
    out = (
        P("dp", "tensor", None),
        P("dp", "tensor", None),
        P("tensor", None),
        P("tensor"),
        P("tensor", None),
        P("tensor"),
        P("tensor"),
        P("tensor"),
        P("tensor"),
        P("tensor"),
    )
    return jax.shard_map(on_device, mesh=mesh, in_specs=spec, out_specs=out, check_vma=False)
```

```python
import math

import jax
import jax.numpy as jnp
import numpy as np
from jax import lax
from jax.experimental import pallas as pl
from jax.experimental.pallas import tpu as pltpu
from jax.sharding import PartitionSpec as P

EPSILON = 1e-12
MESH = pl.DeviceIdType.MESH
BF = jnp.bfloat16
F32 = jnp.float32


def token_tables(length, group):
    half = length // (2 * group)

    def wave(n, k):
        angle = (n[:, None] * k[None, :] % length) * (2.0 * math.pi / length)
        return np.cos(angle), np.sin(angle)

    n = np.arange(length, dtype=np.int64)
    k = np.arange(length // 2).reshape(group, half)
    columns = np.stack([k[:, 0::2], k[:, 1::2]], axis=1)
    cos, sin = wave(n[: length // 2], columns.reshape(-1))
    shape = (length // 2, group, 2, 1, half // 2)
    main = np.concatenate([cos.reshape(shape), sin.reshape(shape)], axis=3)
    main = main.reshape(length // 2, group, 2 * half).transpose(1, 0, 2).reshape(-1, 2 * half)
    edge_cos, edge_sin = wave(half * (np.arange(group) + 1), n)
    edge = np.stack([edge_cos, np.where(np.abs(edge_sin) < 1e-9, 0.0, edge_sin)], axis=1)
    return main.astype(BF), edge.reshape(2 * group, length).astype(BF)


def hidden_tables(width):
    ids = np.arange(width, dtype=np.int64)
    angle = (ids[:, None] * ids[None, :] % width) * (2.0 * math.pi / width)
    return np.cos(angle).astype(BF), np.sin(angle).astype(BF)


class Place:
    def __init__(self, n_dp, n_tensor):
        self.n_dp, self.n_tensor = n_dp, n_tensor
        self.slices = n_tensor // 2
        self.group = 2 * n_dp
        self.dp = lax.axis_index("dp")
        self.tensor = lax.axis_index("tensor")
        self.z = self.tensor // 2
        self.y = self.tensor % 2
        self.g = self.dp * 2 + self.y
        self.block = self.block_of(self.dp, self.y)

    def block_of(self, dp, y):
        return ((dp % (self.n_dp // 2)) * 2 + dp // (self.n_dp // 2)) * 2 + y

    def dp_of(self, z):
        return (z % 2) * (self.n_dp // 2) + z // 2

    def z_of(self, j):
        return ((self.dp % 2) * (self.n_dp // 2) + self.dp // 2) ^ j

    def dp_from(self, j):
        v = self.z ^ j
        return (v % (self.n_dp // 2)) * 2 + v // (self.n_dp // 2)

    def peer(self, offset):
        g = self.g ^ offset
        return (g // 2, self.z * 2 + g % 2), g


ANY = pl.BlockSpec(memory_space=pl.ANY)


def on_device(
    words, w_in, b_in, w_out, b_out, gain_one, shift_one, gain_two, shift_two, cotangent, valid
):
    seqs, columns, length = words.shape
    width = w_in.shape[1]
    n_dp, n_tensor = lax.axis_size("dp"), lax.axis_size("tensor")
    assert n_tensor == 2 * n_dp
    group = 2 * n_dp
    half = length // (2 * group)
    mix_scale = 1.0 / math.sqrt(length * width)
    table, edge_table = token_tables(length, group)
    hid_cos, hid_sin = hidden_tables(width)

    table = jnp.asarray(table)
    edge_table = jnp.asarray(edge_table)
    units = w_in.shape[0] * n_tensor
    tokens = 2 * half

    def dot(a, b, da, db):
        return lax.dot_general(a, b, (((da,), (db,)), ((), ())), preferred_element_type=F32)

    wide = 512
    pad = lambda v: jnp.pad(v, (0, wide - v.shape[0]))
    rows_in = jnp.stack(
        [pad(v) for v in (b_in, b_out, gain_one, shift_one, gain_two, shift_two, valid.astype(F32))]
        + [jnp.zeros((wide,), F32)]
    )

    n_slots = 4

    def layer_body(
        x_ref, c_ref, win_ref, wout_ref, cos_ref, sin_ref, table_ref, edge_ref, rows_ref,
        act_o, gu_o, ge_o, gf_o, gw_o, gin_o, gout_o, vec_o,
        win, wout, cos, sin, xb, ub, eb, cb, ab, a_all, m_all, nl, gl, f, tile, edge_v, slots,
        perm, e_send, bacc, vacc, b_in_v, vec, vrows, drows, grows, drows2, spare,
        load, slice_send, slice_recv, tok_send, tok_recv, vec_send, vec_recv, gather_send, gather_recv,
        cot_send, cot_own, cot_recv, act_send, act_own, act_recv, col_send, col_recv,
        ready, rs_send, rs_recv, table_sem, home_send, home_recv, more_send, more_recv, more_free,
        vg_send, vg_recv,
    ):
        at = Place(n_dp, n_tensor)
        barrier = pltpu.get_barrier_semaphore()
        others = n_dp * n_tensor - 1
        def greet(i, c):
            k = (at.dp * n_tensor + at.tensor + i) % (others + 1)
            pl.semaphore_signal(
                barrier, inc=1, device_id=(k // n_tensor, k % n_tensor), device_id_type=MESH)
            return c
        lax.fori_loop(1, others + 1, greet, 0)
        pl.semaphore_wait(barrier, others)

        def wait(ref, sem):
            pltpu.make_async_copy(ref, ref, sem).wait()

        def lanes(g):
            return (
                pl.ds(pl.multiple_of(g * half, 128), half),
                pl.ds(pl.multiple_of(length - (g + 1) * half, 128), half),
            )

        parts = (pl.ds(0, half), pl.ds(half, half))
        own = lambda j: pl.ds(j * tokens, tokens)
        f1, f2, f3 = [f.at[pl.ds(k * width, width)] for k in range(3)]
        rows_of = lambda b: pl.ds(pl.multiple_of(b * columns, 16), columns)

        def cot_start(j):
            z = at.z_of(j)
            for offset in range(group):
                g = at.g ^ offset
                for p in range(2):
                    src = c_ref.at[j, :, lanes(g)[p]]
                    dst = cb.at[pl.ds(pl.multiple_of(j * width + at.tensor * columns, 16), columns), parts[p]]
                    device = (g // 2, z * 2 + g % 2)
                    if offset:
                        pltpu.make_async_remote_copy(src, dst, cot_send.at[j], cot_recv.at[j], device, MESH).start()
                    else:
                        @pl.when(z == at.z)
                        def _():
                            pltpu.make_async_copy(src, dst, cot_recv.at[j]).start()

                        @pl.when(z != at.z)
                        def _():
                            pltpu.make_async_remote_copy(src, dst, cot_own.at[j], cot_recv.at[j], device, MESH).start()

        def cot_finish(j):
            z = at.z_of(j)
            wait(c_ref.at[j, :, pl.ds(0, length - 2 * half)], cot_send.at[j])

            @pl.when(z != at.z)
            def _():
                wait(c_ref.at[j, :, pl.ds(0, 2 * half)], cot_own.at[j])

        def act_start(j):
            dp = at.dp_from(j)
            for offset in range(n_tensor):
                b = at.tensor ^ offset
                for p in range(2):
                    src = ab.at[j, rows_of(b), parts[p]]
                    dst = act_o.at[j, :, lanes(at.g)[p]]
                    if offset:
                        pltpu.make_async_remote_copy(src, dst, act_send.at[j], act_recv.at[j], (dp, b), MESH).start()
                    else:
                        @pl.when(dp == at.dp)
                        def _():
                            pltpu.make_async_copy(src, dst, act_recv.at[j]).start()

                        @pl.when(dp != at.dp)
                        def _():
                            pltpu.make_async_remote_copy(src, dst, act_own.at[j], act_recv.at[j], (dp, b), MESH).start()

        def act_sent(j):
            dp = at.dp_from(j)
            wait(ab.at[j, pl.ds(0, width - columns)], act_send.at[j])

            @pl.when(dp != at.dp)
            def _():
                wait(ab.at[j, pl.ds(0, columns)], act_own.at[j])

            wait(act_o.at[j], act_recv.at[j])

        def col_moves(j):
            for offset in range(group):
                device, g_ = at.peer(offset)
                rows = rows_of(at.block_of(g_ // 2, g_ % 2))
                for i, (src, dst) in enumerate((
                    (ub.at[j, rows], gu_o.at[at.g, pl.ds(j * columns, columns)]),
                    (eb.at[j, pl.ds(pl.multiple_of(at.block_of(g_ // 2, g_ % 2) * er, 16), er)], ge_o.at[at.g, pl.ds(j * er, er)]),
                    (xb.at[j, rows, parts[0]], gf_o.at[j, :, lanes(at.g)[0]]),
                    (xb.at[j, rows, parts[1]], gf_o.at[j, :, lanes(at.g)[1]]),
                )):
                    kind = min(i, 2)
                    if offset:
                        yield pltpu.make_async_remote_copy(
                            src, dst, col_send.at[j, kind], col_recv.at[j, kind], device, MESH)
                    else:
                        yield pltpu.make_async_copy(src, dst, col_recv.at[j, kind])

        def col_finish(j):
            rest = pl.ds(0, width - columns)
            wait(ub.at[j, rest], col_send.at[j, 0])
            wait(eb.at[j, pl.ds(0, (n_tensor - 1) * er)], col_send.at[j, 1])
            wait(xb.at[j, rest], col_send.at[j, 2])

        def col_arrived(j):
            wait(gu_o.at[:, pl.ds(j * columns, columns)], col_recv.at[j, 0])
            wait(ge_o.at[:, pl.ds(j * er, er)], col_recv.at[j, 1])
            wait(gf_o.at[j], col_recv.at[j, 2])

        two = own(2)
        n_pieces = length // tokens

        def slice_at(j):
            z = at.z_of(j)
            dp = at.dp_of(at.z)
            return (dp, z * 2 + at.y), jnp.logical_and(dp == at.dp, z == at.z)

        def slice_start(j):
            device, here = slice_at(j)
            for k in range(n_pieces):
                src = x_ref.at[j, :, pl.ds(k * tokens, tokens)]
                dst = a_all.at[pl.ds(j * width + k * columns, columns), two]

                @pl.when(here)
                def _():
                    pltpu.make_async_copy(src, dst, slice_recv.at[j]).start()

                @pl.when(jnp.logical_not(here))
                def _():
                    pltpu.make_async_remote_copy(src, dst, slice_send.at[j], slice_recv.at[j], device, MESH).start()

        def slice_finish(j):
            _, here = slice_at(j)

            @pl.when(jnp.logical_not(here))
            def _():
                wait(x_ref.at[j], slice_send.at[j])

        n_chunks = length // 2 // depth
        per = depth // tokens
        er = 2 * group
        edge_rows = lambda b: pl.ds(pl.multiple_of(b * er, 16), er)
        def slot_at(i):
            return slots.at[pl.ds(i % n_slots * depth, depth)]

        def table_rows(c, g):
            return table_ref.at[pl.ds(pl.multiple_of(g * (length // 2) + c * depth, 16), depth)]

        order = [(offset, c) for offset in reversed(range(group)) for c in range(n_chunks)]
        def front_load(i):
            offset, c = order[i]
            return pltpu.make_async_copy(table_rows(c, at.g ^ offset), slot_at(i), table_sem.at[i % n_slots])

        def to_tokens(js, offset, kinds):
            device, g = at.peer(offset)
            rows = rows_of(at.block)
            for j in js:
                moves = []
                if "u" in kinds:
                    moves.append((m_all.at[pl.ds(j * width + offset * columns, columns), two], ub.at[j, rows], 0))
                if "e" in kinds:
                    moves.append((e_send.at[pl.ds(j * er, er)], eb.at[j, edge_rows(at.block)], 1))
                if "x" in kinds:
                    for p, i in ((0, g), (1, 2 * group - 1 - g)):
                        moves.append((
                            a_all.at[pl.ds(pl.multiple_of(j * width + i // 2 * columns, 16), columns),
                                     pl.ds(pl.multiple_of(2 * tokens + i % 2 * half, 128), half)],
                            xb.at[j, rows, parts[p]], 2))
                for src, dst, kind in moves:
                    if offset:
                        pltpu.make_async_remote_copy(
                            src, dst, tok_send.at[j, kind], tok_recv.at[j, kind], device, MESH).start()
                    else:
                        pltpu.make_async_copy(src, dst, tok_recv.at[j, kind]).start()

        def front_prefetch():
            for i in range(n_slots):
                front_load(i).start()

        def front_pass(js, first):
            m = len(js) * columns
            for offset in range(1, group):
                to_tokens(js[:first], offset, "x")
            for i, j in enumerate(js):
                edge = jnp.zeros((er, columns), F32)
                for k in range(n_pieces // 2):
                    k2 = k + n_pieces // 2
                    low = a_all[j * width + k * columns : j * width + (k + 1) * columns, 2 * tokens : 3 * tokens]
                    high = a_all[j * width + k2 * columns : j * width + (k2 + 1) * columns, 2 * tokens : 3 * tokens]
                    edge = edge + dot(edge_v[:, k * tokens : (k + 1) * tokens], low, 1, 1)
                    edge = edge + dot(edge_v[:, k2 * tokens : (k2 + 1) * tokens], high, 1, 1)
                    low, high = low.astype(F32), high.astype(F32)
                    rows = pl.ds(k * m + i * columns, columns)
                    nl[rows, two] = (low + high).astype(BF)
                    gl[rows, two] = (low - high).astype(BF)
                e_send[j * er : (j + 1) * er, 0:columns] = edge.astype(BF)
            for n, (offset, c) in enumerate(order):
                if c == 0:
                    even = jnp.zeros((m, half), F32)
                    odd = jnp.zeros((m, half), F32)
                front_load(n).wait()
                slot = slot_at(n)
                for s_ in range(per):
                    k = c * per + s_
                    rows = pl.ds(s_ * tokens, tokens)
                    even = even + dot(nl[k * m : (k + 1) * m, two], slot[rows, A], 1, 0)
                    odd = odd + dot(gl[k * m : (k + 1) * m, two], slot[rows, B], 1, 0)
                if n + n_slots < len(order):
                    front_load(n + n_slots).start()
                if c == n_chunks - 1:
                    for i, j in enumerate(js):
                        rows = pl.ds(j * width + offset * columns, columns)
                        mine = slice(i * columns, (i + 1) * columns)
                        m_all[rows, 2 * tokens : 2 * tokens + half] = even[mine].astype(BF)
                        m_all[rows, 2 * tokens + half : 3 * tokens] = odd[mine].astype(BF)
                    to_tokens(js[:first], offset, "ue" if offset else "uex")

        def later_tokens(j):
            for offset in reversed(range(group)):
                to_tokens([j], offset, "uex")

        def tokens_arrived(j):
            wait(ub.at[j], tok_recv.at[j, 0])
            wait(eb.at[j], tok_recv.at[j, 1])
            wait(xb.at[j], tok_recv.at[j, 2])

        def tokens_sent(j):
            rest = pl.ds(0, width - columns)
            wait(ub.at[j, rest], tok_send.at[j, 0])
            wait(eb.at[j, pl.ds(0, (n_tensor - 1) * er)], tok_send.at[j, 1])
            wait(xb.at[j, rest], tok_send.at[j, 2])

        bt = units // n_tensor
        hb, qb = bt // 2, bt // 4
        slices = at.slices
        core, x = at.dp % 2, at.dp // 2 % 2
        flip = lambda bit: (at.dp ^ bit, at.tensor)
        core_peer, x_peer, y_peer = flip(1), flip(2), (at.dp, at.tensor ^ 1)
        z_peer = lambda offset: (at.dp, (at.z ^ offset) * 2 + at.y)
        w_refs, w_bufs = (win_ref, wout_ref), (win, wout)
        n_far = slices - 1

        def piece_rows(o, y, n_quarters, xx):
            start = ((at.z ^ o) * 2 + y) * bt + core * hb + xx * qb
            return pl.ds(pl.multiple_of(start, 16), n_quarters * qb)

        def pass_on(level, arr, rows, key, device):
            ref = w_bufs[arr].at[rows]
            pltpu.make_async_remote_copy(
                ref, ref, gather_send.at[level, arr], gather_recv.at[level, arr, key], device, MESH).start()

        def arrive(level, arr, rows, key):
            wait(w_bufs[arr].at[rows], gather_recv.at[level, arr, key])

        def gather_one():
            mine = pl.ds(pl.multiple_of(core * hb + x * qb, 16), qb)
            for arr in range(2):
                for o in range(1, slices):
                    pltpu.make_async_remote_copy(
                        w_refs[arr].at[mine], w_bufs[arr].at[piece_rows(0, at.y, 1, x)],
                        gather_send.at[0, arr], gather_recv.at[0, arr, o - 1], z_peer(o), MESH).start()

        def gather_start():
            half_rows = pl.ds(pl.multiple_of(core * hb, 16), hb)
            for arr in range(2):
                pltpu.make_async_remote_copy(
                    w_refs[arr].at[half_rows], w_bufs[arr].at[piece_rows(0, at.y, 2, 0)],
                    gather_send.at[2, arr], gather_recv.at[2, arr, 0], y_peer, MESH).start()
                pltpu.make_async_copy(
                    w_refs[arr], w_bufs[arr].at[pl.ds(pl.multiple_of(at.tensor * bt, 16), bt)], load.at[arr]).start()

        def gather_two():
            for arr in range(2):
                for o in range(1, slices):
                    rows = piece_rows(o, at.y, 1, x)
                    arrive(0, arr, rows, o - 1)
                    pass_on(1, arr, rows, o - 1, x_peer)
                    pass_on(2, arr, rows, 2 * o - 1, y_peer)
                    pass_on(3, arr, rows, 2 * o - 2, core_peer)

        def gather_three():
            for arr in range(2):
                for o in range(1, slices):
                    rows = piece_rows(o, at.y, 1, 1 - x)
                    arrive(1, arr, rows, o - 1)
                    pass_on(2, arr, rows, 2 * o, y_peer)
                    pass_on(3, arr, rows, 2 * o - 1, core_peer)

        def gather_four(arr):
            other = 1 - at.y
            keys = [(0, 2, 0, 0)] + [(o, 1, q, 2 * o - 1 + q) for o in range(1, slices) for q in range(2)]
            for o, n, q, key in keys:
                xx = 0 if n == 2 else (1 - x if q else x)
                rows = piece_rows(o, other, n, xx)
                arrive(2, arr, rows, key)
                pass_on(3, arr, rows, 2 * n_far + key, core_peer)

        def gather_last(arr):
            def theirs(o, y, n, xx):
                start = ((at.z ^ o) * 2 + y) * bt + (1 - core) * hb + xx * qb
                return pl.ds(pl.multiple_of(start, 16), n * qb)
            pltpu.make_async_copy(
                w_refs[arr], w_bufs[arr].at[pl.ds(pl.multiple_of(at.tensor * bt, 16), bt)], load.at[arr]).wait()
            for o in range(1, slices):
                for q in range(2):
                    arrive(3, arr, theirs(o, at.y, 1, 1 - x if q else x), 2 * o - 2 + q)
            arrive(3, arr, theirs(0, 1 - at.y, 2, 0), 2 * n_far)
            for o in range(1, slices):
                for q in range(2):
                    arrive(3, arr, theirs(o, 1 - at.y, 1, 1 - x if q else x), 2 * n_far + 2 * o - 1 + q)

        def gather_sent():
            for arr in range(2):
                g = w_bufs[arr]
                for level, quarters in enumerate((n_far, n_far, 2 + 2 * n_far, 2 * n_far + 2 + 2 * n_far)):
                    wait(g.at[pl.ds(0, quarters * qb)], gather_send.at[level, arr])

        def vectors_start():
            pltpu.make_async_copy(rows_ref, vrows.at[pl.ds(pl.multiple_of(at.tensor * 8, 8), 8)], vec_recv.at[0]).start()
            pltpu.make_async_copy(rows_ref, drows.at[pl.ds(pl.multiple_of(at.dp * 8, 8), 8)], vec_recv.at[1]).start()
            for offset in range(1, n_tensor):
                pltpu.make_async_remote_copy(
                    rows_ref, vrows.at[pl.ds(pl.multiple_of(at.tensor * 8, 8), 8)],
                    vec_send.at[0], vec_recv.at[0], (at.dp, at.tensor ^ offset), MESH).start()
            for offset in range(1, n_dp):
                pltpu.make_async_remote_copy(
                    rows_ref, drows.at[pl.ds(pl.multiple_of(at.dp * 8, 8), 8)],
                    vec_send.at[1], vec_recv.at[1], (at.dp ^ offset, at.tensor), MESH).start()

        def vectors_arrived():
            wait(vrows.at[pl.ds(0, 8 * n_tensor)], vec_recv.at[0])
            wait(drows, vec_recv.at[1])
            wait(vrows.at[pl.ds(0, 8 * (n_tensor - 1))], vec_send.at[0])
            wait(drows.at[pl.ds(0, 8 * (n_dp - 1))], vec_send.at[1])
            turned = vrows[...].T
            for t in range(n_tensor):
                b_in_v[t * bt : (t + 1) * bt, :] = turned[0:bt, 8 * t : 8 * t + 1]
                vec[t * columns : (t + 1) * columns, :] = turned[0:columns, 8 * t + 1 : 8 * t + 6]

        place0 = lax.broadcasted_iota(jnp.int32, (tokens, half), 0)
        k1 = lax.broadcasted_iota(jnp.int32, (tokens, half), 1)
        place = lambda k, shift: k // 2 + k % 2 * half + shift * (half // 2)
        one_hot = lambda hit: jnp.where(hit, 1.0, 0.0).astype(BF)
        for shift in range(2):
            perm[:, shift * half : (shift + 1) * half] = one_hot(place0 == place(k1, shift))
            perm[:, (2 + shift) * half : (3 + shift) * half] = one_hot(
                (place0 == place(half - k1, shift)) & (k1 > 0))
        turn0 = lax.broadcasted_iota(jnp.int32, (half, half), 0)
        turn1 = lax.broadcasted_iota(jnp.int32, (half, half), 1)
        turn = one_hot(turn0 + turn1 == half)
        edge0 = lax.broadcasted_iota(jnp.int32, (2 * group, half), 0)
        edge1 = lax.broadcasted_iota(jnp.int32, (2 * group, half), 1)
        pick_u = one_hot((edge0 == 2 * at.g) & (edge1 == 0))
        pick_v = one_hot((edge0 == 2 * at.g + 1) & (edge1 == 0))
        e_send[...] = jnp.zeros_like(e_send)
        A, B = parts
        block = 256
        step = 32

        def over(rows, size, body, carry=None, unroll=2):
            def inner(i, c):
                r = pl.ds(pl.multiple_of(i * size, size), size)
                return body(r, c)
            return lax.fori_loop(0, rows // size, inner, carry, unroll=unroll)

        def fold(v):
            return jnp.sum(v.reshape(v.shape[0] // 8, 8, v.shape[1]), axis=0)

        def lane_fold(v):
            return sum(v[:, k * 128 : (k + 1) * 128] for k in range(v.shape[1] // 128))

        zeros8 = jnp.zeros((8, tokens), F32)

        def mean_of(total):
            return jnp.sum(total, axis=0, keepdims=True) / width

        def statistics(ref):
            total = over(width, step, lambda r, c: c + fold(ref[r, :]), zeros8)
            center = mean_of(total)
            def spread(r, c):
                off = ref[r, :] - center
                return c + fold(off * off)
            var = mean_of(over(width, step, spread, zeros8))
            return center, lax.rsqrt(var + EPSILON)

        bacc[...] = jnp.zeros_like(bacc)
        vacc[...] = jnp.zeros_like(vacc)

        def forward_mix(j):
            tokens_arrived(j)
            for b in range(n_tensor):
                r = pl.ds(b * columns, columns)
                e = eb[j, b * er : (b + 1) * er, 0:columns]
                all_four = dot(ub[j, r, :], perm[...], 1, 0)
                ub[j, r, :] = all_four[:, : 2 * half].astype(BF)
                tile[r, A] = (all_four[:, 2 * half : 3 * half] + dot(e, pick_u, 0, 0)).astype(BF)
                tile[r, B] = (all_four[:, 3 * half :] + dot(e, pick_v, 0, 0)).astype(BF)
            def mixed(r, c):
                f1[r, A] = xb[j, r, A].astype(F32) + mix_scale * (
                    dot(cos[r, :], ub[j, :, A], 1, 0) - dot(sin[r, :], ub[j, :, B], 1, 0))
                f1[r, B] = xb[j, r, B].astype(F32) + mix_scale * (
                    dot(cos[r, :], tile[:, A], 1, 0) + dot(sin[r, :], tile[:, B], 1, 0))
                return c
            over(width, block, mixed, 0, unroll=1)
            center, inverse = statistics(f1)
            def scale(r, c):
                h = (f1[r, :] - center) * inverse
                f1[r, :] = h
                n = h * vec[r, 1:2] + vec[r, 2:3]
                f2[r, :] = n
                nl[r, own(j)] = n.astype(BF)
                return c
            over(width, step, scale, 0)
            return inverse

        c0 = math.sqrt(2.0 / math.pi)
        c1 = c0 * 0.044715

        def forward_mlp(j):
            def inner(r, c):
                v = dot(win[r, :], nl[:, own(j)], 1, 0) + b_in_v[r, :]
                v2 = v * v
                p = 0.5 + 0.5 * jnp.tanh(v * (c0 + c1 * v2))
                a = v * p
                a_all[r, own(j)] = a.astype(BF)
                m_all[r, own(j)] = (p + a * (1.0 - p) * (2.0 * c0 + 6.0 * c1 * v2)).astype(BF)
                return c
            over(units, block, inner, 0, unroll=1)
            def outer(r, c):
                f2[r, :] = f2[r, :] + dot(wout[:, r], a_all[:, own(j)], 0, 0) + vec[r, 0:1]
                return c
            for k in range(width // block):
                outer(pl.ds(k * block, block), 0)

        def second_norm(j):
            center, inverse = statistics(f2)
            flag = drows[pl.ds(pl.multiple_of(at.dp_from(j) * 8, 8), 8), 0:128][6:7, j : j + 1]
            def result(r, c):
                h = (f2[r, :] - center) * inverse
                f2[r, :] = h
                ab[j, r, :] = (h * vec[r, 3:4] + vec[r, 4:5]).astype(BF)
                return c
            over(width, step, result, 0)
            act_start(j)
            wait(cb.at[pl.ds(j * width, width)], cot_recv.at[j])
            def sums(r, c):
                go = cb[pl.ds(pl.multiple_of(j * width + r.start, 16), r.size), :].astype(F32) * flag
                h = f2[r, :]
                goh = go * h
                vacc[3, r, :] += lane_fold(goh)
                vacc[4, r, :] += lane_fold(go)
                gh = go * vec[r, 3:4]
                return c[0] + fold(gh), c[1] + fold(gh * h)
            m1, m2 = over(width, step, sums, (zeros8, zeros8))
            m1, m2 = mean_of(m1), mean_of(m2)
            def back(r, c):
                gh = cb[pl.ds(pl.multiple_of(j * width + r.start, 16), r.size), :].astype(F32) * flag * vec[r, 3:4]
                gs = inverse * (gh - m1 - f2[r, :] * m2)
                vacc[0, r, :] += lane_fold(gs)
                f3[r, :] = gs
                gl[r, own(j)] = gs.astype(BF)
                return c
            over(width, step, back, 0)

        def backward_inner(j):
            def inner(r, c):
                gi = dot(wout[r, :], gl[:, own(j)], 1, 0) * m_all[r, own(j)].astype(F32)
                bacc[r, :] += lane_fold(gi)
                m_all[r, own(j)] = gi.astype(BF)
                return c
            over(units, block, inner, 0, unroll=1)

        def backward_outer(j):
            for k in range(width // block):
                r = pl.ds(k * block, block)
                f3[r, :] = f3[r, :] + dot(win[:, r], m_all[:, own(j)], 0, 0)

        def first_back(j, inverse):
            def sums(r, c):
                gn = f3[r, :]
                h = f1[r, :]
                gnh = gn * h
                vacc[1, r, :] += lane_fold(gnh)
                vacc[2, r, :] += lane_fold(gn)
                gh = gn * vec[r, 1:2]
                return c[0] + fold(gh), c[1] + fold(gh * h)
            m1, m2 = over(width, step, sums, (zeros8, zeros8))
            m1, m2 = mean_of(m1), mean_of(m2)
            def back(r, c):
                gf = inverse * (f3[r, :] * vec[r, 1:2] - m1 - f1[r, :] * m2)
                xb[j, r, :] = gf.astype(BF)
                tile[r, :] = (gf * mix_scale).astype(BF)
                return c
            over(width, step, back, 0)
            def fold_pairs(r, c):
                a = tile[r, A].astype(F32)
                b = tile[r, B]
                t = dot(b, turn, 1, 0)
                ub[j, r, A] = (t + a).astype(BF)
                ub[j, r, B] = (t - a).astype(BF)
                return c
            over(width, block, fold_pairs, 0, unroll=1)
            edge = dot(pick_u + pick_v, tile[:, B], 1, 1).astype(BF)
            is_cos = lax.broadcasted_iota(jnp.int32, (er, columns), 0) % 2 == 0
            for b in range(n_tensor):
                r = pl.ds(b * columns, columns)
                eb[j, b * er : (b + 1) * er, 0:columns] = jnp.where(
                    is_cos, dot(edge, cos[r, :], 1, 1), dot(edge, sin[r, :], 1, 1)).astype(BF)
            for k in range(width // block):
                r = pl.ds(k * block, block)
                tile[r, A] = dot(cos[r, :], ub[j, :, A], 1, 0).astype(BF)
                tile[r, B] = dot(sin[r, :], ub[j, :, B], 1, 0).astype(BF)
            for k in range(width // block):
                r = pl.ds(k * block, block)
                ub[j, r, :] = dot(tile[r, :], perm[:, : 2 * half], 1, 1).astype(BF)
            for move in col_moves(j):
                move.start()

        grads = (wout, win)
        if seqs * tokens >= 2 * width:
            land = lambda rows, arr: a_all.at[rows, pl.ds(arr * width, width)]
        else:
            land = lambda rows, arr: spare.at[rows, pl.ds(arr * width, width)]
        at2 = n_tensor * hb
        at3 = at2 + slices * hb
        at4 = at3 + slices * qb
        at5 = at4 + (slices - 1) * qb
        land1 = lambda arr, k: land(pl.ds(pl.multiple_of(k * hb, 16), hb), arr)
        land2 = lambda arr, k, n: land(pl.ds(at2 + k * n, n), arr)
        land3 = lambda arr, k: land(pl.ds(at3 + k * qb, qb), arr)
        land4 = lambda arr, k: land(pl.ds(at4 + k * qb, qb), arr)
        land5 = lambda arr: land(pl.ds(at5, qb), arr)
        def block_at(k):
            y = jnp.where(k < slices, 1 - at.y, at.y)
            return (k % slices) * 2 + y
        def rows_half(k, c):
            return pl.ds(pl.multiple_of(block_at(k) * bt + c * hb, 16), hb)
        def rows_quarter(k, xx):
            return pl.ds(pl.multiple_of(block_at(k) * bt + core * hb + xx * qb, 16), qb)

        def send(src, dst, level, arr, k, device):
            pltpu.make_async_remote_copy(
                src, dst, rs_send.at[level, arr], rs_recv.at[level, arr, k], device, MESH).start()

        def ready_signal():
            for i, device in enumerate([core_peer, x_peer, y_peer] + [z_peer(o) for o in range(1, slices)]
                                       + [flip(1 << b) for b in range(2, n_dp.bit_length() - 1)]):
                pl.semaphore_signal(ready.at[i], inc=1, device_id=device, device_id_type=MESH)

        def ready_wait(i):
            pl.semaphore_wait(ready.at[i], 1)

        def weight_grads(arr, left, right):
            def tile_step(k, c):
                r = pl.ds(pl.multiple_of(block_at(k) * bt, 16), bt)
                grads[arr][r, :] = dot(left[r, :], right[...], 1, 1).astype(BF)
                return c
            lax.fori_loop(0, n_tensor, tile_step, 0)

        def level1(arr):
            def go(k, c):
                send(grads[arr].at[rows_half(k, 1 - core)], land1(arr, k), 0, arr, k, core_peer)
                return c
            lax.fori_loop(0, n_tensor, go, 0)

        def add(arr, rows, landed, level, k):
            wait(landed, rs_recv.at[level, arr, k])
            ref = grads[arr].at[rows]
            n = ref.shape[0]
            def go(i, c):
                r = pl.ds(pl.multiple_of(i * 16, 16), 16)
                ref[r, :] = (ref[r, :].astype(F32) + landed[r, :].astype(F32)).astype(BF)
                return c
            lax.fori_loop(0, n // 16, go, 0, unroll=2)

        def after1(arr):
            def go(k, c):
                add(arr, rows_half(k, core), land1(arr, k), 0, k)

                @pl.when(k < slices)
                def _():
                    send(grads[arr].at[rows_half(k, core)], land2(arr, k, hb), 1, arr, k, y_peer)
                return c
            lax.fori_loop(0, n_tensor, go, 0)

        def after2(arr):
            def go(k, c):
                add(arr, rows_half(slices + k, core), land2(arr, k, hb), 1, k)
                send(grads[arr].at[rows_quarter(slices + k, 1 - x)], land3(arr, k), 2, arr, k, x_peer)
                return c
            lax.fori_loop(0, slices, go, 0)

        def after3(arr):
            for offset in range(slices):
                k = at.z ^ offset
                add(arr, rows_quarter(slices + k, x), land3(arr, k), 2, k)
                if offset:
                    send(grads[arr].at[rows_quarter(slices + k, x)], land4(arr, offset - 1), 3, arr, offset - 1, z_peer(offset))

        def after4(arr):
            mine = rows_quarter(slices + at.z, x)
            for offset in range(1, slices):
                add(arr, mine, land4(arr, offset - 1), 3, offset - 1)
            for b in range(2, n_dp.bit_length() - 1):
                k = b - 2
                peer_ = flip(1 << b)
                pltpu.make_async_remote_copy(
                    grads[arr].at[mine], land5(arr), more_send.at[arr, k], more_recv.at[arr, k], peer_, MESH).start()
                wait(grads[arr].at[mine], more_send.at[arr, k])
                wait(land5(arr), more_recv.at[arr, k])
                ref = grads[arr].at[mine]
                ref[...] = (ref[...].astype(F32) + land5(arr)[...].astype(F32)).astype(BF)
                if b + 1 < n_dp.bit_length() - 1:
                    pl.semaphore_signal(more_free, inc=1, device_id=peer_, device_id_type=MESH)
                    pl.semaphore_wait(more_free, 1)
            home = pl.ds(pl.multiple_of(core * hb + x * qb, 16), qb)
            out = (gout_o, gin_o)[arr]
            pltpu.make_async_copy(grads[arr].at[mine], out.at[home], rs_recv.at[4, arr, 0]).start()
            for q in range(1, 3):
                pltpu.make_async_remote_copy(
                    grads[arr].at[mine], out.at[home], rs_send.at[4, arr], rs_recv.at[4, arr, q], flip(q), MESH).start()

        def after5(arr):
            out = (gout_o, gin_o)[arr]
            came = out.at[pl.ds(pl.multiple_of(core * hb + (1 - x) * qb, 16), qb)]
            wait(came, rs_recv.at[4, arr, 2])
            pltpu.make_async_remote_copy(came, came, rs_send.at[4, arr], rs_recv.at[4, arr, 3], core_peer, MESH).start()

        def rs_finish(arr):
            g = grads[arr]
            n = n_tensor * hb
            wait(g.at[pl.ds(0, n)], rs_send.at[0, arr])
            wait(g.at[pl.ds(0, slices * hb)], rs_send.at[1, arr])
            wait(g.at[pl.ds(0, slices * qb)], rs_send.at[2, arr])
            wait(g.at[pl.ds(0, (slices - 1) * qb)], rs_send.at[3, arr])
            wait(g.at[pl.ds(0, 3 * qb)], rs_send.at[4, arr])
            for q in (0, 1, 3):
                wait((gout_o, gin_o)[arr].at[pl.ds(0, qb)], rs_recv.at[4, arr, q])

        def table_start(i):
            c, g = i // group, i % group
            return pltpu.make_async_copy(table_rows(c, g), slot_at(i), table_sem.at[i % n_slots])

        def back_prefetch():
            for i in range(n_slots):
                table_start(i).start()

        def words_back(js, acc):
            m = len(js) * columns
            base = js[0] * width
            n_edge = len(js) * er
            some = pl.ds(js[0] * columns, m)
            some_edges = pl.ds(js[0] * er, n_edge)
            for j in js:
                col_arrived(j)
                act_sent(j)
            for g in range(group):
                pltpu.make_async_copy(gu_o.at[g, some], cb.at[pl.ds(base + g * m, m)], table_sem.at[n_slots]).start()
                pltpu.make_async_copy(
                    ge_o.at[g, some_edges], tile.at[pl.ds(g * n_edge, n_edge), pl.ds(0, 128)],
                    table_sem.at[n_slots + 1]).start()
            for j in js:
                for k in range(n_pieces):
                    pltpu.make_async_copy(
                        gf_o.at[j, :, pl.ds(k * tokens, tokens)], ab.at[j, pl.ds(k * columns, columns)],
                        table_sem.at[n_slots + 2]).start()
            wait(cb.at[pl.ds(base, group * m)], table_sem.at[n_slots])
            wait(tile.at[pl.ds(0, group * n_edge), pl.ds(0, 128)], table_sem.at[n_slots + 1])
            for j in js:
                wait(ab.at[j], table_sem.at[n_slots + 2])
            edges = tile[0:n_edge, 0:128].astype(F32)
            for g in range(1, group):
                edges = edges + tile[g * n_edge : (g + 1) * n_edge, 0:128].astype(F32)
            edges = edges.astype(BF)
            for c in range(n_chunks):
                for g in range(group):
                    i = c * group + g
                    table_start(i).wait()
                    for s_ in range(per):
                        t = slot_at(i)[pl.ds(s_ * tokens, tokens), :]
                        left = cb[base + g * m : base + (g + 1) * m, :]
                        even = dot(left[:, :half], t[:, :half], 1, 1)
                        odd = dot(left[:, half:], t[:, half:], 1, 1)
                        at_even = pl.ds(s_ * m, m)
                        at_odd = pl.ds((per + s_) * m, m)
                        if g:
                            acc[at_even, :] += even
                            acc[at_odd, :] += odd
                        else:
                            acc[at_even, :] = even
                            acc[at_odd, :] = odd
                    if i + n_slots < n_chunks * group:
                        table_start(i + n_slots).start()
                for s_ in range(per):
                    for sign in range(2):
                        k = c * per + s_ + sign * (n_pieces // 2)
                        for n, j in enumerate(js):
                            rows = pl.ds(k * columns, columns)
                            even = acc[pl.ds(s_ * m + n * columns, columns), :]
                            odd = acc[pl.ds((per + s_) * m + n * columns, columns), :]
                            edge = dot(edges[n * er : (n + 1) * er, 0:columns], edge_v[:, k * tokens : (k + 1) * tokens], 0, 0)
                            both = even - odd if sign else even + odd
                            ab[j, rows, :] = (both + edge + ab[j, rows, :].astype(F32)).astype(BF)
                            home_start(j, k)

        def home_at(j):
            dp = at.dp_from(j)
            return dp, jnp.logical_and(dp == at.dp, at.block == at.tensor)

        def home_start(j, k):
            dp, here = home_at(j)
            src = ab.at[j, pl.ds(k * columns, columns)]
            dst = gw_o.at[j, :, pl.ds(k * tokens, tokens)]

            @pl.when(here)
            def _():
                pltpu.make_async_copy(src, dst, home_recv.at[j]).start()

            @pl.when(jnp.logical_not(here))
            def _():
                pltpu.make_async_remote_copy(src, dst, home_send.at[j], home_recv.at[j], (dp, at.block), MESH).start()

        def home_finish(j):
            dp, here = home_at(j)

            @pl.when(jnp.logical_not(here))
            def _():
                wait(gw_o.at[j], home_send.at[j])

            wait(gw_o.at[j], home_recv.at[j])

        def vector_grads():
            cols = pl.ds(0, 128)
            vrows[...] = jnp.zeros_like(vrows)
            turned = jnp.zeros((wide, 128), F32)
            scratch = f1.at[pl.ds(0, wide), cols]
            scratch[...] = turned
            for t in range(n_tensor):
                scratch[0:bt, 8 * t : 8 * t + 1] = jnp.sum(bacc[t * bt : (t + 1) * bt, :], axis=1, keepdims=True)
                for i in range(5):
                    scratch[0:columns, 8 * t + 1 + i : 8 * t + 2 + i] = jnp.sum(
                        vacc[i, t * columns : (t + 1) * columns, :], axis=1, keepdims=True)
            vrows[...] = scratch[...].T
            n = 8 * n_tensor
            for offset in range(1, n_dp):
                pltpu.make_async_remote_copy(
                    vrows.at[pl.ds(0, n)], grows.at[pl.ds((offset - 1) * n, n)],
                    vg_send.at[0], vg_recv.at[0], (at.dp ^ offset, at.tensor), MESH).start()

        def vector_grads_two():
            n = 8 * n_tensor
            wait(grows.at[pl.ds(0, (n_dp - 1) * n)], vg_recv.at[0])
            wait(grows.at[pl.ds(0, (n_dp - 1) * n)], vg_send.at[0])
            total = vrows[0:n, :]
            for offset in range(1, n_dp):
                total = total + grows[(offset - 1) * n : offset * n, :]
            vrows[0:n, :] = total
            for offset in range(1, n_tensor):
                t = at.tensor ^ offset
                pltpu.make_async_remote_copy(
                    vrows.at[pl.ds(pl.multiple_of(t * 8, 8), 8)], drows2.at[pl.ds((offset - 1) * 8, 8)],
                    vg_send.at[1], vg_recv.at[1], (at.dp, t), MESH).start()

        def vector_grads_three():
            n = 8 * (n_tensor - 1)
            wait(drows2.at[pl.ds(0, n)], vg_recv.at[1])
            wait(drows2.at[pl.ds(0, n)], vg_send.at[1])
            total = vrows[pl.ds(pl.multiple_of(at.tensor * 8, 8), 8), :]
            for offset in range(1, n_tensor):
                total = total + drows2[(offset - 1) * 8 : offset * 8, :]
            vec_o[...] = total

        tables = [
            pltpu.make_async_copy(src, dst, load.at[2 + i])
            for i, (src, dst) in enumerate(((edge_ref, edge_v), (cos_ref, cos), (sin_ref, sin)))
        ]
        gather_one()
        gather_start()
        vectors_start()
        for move in tables:
            move.start()
        front_prefetch()
        gather_two()
        slice_start(0)
        gather_three()
        tables[1].wait()
        tables[2].wait()
        vectors_arrived()
        tables[0].wait()
        wait(a_all.at[pl.ds(0, width), two], slice_recv.at[0])
        front_pass([0], 1)
        front_prefetch()
        slice_start(1)
        for arr in range(2):
            gather_four(arr)
        for j in range(2, seqs):
            slice_start(j)
        inverse = forward_mix(0)
        cot_start(0)
        for arr in range(2):
            gather_last(arr)
        last = seqs - 1
        for j in range(seqs):
            if j:
                inverse = forward_mix(j)
            if j == last:
                for i in range(seqs):
                    tokens_sent(i)
                back_prefetch()
            forward_mlp(j)
            if j == 0:
                wait(a_all.at[pl.ds(width, width), two], slice_recv.at[1])
                front_pass([1], 1)
                front_prefetch()
            if j + 1 < seqs:
                cot_start(j + 1)
            if j == last:
                words_back([0], f3)
                back_prefetch()
            second_norm(j)
            backward_inner(j)
            if j == last:
                gather_sent()
                weight_grads(0, a_all, gl)
                ready_signal()
                ready_wait(0)
                level1(0)
            backward_outer(j)
            first_back(j, inverse)
            if j + 2 < seqs:
                i = j + 2
                wait(a_all.at[pl.ds(i * width, width), two], slice_recv.at[i])
                front_pass([i], 1)
        ready_wait(2)
        after1(0)
        weight_grads(1, m_all, nl)
        level1(1)
        vector_grads()
        after1(1)
        for j in range(1, last):
            words_back([j], f2)
            back_prefetch()
        words_back([last], f2)
        ready_wait(1)
        after2(0)
        for i in range(3, 3 + slices - 1 + max(0, n_dp.bit_length() - 3)):
            ready_wait(i)
        after3(0)
        after2(1)
        after3(1)
        vector_grads_two()
        after4(0)
        after4(1)
        vector_grads_three()
        after5(0)
        after5(1)
        for j in range(seqs):
            slice_finish(j)
            cot_finish(j)
            col_finish(j)
            home_finish(j)
        rs_finish(0)
        rs_finish(1)


    shape = jax.ShapeDtypeStruct
    dma = pltpu.SemaphoreType.DMA
    whole_vmem = pl.BlockSpec(memory_space=pltpu.VMEM)
    depth = min(1024, length // 2)
    need_spare = seqs * tokens < 2 * width
    regular = pltpu.SemaphoreType.REGULAR
    activations, _, _, _, gw, g_in, g_out, vec_g = pl.pallas_call(
        layer_body,
        out_shape=[
            shape(words.shape, BF),
            shape((group, seqs * columns, tokens), BF),
            shape((group, seqs * 2 * group, 128), BF),
            shape((seqs, columns, length), BF),
            shape((seqs, columns, length), BF),
            shape(w_in.shape, BF),
            shape(w_in.shape, BF),
            shape((8, wide), F32),
        ],
        in_specs=[ANY] * 9,
        out_specs=[ANY] * 7 + [whole_vmem],
        scratch_shapes=[
            pltpu.VMEM((units, width), BF),
            pltpu.VMEM((units, width), BF),
            pltpu.VMEM((width, width), BF),
            pltpu.VMEM((width, width), BF),
            pltpu.VMEM((seqs, width, tokens), BF),
            pltpu.VMEM((seqs, width, tokens), BF),
            pltpu.VMEM((seqs, n_tensor * 2 * group, 128), BF),
            pltpu.VMEM((group * seqs * columns, tokens), BF),
            pltpu.VMEM((seqs, width, tokens), BF),
            pltpu.VMEM((units, seqs * tokens), BF),
            pltpu.VMEM((units, seqs * tokens), BF),
            pltpu.VMEM((width, seqs * tokens), BF),
            pltpu.VMEM((width, seqs * tokens), BF),
            pltpu.VMEM((3 * width, tokens), F32),
            pltpu.VMEM((width, tokens), BF),
            pltpu.VMEM((2 * group, length), BF),
            pltpu.VMEM((n_slots * depth, tokens), BF),
            pltpu.VMEM((tokens, 4 * half), BF),
            pltpu.VMEM((seqs * 2 * group, 128), BF),
            pltpu.VMEM((units, 128), F32),
            pltpu.VMEM((5, width, 128), F32),
            pltpu.VMEM((units, 1), F32),
            pltpu.VMEM((width, 5), F32),
            pltpu.VMEM((128, wide), F32),
            pltpu.VMEM((8 * n_dp, wide), F32),
            pltpu.VMEM((8 * n_tensor * (n_dp - 1), wide), F32),
            pltpu.VMEM((8 * (n_tensor - 1), wide), F32),
            pltpu.VMEM((units, 2 * width) if need_spare else (16, 128), BF),
            dma((5,)),
            dma((seqs,)),
            dma((seqs,)),
            dma((seqs, 3)),
            dma((seqs, 3)),
            dma((2,)),
            dma((2,)),
            dma((4, 2)),
            dma((4, 2, 2 * n_tensor)),
            dma((seqs,)),
            dma((seqs,)),
            dma((seqs,)),
            dma((seqs,)),
            dma((seqs,)),
            dma((seqs,)),
            dma((seqs, 3)),
            dma((seqs, 3)),
            regular((3 + n_tensor // 2 + n_dp,)),
            dma((5, 2)),
            dma((5, 2, n_tensor)),
            dma((n_slots + 3,)),
            dma((seqs,)),
            dma((seqs,)),
            dma((2, n_dp)),
            dma((2, n_dp)),
            regular,
            dma((2,)),
            dma((2,)),
        ],
        compiler_params=pltpu.CompilerParams(
            collective_id=1, has_side_effects=True, vmem_limit_bytes=64 * 1024 * 1024
        ),
    )(
        words, cotangent, w_in, w_out, jnp.asarray(hid_cos), jnp.asarray(hid_sin), table, edge_table, rows_in
    )
    grad_words = gw.astype(F32)

    grad_w_in = g_in.astype(F32)
    grad_w_out = g_out.astype(F32)
    return (
        activations,
        grad_words,
        grad_w_in,
        vec_g[0, : w_in.shape[0]],
        grad_w_out,
        vec_g[1, :columns],
        vec_g[2, :columns],
        vec_g[3, :columns],
        vec_g[4, :columns],
        vec_g[5, :columns],
    )


def solution(mesh):
    spec = (
        P("dp", "tensor", None),
        P("tensor", None),
        P("tensor"),
        P("tensor", None),
        P("tensor"),
        P("tensor"),
        P("tensor"),
        P("tensor"),
        P("tensor"),
        P("dp", "tensor", None),
        P("dp"),
    )
    out = (
        P("dp", "tensor", None),
        P("dp", "tensor", None),
        P("tensor", None),
        P("tensor"),
        P("tensor", None),
        P("tensor"),
        P("tensor"),
        P("tensor"),
        P("tensor"),
        P("tensor"),
    )
    return jax.shard_map(on_device, mesh=mesh, in_specs=spec, out_specs=out, check_vma=False)
```

```python
import math

import jax
import jax.numpy as jnp
import numpy as np
from jax import lax
from jax.experimental import pallas as pl
from jax.experimental.pallas import tpu as pltpu
from jax.sharding import PartitionSpec as P

EPSILON = 1e-12
MESH = pl.DeviceIdType.MESH
BF = jnp.bfloat16
F32 = jnp.float32


def token_tables(length, group):
    half = length // (2 * group)

    def wave(n, k):
        angle = (n[:, None] * k[None, :] % length) * (2.0 * math.pi / length)
        return np.cos(angle), np.sin(angle)

    n = np.arange(length, dtype=np.int64)
    k = np.arange(length // 2).reshape(group, half)
    columns = np.stack([k[:, 0::2], k[:, 1::2]], axis=1)
    cos, sin = wave(n[: length // 2], columns.reshape(-1))
    shape = (length // 2, group, 2, 1, half // 2)
    main = np.concatenate([cos.reshape(shape), sin.reshape(shape)], axis=3)
    main = main.reshape(length // 2, group, 2 * half).transpose(1, 0, 2).reshape(-1, 2 * half)
    edge_cos, edge_sin = wave(half * (np.arange(group) + 1), n)
    edge = np.stack([edge_cos, np.where(np.abs(edge_sin) < 1e-9, 0.0, edge_sin)], axis=1)
    return main.astype(BF), edge.reshape(2 * group, length).astype(BF)


def hidden_tables(width):
    ids = np.arange(width, dtype=np.int64)
    angle = (ids[:, None] * ids[None, :] % width) * (2.0 * math.pi / width)
    return np.cos(angle).astype(BF), np.sin(angle).astype(BF)


class Place:
    def __init__(self, n_dp, n_tensor):
        self.n_dp, self.n_tensor = n_dp, n_tensor
        self.slices = n_tensor // 2
        self.low = self.slices // 2
        self.dp = lax.axis_index("dp")
        self.tensor = lax.axis_index("tensor")
        self.x, self.core = self.dp // 2, self.dp % 2
        self.z, self.y = self.tensor // 2, self.tensor % 2
        self.z_high, self.z_low = self.z // self.low, self.z % self.low
        self.g = (self.z_low * 2 + self.core) * 2 + self.y
        self.block = self.block_of(self.g)

    def block_of(self, g):
        return (g // 2 % 2 * self.low + g // 4) * 2 + g % 2

    def member(self, g, z_high):
        return (self.x * 2 + g // 2 % 2, (z_high * self.low + g // 4) * 2 + g % 2)

    def high_of(self, j):
        return self.core ^ (j % 2)

    def dp_from(self, j):
        return self.x * 2 + (self.z_high ^ (j % 2))

    def peer(self, offset):
        g = self.g ^ offset
        return self.member(g, self.z_high), g


ANY = pl.BlockSpec(memory_space=pl.ANY)


def on_device(
    words, w_in, b_in, w_out, b_out, gain_one, shift_one, gain_two, shift_two, cotangent, valid
):
    seqs, columns, length = words.shape
    width = w_in.shape[1]
    n_dp, n_tensor = lax.axis_size("dp"), lax.axis_size("tensor")
    group = n_tensor
    half = length // (2 * group)
    mix_scale = 1.0 / math.sqrt(length * width)
    table, edge_table = token_tables(length, group)
    hid_cos, hid_sin = hidden_tables(width)

    table = jnp.asarray(table)
    edge_table = jnp.asarray(edge_table)
    units = w_in.shape[0] * n_tensor
    tokens = 2 * half

    def dot(a, b, da, db):
        return lax.dot_general(a, b, (((da,), (db,)), ((), ())), preferred_element_type=F32)

    wide = 512

    n_slots = 4

    def layer_body(
        x_ref, c_ref, win_ref, wout_ref, cos_ref, sin_ref, table_ref, edge_ref,
        b_in_ref, b_out_ref, gain_one_ref, shift_one_ref, gain_two_ref, shift_two_ref, valid_ref,
        act_o, gu_o, ge_o, gf_o, gw_o, gin_o, gout_o, vec_o,
        win, wout, cos, sin, xb, ub, eb, cb, ab, a_all, m_all, nl, gl, f, tile, edge_v, slots,
        perm, e_send, rows_ref, bacc, vacc, b_in_v, vec, vrows, drows, grows, drows2, spare,
        load, slice_send, slice_recv, tok_send, tok_recv, vec_send, vec_recv, gather_send, gather_recv,
        cot_send, cot_own, cot_recv, act_send, act_own, act_recv, col_send, col_recv,
        ready, rs_send, rs_recv, table_sem, home_send, home_recv, more_send, more_recv, more_free,
        vg_send, vg_recv,
    ):
        at = Place(n_dp, n_tensor)
        barrier = pltpu.get_barrier_semaphore()
        others = n_dp * n_tensor - 1
        def greet(i, c):
            k = (at.dp * n_tensor + at.tensor + i) % (others + 1)
            pl.semaphore_signal(
                barrier, inc=1, device_id=(k // n_tensor, k % n_tensor), device_id_type=MESH)
            return c
        lax.fori_loop(1, others + 1, greet, 0)
        pl.semaphore_wait(barrier, others)

        def wait(ref, sem):
            pltpu.make_async_copy(ref, ref, sem).wait()

        def lanes(g):
            return (
                pl.ds(pl.multiple_of(g * half, 128), half),
                pl.ds(pl.multiple_of(length - (g + 1) * half, 128), half),
            )

        parts = (pl.ds(0, half), pl.ds(half, half))
        own = lambda j: pl.ds(j * tokens, tokens)
        f1, f2, f3 = [f.at[pl.ds(k * width, width)] for k in range(3)]
        rows_of = lambda b: pl.ds(pl.multiple_of(b * columns, 16), columns)

        def cot_start(j):
            high = at.high_of(j)
            for offset in range(group):
                g = at.g ^ offset
                for p in range(2):
                    src = c_ref.at[j, :, lanes(g)[p]]
                    dst = cb.at[pl.ds(pl.multiple_of(j * width + at.tensor * columns, 16), columns), parts[p]]
                    device = at.member(g, high)
                    if offset:
                        pltpu.make_async_remote_copy(src, dst, cot_send.at[j], cot_recv.at[j], device, MESH).start()
                    else:
                        @pl.when(high == at.z_high)
                        def _():
                            pltpu.make_async_copy(src, dst, cot_recv.at[j]).start()

                        @pl.when(high != at.z_high)
                        def _():
                            pltpu.make_async_remote_copy(src, dst, cot_own.at[j], cot_recv.at[j], device, MESH).start()

        def cot_finish(j):
            high = at.high_of(j)
            wait(c_ref.at[j, :, pl.ds(0, length - 2 * half)], cot_send.at[j])

            @pl.when(high != at.z_high)
            def _():
                wait(c_ref.at[j, :, pl.ds(0, 2 * half)], cot_own.at[j])

        def act_start(j):
            dp = at.dp_from(j)
            for offset in range(n_tensor):
                b = at.tensor ^ offset
                for p in range(2):
                    src = ab.at[j, rows_of(b), parts[p]]
                    dst = act_o.at[j, :, lanes(at.g)[p]]
                    if offset:
                        pltpu.make_async_remote_copy(src, dst, act_send.at[j], act_recv.at[j], (dp, b), MESH).start()
                    else:
                        @pl.when(dp == at.dp)
                        def _():
                            pltpu.make_async_copy(src, dst, act_recv.at[j]).start()

                        @pl.when(dp != at.dp)
                        def _():
                            pltpu.make_async_remote_copy(src, dst, act_own.at[j], act_recv.at[j], (dp, b), MESH).start()

        def act_sent(j):
            dp = at.dp_from(j)
            wait(ab.at[j, pl.ds(0, width - columns)], act_send.at[j])

            @pl.when(dp != at.dp)
            def _():
                wait(ab.at[j, pl.ds(0, columns)], act_own.at[j])

            wait(act_o.at[j], act_recv.at[j])

        def col_moves(j):
            for offset in range(group):
                device, g_ = at.peer(offset)
                rows = rows_of(at.block_of(g_))
                for i, (src, dst) in enumerate((
                    (ub.at[j, rows], gu_o.at[at.g, pl.ds(j * columns, columns)]),
                    (eb.at[j, pl.ds(pl.multiple_of(at.block_of(g_) * er, 16), er)], ge_o.at[at.g, pl.ds(j * er, er)]),
                    (xb.at[j, rows, parts[0]], gf_o.at[j, :, lanes(at.g)[0]]),
                    (xb.at[j, rows, parts[1]], gf_o.at[j, :, lanes(at.g)[1]]),
                )):
                    kind = min(i, 2)
                    if offset:
                        yield pltpu.make_async_remote_copy(
                            src, dst, col_send.at[j, kind], col_recv.at[j, kind], device, MESH)
                    else:
                        yield pltpu.make_async_copy(src, dst, col_recv.at[j, kind])

        def col_finish(j):
            rest = pl.ds(0, width - columns)
            wait(ub.at[j, rest], col_send.at[j, 0])
            wait(eb.at[j, pl.ds(0, (n_tensor - 1) * er)], col_send.at[j, 1])
            wait(xb.at[j, rest], col_send.at[j, 2])

        def col_arrived(j):
            wait(gu_o.at[:, pl.ds(j * columns, columns)], col_recv.at[j, 0])
            wait(ge_o.at[:, pl.ds(j * er, er)], col_recv.at[j, 1])
            wait(gf_o.at[j], col_recv.at[j, 2])

        two = own(2)
        n_pieces = length // tokens

        def slice_at(j):
            high = at.high_of(j)
            dp = at.x * 2 + at.z_high
            return (dp, (high * at.low + at.z_low) * 2 + at.y), jnp.logical_and(dp == at.dp, high == at.z_high)

        def slice_start(j):
            device, here = slice_at(j)
            for k in range(n_pieces):
                src = x_ref.at[j, :, pl.ds(k * tokens, tokens)]
                dst = a_all.at[pl.ds(j * width + k * columns, columns), two]

                @pl.when(here)
                def _():
                    pltpu.make_async_copy(src, dst, slice_recv.at[j]).start()

                @pl.when(jnp.logical_not(here))
                def _():
                    pltpu.make_async_remote_copy(src, dst, slice_send.at[j], slice_recv.at[j], device, MESH).start()

        def slice_finish(j):
            _, here = slice_at(j)

            @pl.when(jnp.logical_not(here))
            def _():
                wait(x_ref.at[j], slice_send.at[j])

        n_chunks = length // 2 // depth
        per = depth // tokens
        er = 2 * group
        edge_rows = lambda b: pl.ds(pl.multiple_of(b * er, 16), er)
        def slot_at(i):
            return slots.at[pl.ds(i % n_slots * depth, depth)]

        def table_rows(c, g):
            return table_ref.at[pl.ds(pl.multiple_of(g * (length // 2) + c * depth, 16), depth)]

        order = [(offset, c) for offset in reversed(range(group)) for c in range(n_chunks)]
        def front_load(i):
            offset, c = order[i]
            return pltpu.make_async_copy(table_rows(c, at.g ^ offset), slot_at(i), table_sem.at[i % n_slots])

        def to_tokens(js, offset, kinds):
            device, g = at.peer(offset)
            rows = rows_of(at.block)
            for j in js:
                moves = []
                if "u" in kinds:
                    moves.append((m_all.at[pl.ds(j * width + offset * columns, columns), two], ub.at[j, rows], 0))
                if "e" in kinds:
                    moves.append((e_send.at[pl.ds(j * er, er)], eb.at[j, edge_rows(at.block)], 1))
                if "x" in kinds:
                    for p, i in ((0, g), (1, 2 * group - 1 - g)):
                        moves.append((
                            a_all.at[pl.ds(pl.multiple_of(j * width + i // 2 * columns, 16), columns),
                                     pl.ds(pl.multiple_of(2 * tokens + i % 2 * half, 128), half)],
                            xb.at[j, rows, parts[p]], 2))
                for src, dst, kind in moves:
                    if offset:
                        pltpu.make_async_remote_copy(
                            src, dst, tok_send.at[j, kind], tok_recv.at[j, kind], device, MESH).start()
                    else:
                        pltpu.make_async_copy(src, dst, tok_recv.at[j, kind]).start()

        def front_prefetch():
            for i in range(n_slots):
                front_load(i).start()

        def front_pass(js, first):
            m = len(js) * columns
            for offset in range(1, group):
                to_tokens(js[:first], offset, "x")
            for i, j in enumerate(js):
                edge = jnp.zeros((er, columns), F32)
                for k in range(n_pieces // 2):
                    k2 = k + n_pieces // 2
                    low = a_all[j * width + k * columns : j * width + (k + 1) * columns, 2 * tokens : 3 * tokens]
                    high = a_all[j * width + k2 * columns : j * width + (k2 + 1) * columns, 2 * tokens : 3 * tokens]
                    edge = edge + dot(edge_v[:, k * tokens : (k + 1) * tokens], low, 1, 1)
                    edge = edge + dot(edge_v[:, k2 * tokens : (k2 + 1) * tokens], high, 1, 1)
                    low, high = low.astype(F32), high.astype(F32)
                    rows = pl.ds(k * m + i * columns, columns)
                    nl[rows, two] = (low + high).astype(BF)
                    gl[rows, two] = (low - high).astype(BF)
                e_send[j * er : (j + 1) * er, 0:columns] = edge.astype(BF)
            for n, (offset, c) in enumerate(order):
                if c == 0:
                    even = jnp.zeros((m, half), F32)
                    odd = jnp.zeros((m, half), F32)
                front_load(n).wait()
                slot = slot_at(n)
                for s_ in range(per):
                    k = c * per + s_
                    rows = pl.ds(s_ * tokens, tokens)
                    even = even + dot(nl[k * m : (k + 1) * m, two], slot[rows, A], 1, 0)
                    odd = odd + dot(gl[k * m : (k + 1) * m, two], slot[rows, B], 1, 0)
                if n + n_slots < len(order):
                    front_load(n + n_slots).start()
                if c == n_chunks - 1:
                    for i, j in enumerate(js):
                        rows = pl.ds(j * width + offset * columns, columns)
                        mine = slice(i * columns, (i + 1) * columns)
                        m_all[rows, 2 * tokens : 2 * tokens + half] = even[mine].astype(BF)
                        m_all[rows, 2 * tokens + half : 3 * tokens] = odd[mine].astype(BF)
                    to_tokens(js[:first], offset, "ue" if offset else "uex")

        def later_tokens(j):
            for offset in reversed(range(group)):
                to_tokens([j], offset, "uex")

        def tokens_arrived(j):
            wait(ub.at[j], tok_recv.at[j, 0])
            wait(eb.at[j], tok_recv.at[j, 1])
            wait(xb.at[j], tok_recv.at[j, 2])

        def tokens_sent(j):
            rest = pl.ds(0, width - columns)
            wait(ub.at[j, rest], tok_send.at[j, 0])
            wait(eb.at[j, pl.ds(0, (n_tensor - 1) * er)], tok_send.at[j, 1])
            wait(xb.at[j, rest], tok_send.at[j, 2])

        bt = units // n_tensor
        hb, qb = bt // 2, bt // 4
        slices = at.slices
        core, x = at.dp % 2, at.dp // 2 % 2
        flip = lambda bit: (at.dp ^ bit, at.tensor)
        core_peer, x_peer, y_peer = flip(1), flip(2), (at.dp, at.tensor ^ 1)
        z_peer = lambda offset: (at.dp, (at.z ^ offset) * 2 + at.y)
        w_refs, w_bufs = (win_ref, wout_ref), (win, wout)

        far = [(o, p) for o in range(slices) for p in range(2) if o or p]

        def piece(z, p, cc, xx):
            start = (z * 2 + (at.y ^ p)) * bt + cc * hb + xx * qb
            return pl.ds(pl.multiple_of(start, 16), qb)

        def pass_on(level, arr, rows, key, device):
            ref = w_bufs[arr].at[rows]
            pltpu.make_async_remote_copy(
                ref, ref, gather_send.at[level, arr], gather_recv.at[level, arr, key], device, MESH).start()

        def arrive(level, arr, rows, key):
            wait(w_bufs[arr].at[rows], gather_recv.at[level, arr, key])

        ways = [(1, at.z < slices - 1), (-1, at.z > 0)]

        def neighbour(way):
            return (at.dp, (at.z + way) * 2 + at.y)

        def gather_start(arr):
            mine = pl.ds(pl.multiple_of(core * hb + x * qb, 16), qb)
            for way, there in ways:
                @pl.when(there)
                def _():
                    pltpu.make_async_remote_copy(
                        w_refs[arr].at[mine], w_bufs[arr].at[piece(at.z, 0, core, x)],
                        gather_send.at[0, arr], gather_recv.at[0, arr, at.z], neighbour(way), MESH).start()
            pltpu.make_async_remote_copy(
                w_refs[arr].at[mine], w_bufs[arr].at[piece(at.z, 0, core, x)],
                gather_send.at[1, arr], gather_recv.at[1, arr, at.z], y_peer, MESH).start()
            pltpu.make_async_copy(
                w_refs[arr], w_bufs[arr].at[pl.ds(pl.multiple_of(at.tensor * bt, 16), bt)], load.at[arr]).start()

        def gather_two(arr):
            for step in range(1, slices):
                for way, there in ways:
                    z = at.z - way * step

                    @pl.when((z >= 0) & (z < slices))
                    def _():
                        rows = piece(z, 0, core, x)
                        arrive(0, arr, rows, z)

                        @pl.when(there)
                        def _():
                            pass_on(0, arr, rows, z, neighbour(way))

                        pass_on(1, arr, rows, z, y_peer)
                        pass_on(2, arr, rows, 2 * z, x_peer)
                        pass_on(3, arr, rows, 4 * z, core_peer)

        def gather_three(arr):
            for o in range(slices):
                z = at.z ^ o
                rows = piece(z, 1, core, x)
                arrive(1, arr, rows, z)
                pass_on(2, arr, rows, 2 * z + 1, x_peer)
                pass_on(3, arr, rows, 4 * z + 2, core_peer)

        def gather_four(arr):
            for o, p in far:
                z = at.z ^ o
                rows = piece(z, p, core, 1 - x)
                arrive(2, arr, rows, 2 * z + p)
                pass_on(3, arr, rows, 2 * (2 * z + p) + 1, core_peer)

        def gather_last(arr):
            pltpu.make_async_copy(
                w_refs[arr], w_bufs[arr].at[pl.ds(pl.multiple_of(at.tensor * bt, 16), bt)], load.at[arr]).wait()
            for o, p in far:
                z = at.z ^ o
                for q in range(2):
                    arrive(3, arr, piece(z, p, 1 - core, 1 - x if q else x), 2 * (2 * z + p) + q)

        def gather_sent():
            for arr in range(2):
                g = w_bufs[arr]
                for step in range(slices):
                    for way, there in ways:
                        z = at.z - way * step

                        @pl.when((z >= 0) & (z < slices) & there)
                        def _():
                            wait(g.at[pl.ds(0, qb)], gather_send.at[0, arr])
                for level, quarters in ((1, slices), (2, len(far)), (3, 2 * len(far))):
                    wait(g.at[pl.ds(0, quarters * qb)], gather_send.at[level, arr])

        def vectors_start():
            rows_ref[...] = jnp.zeros_like(rows_ref)
            for i, ref in enumerate(
                (b_in_ref, b_out_ref, gain_one_ref, shift_one_ref, gain_two_ref, shift_two_ref, valid_ref)):
                rows_ref[i : i + 1, 0 : ref.shape[1]] = ref[...].astype(F32)
            pltpu.make_async_copy(rows_ref, vrows.at[pl.ds(pl.multiple_of(at.tensor * 8, 8), 8)], vec_recv.at[0]).start()
            pltpu.make_async_copy(rows_ref, drows.at[pl.ds(pl.multiple_of(at.dp * 8, 8), 8)], vec_recv.at[1]).start()
            for offset in range(1, n_tensor):
                pltpu.make_async_remote_copy(
                    rows_ref, vrows.at[pl.ds(pl.multiple_of(at.tensor * 8, 8), 8)],
                    vec_send.at[0], vec_recv.at[0], (at.dp, at.tensor ^ offset), MESH).start()
            for offset in range(1, n_dp):
                pltpu.make_async_remote_copy(
                    rows_ref, drows.at[pl.ds(pl.multiple_of(at.dp * 8, 8), 8)],
                    vec_send.at[1], vec_recv.at[1], (at.dp ^ offset, at.tensor), MESH).start()

        def vectors_arrived():
            wait(vrows.at[pl.ds(0, 8 * n_tensor)], vec_recv.at[0])
            wait(drows, vec_recv.at[1])
            wait(vrows.at[pl.ds(0, 8 * (n_tensor - 1))], vec_send.at[0])
            wait(drows.at[pl.ds(0, 8 * (n_dp - 1))], vec_send.at[1])
            turned = vrows[...].T
            for t in range(n_tensor):
                b_in_v[t * bt : (t + 1) * bt, :] = turned[0:bt, 8 * t : 8 * t + 1]
                vec[t * columns : (t + 1) * columns, :] = turned[0:columns, 8 * t + 1 : 8 * t + 6]

        gather_start(0)
        gather_start(1)
        slice_start(0)
        tables = [
            pltpu.make_async_copy(src, dst, load.at[2 + i])
            for i, (src, dst) in enumerate(((edge_ref, edge_v), (cos_ref, cos), (sin_ref, sin)))
        ]
        for move in tables:
            move.start()
        vectors_start()
        front_prefetch()

        place0 = lax.broadcasted_iota(jnp.int32, (tokens, half), 0)
        k1 = lax.broadcasted_iota(jnp.int32, (tokens, half), 1)
        place = lambda k, shift: k // 2 + k % 2 * half + shift * (half // 2)
        one_hot = lambda hit: jnp.where(hit, 1.0, 0.0).astype(BF)
        for shift in range(2):
            perm[:, shift * half : (shift + 1) * half] = one_hot(place0 == place(k1, shift))
            perm[:, (2 + shift) * half : (3 + shift) * half] = one_hot(
                (place0 == place(half - k1, shift)) & (k1 > 0))
        turn0 = lax.broadcasted_iota(jnp.int32, (half, half), 0)
        turn1 = lax.broadcasted_iota(jnp.int32, (half, half), 1)
        turn = one_hot(turn0 + turn1 == half)
        edge0 = lax.broadcasted_iota(jnp.int32, (2 * group, half), 0)
        edge1 = lax.broadcasted_iota(jnp.int32, (2 * group, half), 1)
        pick_u = one_hot((edge0 == 2 * at.g) & (edge1 == 0))
        pick_v = one_hot((edge0 == 2 * at.g + 1) & (edge1 == 0))
        e_send[...] = jnp.zeros_like(e_send)
        A, B = parts
        block = 256
        step = 32

        def over(rows, size, body, carry=None, unroll=2):
            def inner(i, c):
                r = pl.ds(pl.multiple_of(i * size, size), size)
                return body(r, c)
            return lax.fori_loop(0, rows // size, inner, carry, unroll=unroll)

        def fold(v):
            return jnp.sum(v.reshape(v.shape[0] // 8, 8, v.shape[1]), axis=0)

        def lane_fold(v):
            return sum(v[:, k * 128 : (k + 1) * 128] for k in range(v.shape[1] // 128))

        zeros8 = jnp.zeros((8, tokens), F32)

        def mean_of(total):
            return jnp.sum(total, axis=0, keepdims=True) / width

        def statistics(ref):
            total = over(width, step, lambda r, c: c + fold(ref[r, :]), zeros8)
            center = mean_of(total)
            def spread(r, c):
                off = ref[r, :] - center
                return c + fold(off * off)
            var = mean_of(over(width, step, spread, zeros8))
            return center, lax.rsqrt(var + EPSILON)

        bacc[...] = jnp.zeros_like(bacc)
        vacc[...] = jnp.zeros_like(vacc)

        def forward_mix(j):
            tokens_arrived(j)
            for b in range(n_tensor):
                r = pl.ds(b * columns, columns)
                e = eb[j, b * er : (b + 1) * er, 0:columns]
                all_four = dot(ub[j, r, :], perm[...], 1, 0)
                ub[j, r, :] = all_four[:, : 2 * half].astype(BF)
                tile[r, A] = (all_four[:, 2 * half : 3 * half] + dot(e, pick_u, 0, 0)).astype(BF)
                tile[r, B] = (all_four[:, 3 * half :] + dot(e, pick_v, 0, 0)).astype(BF)
            def mixed(r, c):
                f1[r, A] = xb[j, r, A].astype(F32) + mix_scale * (
                    dot(cos[r, :], ub[j, :, A], 1, 0) - dot(sin[r, :], ub[j, :, B], 1, 0))
                f1[r, B] = xb[j, r, B].astype(F32) + mix_scale * (
                    dot(cos[r, :], tile[:, A], 1, 0) + dot(sin[r, :], tile[:, B], 1, 0))
                return c
            over(width, block, mixed, 0, unroll=1)
            center, inverse = statistics(f1)
            def scale(r, c):
                h = (f1[r, :] - center) * inverse
                f1[r, :] = h
                n = h * vec[r, 1:2] + vec[r, 2:3]
                f2[r, :] = n
                nl[r, own(j)] = n.astype(BF)
                return c
            over(width, step, scale, 0)
            return inverse

        c0 = math.sqrt(2.0 / math.pi)
        c1 = c0 * 0.044715

        def forward_mlp(j):
            def inner(r, c):
                v = dot(win[r, :], nl[:, own(j)], 1, 0) + b_in_v[r, :]
                v2 = v * v
                p = 0.5 + 0.5 * jnp.tanh(v * (c0 + c1 * v2))
                a = v * p
                a_all[r, own(j)] = a.astype(BF)
                m_all[r, own(j)] = (p + a * (1.0 - p) * (2.0 * c0 + 6.0 * c1 * v2)).astype(BF)
                return c
            over(units, block, inner, 0, unroll=1)
            def outer(r, c):
                f2[r, :] = f2[r, :] + dot(wout[:, r], a_all[:, own(j)], 0, 0) + vec[r, 0:1]
                return c
            for k in range(width // block):
                outer(pl.ds(k * block, block), 0)

        def second_norm(j):
            center, inverse = statistics(f2)
            flag = drows[pl.ds(pl.multiple_of(at.dp_from(j) * 8, 8), 8), 0:128][6:7, j : j + 1]
            def result(r, c):
                h = (f2[r, :] - center) * inverse
                f2[r, :] = h
                ab[j, r, :] = (h * vec[r, 3:4] + vec[r, 4:5]).astype(BF)
                return c
            over(width, step, result, 0)
            act_start(j)
            wait(cb.at[pl.ds(j * width, width)], cot_recv.at[j])
            def sums(r, c):
                go = cb[pl.ds(pl.multiple_of(j * width + r.start, 16), r.size), :].astype(F32) * flag
                h = f2[r, :]
                goh = go * h
                vacc[3, r, :] += lane_fold(goh)
                vacc[4, r, :] += lane_fold(go)
                gh = go * vec[r, 3:4]
                return c[0] + fold(gh), c[1] + fold(gh * h)
            m1, m2 = over(width, step, sums, (zeros8, zeros8))
            m1, m2 = mean_of(m1), mean_of(m2)
            def back(r, c):
                gh = cb[pl.ds(pl.multiple_of(j * width + r.start, 16), r.size), :].astype(F32) * flag * vec[r, 3:4]
                gs = inverse * (gh - m1 - f2[r, :] * m2)
                vacc[0, r, :] += lane_fold(gs)
                f3[r, :] = gs
                gl[r, own(j)] = gs.astype(BF)
                return c
            over(width, step, back, 0)

        def backward_inner(j):
            def inner(r, c):
                gi = dot(wout[r, :], gl[:, own(j)], 1, 0) * m_all[r, own(j)].astype(F32)
                bacc[r, :] += lane_fold(gi)
                m_all[r, own(j)] = gi.astype(BF)
                return c
            over(units, block, inner, 0, unroll=1)

        def backward_outer(j):
            for k in range(width // block):
                r = pl.ds(k * block, block)
                f3[r, :] = f3[r, :] + dot(win[:, r], m_all[:, own(j)], 0, 0)

        def first_back(j, inverse):
            def sums(r, c):
                gn = f3[r, :]
                h = f1[r, :]
                gnh = gn * h
                vacc[1, r, :] += lane_fold(gnh)
                vacc[2, r, :] += lane_fold(gn)
                gh = gn * vec[r, 1:2]
                return c[0] + fold(gh), c[1] + fold(gh * h)
            m1, m2 = over(width, step, sums, (zeros8, zeros8))
            m1, m2 = mean_of(m1), mean_of(m2)
            def back(r, c):
                gf = inverse * (f3[r, :] * vec[r, 1:2] - m1 - f1[r, :] * m2)
                xb[j, r, :] = gf.astype(BF)
                tile[r, :] = (gf * mix_scale).astype(BF)
                return c
            over(width, step, back, 0)
            def fold_pairs(r, c):
                a = tile[r, A].astype(F32)
                b = tile[r, B]
                t = dot(b, turn, 1, 0)
                ub[j, r, A] = (t + a).astype(BF)
                ub[j, r, B] = (t - a).astype(BF)
                return c
            over(width, block, fold_pairs, 0, unroll=1)
            edge = dot(pick_u + pick_v, tile[:, B], 1, 1).astype(BF)
            is_cos = lax.broadcasted_iota(jnp.int32, (er, columns), 0) % 2 == 0
            for b in range(n_tensor):
                r = pl.ds(b * columns, columns)
                eb[j, b * er : (b + 1) * er, 0:columns] = jnp.where(
                    is_cos, dot(edge, cos[r, :], 1, 1), dot(edge, sin[r, :], 1, 1)).astype(BF)
            for k in range(width // block):
                r = pl.ds(k * block, block)
                tile[r, A] = dot(cos[r, :], ub[j, :, A], 1, 0).astype(BF)
                tile[r, B] = dot(sin[r, :], ub[j, :, B], 1, 0).astype(BF)
            for k in range(width // block):
                r = pl.ds(k * block, block)
                ub[j, r, :] = dot(tile[r, :], perm[:, : 2 * half], 1, 1).astype(BF)
            for move in col_moves(j):
                move.start()

        grads = (wout, win)
        if seqs * tokens >= 2 * width:
            land = lambda rows, arr: a_all.at[rows, pl.ds(arr * width, width)]
        else:
            land = lambda rows, arr: spare.at[rows, pl.ds(arr * width, width)]
        at2 = n_tensor * hb
        at3 = at2 + slices * hb
        at4 = at3 + slices * qb
        at5 = at4 + (slices - 1) * qb
        land1 = lambda arr, k: land(pl.ds(pl.multiple_of(k * hb, 16), hb), arr)
        land3 = lambda arr, k: land(pl.ds(at3 + k * qb, qb), arr)
        land4 = lambda arr, k: land(pl.ds(at4 + k * qb, qb), arr)
        land5 = lambda arr: land(pl.ds(at5, qb), arr)
        def block_at(k):
            y = jnp.where(k < slices, 1 - at.y, at.y)
            return (k % slices) * 2 + y
        def rows_half(k, c):
            return pl.ds(pl.multiple_of(block_at(k) * bt + c * hb, 16), hb)
        def rows_quarter(k, xx):
            return pl.ds(pl.multiple_of(block_at(k) * bt + core * hb + xx * qb, 16), qb)

        def send(src, dst, level, arr, k, device):
            pltpu.make_async_remote_copy(
                src, dst, rs_send.at[level, arr], rs_recv.at[level, arr, k], device, MESH).start()

        def ready_signal():
            for i, device in enumerate([core_peer, x_peer, y_peer] + [z_peer(o) for o in range(1, slices)]
                                       + [flip(1 << b) for b in range(2, n_dp.bit_length() - 1)]):
                pl.semaphore_signal(ready.at[i], inc=1, device_id=device, device_id_type=MESH)

        def ready_wait(i):
            pl.semaphore_wait(ready.at[i], 1)

        def weight_grads(arr, left, right):
            def tile_step(k, c):
                r = pl.ds(pl.multiple_of(block_at(k) * bt, 16), bt)
                grads[arr][r, :] = dot(left[r, :], right[...], 1, 1).astype(BF)
                return c
            lax.fori_loop(0, n_tensor, tile_step, 0)

        def level1(arr):
            def go(k, c):
                send(grads[arr].at[rows_half(k, 1 - core)], land1(arr, k), 0, arr, k, core_peer)
                return c
            lax.fori_loop(0, n_tensor, go, 0)

        def add(arr, rows, landed, level, k):
            wait(landed, rs_recv.at[level, arr, k])
            ref = grads[arr].at[rows]
            n = ref.shape[0]
            def go(i, c):
                r = pl.ds(pl.multiple_of(i * 16, 16), 16)
                ref[r, :] = (ref[r, :].astype(F32) + landed[r, :].astype(F32)).astype(BF)
                return c
            lax.fori_loop(0, n // 16, go, 0, unroll=2)

        def y_first(arr, z):
            return arr == 1 and z >= slices // 2

        def land2_x(arr, z, own_y):
            return land(pl.ds(at2 + z * hb + (qb if own_y else 0), qb), arr)

        def land2_y(arr, z):
            return land(pl.ds(at2 + z * hb, hb), arr)

        def after1(arr):
            for k in range(n_tensor):
                z, own_y = k % slices, k >= slices
                add(arr, rows_half(k, core), land1(arr, k), 0, k)
                if not y_first(arr, z):
                    send(grads[arr].at[rows_quarter(k, 1 - x)], land2_x(arr, z, own_y), 1, arr, k, x_peer)
                elif not own_y:
                    send(grads[arr].at[rows_half(k, core)], land2_y(arr, z), 1, arr, k, y_peer)

        def after2(arr):
            for z in range(slices):
                if y_first(arr, z):
                    add(arr, rows_half(slices + z, core), land2_y(arr, z), 1, z)
                    send(grads[arr].at[rows_quarter(slices + z, 1 - x)], land3(arr, z), 2, arr, z, x_peer)
                else:
                    add(arr, rows_quarter(z, x), land2_x(arr, z, False), 1, z)
                    send(grads[arr].at[rows_quarter(z, x)], land3(arr, z), 2, arr, z, y_peer)
            for z in range(slices):
                if not y_first(arr, z):
                    add(arr, rows_quarter(slices + z, x), land2_x(arr, z, True), 1, slices + z)

        def after3(arr):
            for offset in range(slices):
                k = at.z ^ offset
                add(arr, rows_quarter(slices + k, x), land3(arr, k), 2, k)
                if offset:
                    send(grads[arr].at[rows_quarter(slices + k, x)], land4(arr, offset - 1), 3, arr, offset - 1, z_peer(offset))

        def after4(arr):
            mine = rows_quarter(slices + at.z, x)
            for offset in range(1, slices):
                add(arr, mine, land4(arr, offset - 1), 3, offset - 1)
            for b in range(2, n_dp.bit_length() - 1):
                k = b - 2
                peer_ = flip(1 << b)
                pltpu.make_async_remote_copy(
                    grads[arr].at[mine], land5(arr), more_send.at[arr, k], more_recv.at[arr, k], peer_, MESH).start()
                wait(grads[arr].at[mine], more_send.at[arr, k])
                wait(land5(arr), more_recv.at[arr, k])
                ref = grads[arr].at[mine]
                ref[...] = (ref[...].astype(F32) + land5(arr)[...].astype(F32)).astype(BF)
                if b + 1 < n_dp.bit_length() - 1:
                    pl.semaphore_signal(more_free, inc=1, device_id=peer_, device_id_type=MESH)
                    pl.semaphore_wait(more_free, 1)
            home = pl.ds(pl.multiple_of(core * hb + x * qb, 16), qb)
            out = (gout_o, gin_o)[arr]
            pltpu.make_async_copy(grads[arr].at[mine], out.at[home], rs_recv.at[4, arr, 0]).start()
            for q in range(1, 3):
                pltpu.make_async_remote_copy(
                    grads[arr].at[mine], out.at[home], rs_send.at[4, arr], rs_recv.at[4, arr, q], flip(q), MESH).start()

        def after5(arr):
            out = (gout_o, gin_o)[arr]
            came = out.at[pl.ds(pl.multiple_of(core * hb + (1 - x) * qb, 16), qb)]
            wait(came, rs_recv.at[4, arr, 2])
            pltpu.make_async_remote_copy(came, came, rs_send.at[4, arr], rs_recv.at[4, arr, 3], core_peer, MESH).start()

        def rs_finish(arr):
            g = grads[arr]
            n = n_tensor * hb
            wait(g.at[pl.ds(0, n)], rs_send.at[0, arr])
            wait(g.at[pl.ds(0, slices * hb)], rs_send.at[1, arr])
            wait(g.at[pl.ds(0, slices * qb)], rs_send.at[2, arr])
            wait(g.at[pl.ds(0, (slices - 1) * qb)], rs_send.at[3, arr])
            wait(g.at[pl.ds(0, 3 * qb)], rs_send.at[4, arr])
            for q in (0, 1, 3):
                wait((gout_o, gin_o)[arr].at[pl.ds(0, qb)], rs_recv.at[4, arr, q])

        def table_start(i):
            c, g = i // group, i % group
            return pltpu.make_async_copy(table_rows(c, g), slot_at(i), table_sem.at[i % n_slots])

        def back_prefetch():
            for i in range(n_slots):
                table_start(i).start()

        def words_back(js, acc):
            m = len(js) * columns
            base = js[0] * width
            n_edge = len(js) * er
            some = pl.ds(js[0] * columns, m)
            some_edges = pl.ds(js[0] * er, n_edge)
            for j in js:
                col_arrived(j)
                act_sent(j)
            for g in range(group):
                pltpu.make_async_copy(gu_o.at[g, some], cb.at[pl.ds(base + g * m, m)], table_sem.at[n_slots]).start()
                pltpu.make_async_copy(
                    ge_o.at[g, some_edges], tile.at[pl.ds(g * n_edge, n_edge), pl.ds(0, 128)],
                    table_sem.at[n_slots + 1]).start()
            for j in js:
                for k in range(n_pieces):
                    pltpu.make_async_copy(
                        gf_o.at[j, :, pl.ds(k * tokens, tokens)], ab.at[j, pl.ds(k * columns, columns)],
                        table_sem.at[n_slots + 2]).start()
            wait(cb.at[pl.ds(base, group * m)], table_sem.at[n_slots])
            wait(tile.at[pl.ds(0, group * n_edge), pl.ds(0, 128)], table_sem.at[n_slots + 1])
            for j in js:
                wait(ab.at[j], table_sem.at[n_slots + 2])
            edges = tile[0:n_edge, 0:128].astype(F32)
            for g in range(1, group):
                edges = edges + tile[g * n_edge : (g + 1) * n_edge, 0:128].astype(F32)
            edges = edges.astype(BF)
            for c in range(n_chunks):
                for g in range(group):
                    i = c * group + g
                    table_start(i).wait()
                    for s_ in range(per):
                        t = slot_at(i)[pl.ds(s_ * tokens, tokens), :]
                        left = cb[base + g * m : base + (g + 1) * m, :]
                        even = dot(left[:, :half], t[:, :half], 1, 1)
                        odd = dot(left[:, half:], t[:, half:], 1, 1)
                        at_even = pl.ds(s_ * m, m)
                        at_odd = pl.ds((per + s_) * m, m)
                        if g:
                            acc[at_even, :] += even
                            acc[at_odd, :] += odd
                        else:
                            acc[at_even, :] = even
                            acc[at_odd, :] = odd
                    if i + n_slots < n_chunks * group:
                        table_start(i + n_slots).start()
                for s_ in range(per):
                    for sign in range(2):
                        k = c * per + s_ + sign * (n_pieces // 2)
                        for n, j in enumerate(js):
                            rows = pl.ds(k * columns, columns)
                            even = acc[pl.ds(s_ * m + n * columns, columns), :]
                            odd = acc[pl.ds((per + s_) * m + n * columns, columns), :]
                            edge = dot(edges[n * er : (n + 1) * er, 0:columns], edge_v[:, k * tokens : (k + 1) * tokens], 0, 0)
                            both = even - odd if sign else even + odd
                            ab[j, rows, :] = (both + edge + ab[j, rows, :].astype(F32)).astype(BF)
                            home_start(j, k)

        def home_at(j):
            dp = at.dp_from(j)
            return dp, jnp.logical_and(dp == at.dp, at.block == at.tensor)

        def home_start(j, k):
            dp, here = home_at(j)
            src = ab.at[j, pl.ds(k * columns, columns)]
            dst = gw_o.at[j, :, pl.ds(k * tokens, tokens)]

            @pl.when(here)
            def _():
                pltpu.make_async_copy(src, dst, home_recv.at[j]).start()

            @pl.when(jnp.logical_not(here))
            def _():
                pltpu.make_async_remote_copy(src, dst, home_send.at[j], home_recv.at[j], (dp, at.block), MESH).start()

        def home_finish(j):
            dp, here = home_at(j)

            @pl.when(jnp.logical_not(here))
            def _():
                wait(gw_o.at[j], home_send.at[j])

            wait(gw_o.at[j], home_recv.at[j])

        def vector_grads():
            cols = pl.ds(0, 128)
            vrows[...] = jnp.zeros_like(vrows)
            turned = jnp.zeros((wide, 128), F32)
            scratch = f1.at[pl.ds(0, wide), cols]
            scratch[...] = turned
            for t in range(n_tensor):
                scratch[0:bt, 8 * t : 8 * t + 1] = jnp.sum(bacc[t * bt : (t + 1) * bt, :], axis=1, keepdims=True)
                for i in range(5):
                    scratch[0:columns, 8 * t + 1 + i : 8 * t + 2 + i] = jnp.sum(
                        vacc[i, t * columns : (t + 1) * columns, :], axis=1, keepdims=True)
            vrows[...] = scratch[...].T
            n = 8 * n_tensor
            for offset in range(1, n_dp):
                pltpu.make_async_remote_copy(
                    vrows.at[pl.ds(0, n)], grows.at[pl.ds((offset - 1) * n, n)],
                    vg_send.at[0], vg_recv.at[0], (at.dp ^ offset, at.tensor), MESH).start()

        def vector_grads_two():
            n = 8 * n_tensor
            wait(grows.at[pl.ds(0, (n_dp - 1) * n)], vg_recv.at[0])
            wait(grows.at[pl.ds(0, (n_dp - 1) * n)], vg_send.at[0])
            total = vrows[0:n, :]
            for offset in range(1, n_dp):
                total = total + grows[(offset - 1) * n : offset * n, :]
            vrows[0:n, :] = total
            for offset in range(1, n_tensor):
                t = at.tensor ^ offset
                pltpu.make_async_remote_copy(
                    vrows.at[pl.ds(pl.multiple_of(t * 8, 8), 8)], drows2.at[pl.ds((offset - 1) * 8, 8)],
                    vg_send.at[1], vg_recv.at[1], (at.dp, t), MESH).start()

        def vector_grads_three():
            n = 8 * (n_tensor - 1)
            wait(drows2.at[pl.ds(0, n)], vg_recv.at[1])
            wait(drows2.at[pl.ds(0, n)], vg_send.at[1])
            total = vrows[pl.ds(pl.multiple_of(at.tensor * 8, 8), 8), :]
            for offset in range(1, n_tensor):
                total = total + drows2[(offset - 1) * 8 : offset * 8, :]
            vec_o[...] = total

        gather_two(0)
        slice_start(1)
        gather_two(1)
        gather_three(0)
        gather_three(1)
        for move in tables:
            move.wait()
        vectors_arrived()
        wait(a_all.at[pl.ds(0, width), two], slice_recv.at[0])
        for j in range(2, seqs):
            slice_start(j)
        cot_start(0)
        front_pass([0], 1)
        front_prefetch()
        gather_four(0)
        for i in range(1, seqs):
            wait(a_all.at[pl.ds(i * width, width), two], slice_recv.at[i])
        front_pass(list(range(1, seqs)), 1)
        back_prefetch()
        gather_four(1)
        inverse = forward_mix(0)
        for arr in range(2):
            gather_last(arr)
        cot_start(1)
        last = seqs - 1
        for j in range(seqs):
            if j:
                inverse = forward_mix(j)
            if j == last:
                for i in range(seqs):
                    tokens_sent(i)
            forward_mlp(j)
            if 0 < j and j + 1 < seqs:
                cot_start(j + 1)
            if j == last:
                words_back([0], f3)
                back_prefetch()
            second_norm(j)
            backward_inner(j)
            if j + 2 < seqs:
                later_tokens(j + 2)
            if j == last:
                gather_sent()
                weight_grads(0, a_all, gl)
                ready_signal()
                ready_wait(0)
                level1(0)
            backward_outer(j)
            first_back(j, inverse)
        ready_wait(1)
        after1(0)
        weight_grads(1, m_all, nl)
        level1(1)
        vector_grads()
        ready_wait(2)
        after1(1)
        for j in range(1, last):
            words_back([j], f2)
            back_prefetch()
        words_back([last], f2)
        after2(0)
        for i in range(3, 3 + slices - 1 + max(0, n_dp.bit_length() - 3)):
            ready_wait(i)
        after3(0)
        after2(1)
        after3(1)
        vector_grads_two()
        after4(0)
        after4(1)
        vector_grads_three()
        after5(0)
        after5(1)
        for j in range(seqs):
            slice_finish(j)
            cot_finish(j)
            col_finish(j)
            home_finish(j)
        rs_finish(0)
        rs_finish(1)


    shape = jax.ShapeDtypeStruct
    dma = pltpu.SemaphoreType.DMA
    whole_vmem = pl.BlockSpec(memory_space=pltpu.VMEM)
    depth = min(1024, length // 2)
    need_spare = seqs * tokens < 2 * width
    regular = pltpu.SemaphoreType.REGULAR
    activations, _, _, _, gw, g_in, g_out, vec_g = pl.pallas_call(
        layer_body,
        out_shape=[
            shape(words.shape, BF),
            shape((group, seqs * columns, tokens), BF),
            shape((group, seqs * 2 * group, 128), BF),
            shape((seqs, columns, length), BF),
            shape((seqs, columns, length), BF),
            shape(w_in.shape, BF),
            shape(w_in.shape, BF),
            shape((8, wide), F32),
        ],
        in_specs=[ANY] * 8 + [whole_vmem] * 7,
        out_specs=[ANY] * 7 + [whole_vmem],
        scratch_shapes=[
            pltpu.VMEM((units, width), BF),
            pltpu.VMEM((units, width), BF),
            pltpu.VMEM((width, width), BF),
            pltpu.VMEM((width, width), BF),
            pltpu.VMEM((seqs, width, tokens), BF),
            pltpu.VMEM((seqs, width, tokens), BF),
            pltpu.VMEM((seqs, n_tensor * 2 * group, 128), BF),
            pltpu.VMEM((group * seqs * columns, tokens), BF),
            pltpu.VMEM((seqs, width, tokens), BF),
            pltpu.VMEM((units, seqs * tokens), BF),
            pltpu.VMEM((units, seqs * tokens), BF),
            pltpu.VMEM((width, seqs * tokens), BF),
            pltpu.VMEM((width, seqs * tokens), BF),
            pltpu.VMEM((3 * width, tokens), F32),
            pltpu.VMEM((width, tokens), BF),
            pltpu.VMEM((2 * group, length), BF),
            pltpu.VMEM((n_slots * depth, tokens), BF),
            pltpu.VMEM((tokens, 4 * half), BF),
            pltpu.VMEM((seqs * 2 * group, 128), BF),
            pltpu.VMEM((8, wide), F32),
            pltpu.VMEM((units, 128), F32),
            pltpu.VMEM((5, width, 128), F32),
            pltpu.VMEM((units, 1), F32),
            pltpu.VMEM((width, 5), F32),
            pltpu.VMEM((128, wide), F32),
            pltpu.VMEM((8 * n_dp, wide), F32),
            pltpu.VMEM((8 * n_tensor * (n_dp - 1), wide), F32),
            pltpu.VMEM((8 * (n_tensor - 1), wide), F32),
            pltpu.VMEM((units, 2 * width) if need_spare else (16, 128), BF),
            dma((5,)),
            dma((seqs,)),
            dma((seqs,)),
            dma((seqs, 3)),
            dma((seqs, 3)),
            dma((2,)),
            dma((2,)),
            dma((4, 2)),
            dma((4, 2, 2 * n_tensor)),
            dma((seqs,)),
            dma((seqs,)),
            dma((seqs,)),
            dma((seqs,)),
            dma((seqs,)),
            dma((seqs,)),
            dma((seqs, 3)),
            dma((seqs, 3)),
            regular((3 + n_tensor // 2 + n_dp,)),
            dma((5, 2)),
            dma((5, 2, n_tensor)),
            dma((n_slots + 3,)),
            dma((seqs,)),
            dma((seqs,)),
            dma((2, n_dp)),
            dma((2, n_dp)),
            regular,
            dma((2,)),
            dma((2,)),
        ],
        compiler_params=pltpu.CompilerParams(
            collective_id=1, has_side_effects=True, vmem_limit_bytes=64 * 1024 * 1024
        ),
    )(
        words, cotangent, w_in, w_out, jnp.asarray(hid_cos), jnp.asarray(hid_sin), table, edge_table,
        *[v[None] for v in (b_in, b_out, gain_one, shift_one, gain_two, shift_two, valid)],
    )
    grad_words = gw.astype(F32)

    grad_w_in = g_in.astype(F32)
    grad_w_out = g_out.astype(F32)
    return (
        activations,
        grad_words,
        grad_w_in,
        vec_g[0, : w_in.shape[0]],
        grad_w_out,
        vec_g[1, :columns],
        vec_g[2, :columns],
        vec_g[3, :columns],
        vec_g[4, :columns],
        vec_g[5, :columns],
    )


def solution(mesh):
    spec = (
        P("dp", "tensor", None),
        P("tensor", None),
        P("tensor"),
        P("tensor", None),
        P("tensor"),
        P("tensor"),
        P("tensor"),
        P("tensor"),
        P("tensor"),
        P("dp", "tensor", None),
        P("dp"),
    )
    out = (
        P("dp", "tensor", None),
        P("dp", "tensor", None),
        P("tensor", None),
        P("tensor"),
        P("tensor", None),
        P("tensor"),
        P("tensor"),
        P("tensor"),
        P("tensor"),
        P("tensor"),
    )
    return jax.shard_map(on_device, mesh=mesh, in_specs=spec, out_specs=out, check_vma=False)
```

```python
import math

import jax
import jax.numpy as jnp
import numpy as np
from jax import lax
from jax.experimental import pallas as pl
from jax.experimental.pallas import tpu as pltpu
from jax.sharding import PartitionSpec as P

EPSILON = 1e-12
MESH = pl.DeviceIdType.MESH
BF = jnp.bfloat16
F32 = jnp.float32


def token_tables(length, group):
    half = length // (2 * group)

    def wave(n, k):
        angle = (n[:, None] * k[None, :] % length) * (2.0 * math.pi / length)
        return np.cos(angle), np.sin(angle)

    n = np.arange(length, dtype=np.int64)
    k = np.arange(length // 2).reshape(group, half)
    columns = np.stack([k[:, 0::2], k[:, 1::2]], axis=1)
    cos, sin = wave(n[: length // 2], columns.reshape(-1))
    shape = (length // 2, group, 2, 1, half // 2)
    main = np.concatenate([cos.reshape(shape), sin.reshape(shape)], axis=3)
    main = main.reshape(length // 2, group, 2 * half).transpose(1, 0, 2).reshape(-1, 2 * half)
    edge_cos, edge_sin = wave(half * (np.arange(group) + 1), n)
    edge = np.stack([edge_cos, np.where(np.abs(edge_sin) < 1e-9, 0.0, edge_sin)], axis=1)
    return main.astype(BF), edge.reshape(2 * group, length).astype(BF)


def hidden_tables(width):
    ids = np.arange(width, dtype=np.int64)
    angle = (ids[:, None] * ids[None, :] % width) * (2.0 * math.pi / width)
    return np.cos(angle).astype(BF), np.sin(angle).astype(BF)


class Place:
    def __init__(self, n_dp, n_tensor):
        self.n_dp, self.n_tensor = n_dp, n_tensor
        self.slices = n_tensor // 2
        self.low = self.slices // 2
        self.dp = lax.axis_index("dp")
        self.tensor = lax.axis_index("tensor")
        self.x, self.core = self.dp // 2, self.dp % 2
        self.z, self.y = self.tensor // 2, self.tensor % 2
        self.z_high, self.z_low = self.z // self.low, self.z % self.low
        self.g = (self.z_low * 2 + self.core) * 2 + self.y
        self.block = self.block_of(self.g)

    def block_of(self, g):
        return (g // 2 % 2 * self.low + g // 4) * 2 + g % 2

    def member(self, g, z_high):
        return (self.x * 2 + g // 2 % 2, (z_high * self.low + g // 4) * 2 + g % 2)

    def high_of(self, j):
        return self.core ^ (j % 2)

    def dp_from(self, j):
        return self.x * 2 + (self.z_high ^ (j % 2))

    def peer(self, offset):
        g = self.g ^ offset
        return self.member(g, self.z_high), g


ANY = pl.BlockSpec(memory_space=pl.ANY)


def on_device(
    words, w_in, b_in, w_out, b_out, gain_one, shift_one, gain_two, shift_two, cotangent, valid
):
    seqs, columns, length = words.shape
    width = w_in.shape[1]
    n_dp, n_tensor = lax.axis_size("dp"), lax.axis_size("tensor")
    group = n_tensor
    half = length // (2 * group)
    mix_scale = 1.0 / math.sqrt(length * width)
    table, edge_table = token_tables(length, group)
    hid_cos, hid_sin = hidden_tables(width)

    table = jnp.asarray(table)
    edge_table = jnp.asarray(edge_table)
    units = w_in.shape[0] * n_tensor
    tokens = 2 * half

    def dot(a, b, da, db):
        return lax.dot_general(a, b, (((da,), (db,)), ((), ())), preferred_element_type=F32)

    wide = 512

    n_slots = 4

    def layer_body(
        x_ref, c_ref, win_ref, wout_ref, cos_ref, sin_ref, table_ref, edge_ref,
        b_in_ref, b_out_ref, gain_one_ref, shift_one_ref, gain_two_ref, shift_two_ref, valid_ref,
        act_o, gu_o, ge_o, gf_o, gw_o, gin_o, gout_o, vec_o,
        win, wout, cos, sin, xb, ub, eb, cb, ab, a_all, m_all, nl, gl, f, tile, edge_v, slots,
        perm, e_send, rows_ref, bacc, vacc, b_in_v, vec, vrows, drows, grows, drows2, spare,
        load, slice_send, slice_recv, tok_send, tok_recv, vec_send, vec_recv, gather_send, gather_recv,
        cot_send, cot_own, cot_recv, act_send, act_own, act_recv, col_send, col_recv,
        ready, rs_send, rs_recv, table_sem, home_send, home_recv, more_send, more_recv, more_free,
        vg_send, vg_recv,
    ):
        at = Place(n_dp, n_tensor)
        barrier = pltpu.get_barrier_semaphore()
        others = n_dp * n_tensor - 1
        def greet(i, c):
            k = (at.dp * n_tensor + at.tensor + i) % (others + 1)
            pl.semaphore_signal(
                barrier, inc=1, device_id=(k // n_tensor, k % n_tensor), device_id_type=MESH)
            return c
        lax.fori_loop(1, others + 1, greet, 0)
        pl.semaphore_wait(barrier, others)

        def wait(ref, sem):
            pltpu.make_async_copy(ref, ref, sem).wait()

        def lanes(g):
            return (
                pl.ds(pl.multiple_of(g * half, 128), half),
                pl.ds(pl.multiple_of(length - (g + 1) * half, 128), half),
            )

        parts = (pl.ds(0, half), pl.ds(half, half))
        own = lambda j: pl.ds(j * tokens, tokens)
        f1, f2, f3 = [f.at[pl.ds(k * width, width)] for k in range(3)]
        rows_of = lambda b: pl.ds(pl.multiple_of(b * columns, 16), columns)

        def cot_start(j):
            high = at.high_of(j)
            for offset in range(group):
                g = at.g ^ offset
                for p in range(2):
                    src = c_ref.at[j, :, lanes(g)[p]]
                    dst = cb.at[pl.ds(pl.multiple_of(j * width + at.tensor * columns, 16), columns), parts[p]]
                    device = at.member(g, high)
                    if offset:
                        pltpu.make_async_remote_copy(src, dst, cot_send.at[j], cot_recv.at[j], device, MESH).start()
                    else:
                        @pl.when(high == at.z_high)
                        def _():
                            pltpu.make_async_copy(src, dst, cot_recv.at[j]).start()

                        @pl.when(high != at.z_high)
                        def _():
                            pltpu.make_async_remote_copy(src, dst, cot_own.at[j], cot_recv.at[j], device, MESH).start()

        def cot_finish(j):
            high = at.high_of(j)
            wait(c_ref.at[j, :, pl.ds(0, length - 2 * half)], cot_send.at[j])

            @pl.when(high != at.z_high)
            def _():
                wait(c_ref.at[j, :, pl.ds(0, 2 * half)], cot_own.at[j])

        def act_start(j):
            dp = at.dp_from(j)
            for offset in range(n_tensor):
                b = at.tensor ^ offset
                for p in range(2):
                    src = ab.at[j, rows_of(b), parts[p]]
                    dst = act_o.at[j, :, lanes(at.g)[p]]
                    if offset:
                        pltpu.make_async_remote_copy(src, dst, act_send.at[j], act_recv.at[j], (dp, b), MESH).start()
                    else:
                        @pl.when(dp == at.dp)
                        def _():
                            pltpu.make_async_copy(src, dst, act_recv.at[j]).start()

                        @pl.when(dp != at.dp)
                        def _():
                            pltpu.make_async_remote_copy(src, dst, act_own.at[j], act_recv.at[j], (dp, b), MESH).start()

        def act_sent(j):
            dp = at.dp_from(j)
            wait(ab.at[j, pl.ds(0, width - columns)], act_send.at[j])

            @pl.when(dp != at.dp)
            def _():
                wait(ab.at[j, pl.ds(0, columns)], act_own.at[j])

            wait(act_o.at[j], act_recv.at[j])

        def col_moves(j):
            for offset in range(group):
                device, g_ = at.peer(offset)
                rows = rows_of(at.block_of(g_))
                for i, (src, dst) in enumerate((
                    (ub.at[j, rows], gu_o.at[at.g, pl.ds(j * columns, columns)]),
                    (eb.at[j, pl.ds(pl.multiple_of(at.block_of(g_) * er, 16), er)], ge_o.at[at.g, pl.ds(j * er, er)]),
                    (xb.at[j, rows, parts[0]], gf_o.at[j, :, lanes(at.g)[0]]),
                    (xb.at[j, rows, parts[1]], gf_o.at[j, :, lanes(at.g)[1]]),
                )):
                    kind = min(i, 2)
                    if offset:
                        yield pltpu.make_async_remote_copy(
                            src, dst, col_send.at[j, kind], col_recv.at[j, kind], device, MESH)
                    else:
                        yield pltpu.make_async_copy(src, dst, col_recv.at[j, kind])

        def col_finish(j):
            rest = pl.ds(0, width - columns)
            wait(ub.at[j, rest], col_send.at[j, 0])
            wait(eb.at[j, pl.ds(0, (n_tensor - 1) * er)], col_send.at[j, 1])
            wait(xb.at[j, rest], col_send.at[j, 2])

        def col_arrived(j):
            wait(gu_o.at[:, pl.ds(j * columns, columns)], col_recv.at[j, 0])
            wait(ge_o.at[:, pl.ds(j * er, er)], col_recv.at[j, 1])
            wait(gf_o.at[j], col_recv.at[j, 2])

        two = own(2)
        n_pieces = length // tokens

        def slice_at(j):
            high = at.high_of(j)
            dp = at.x * 2 + at.z_high
            return (dp, (high * at.low + at.z_low) * 2 + at.y), jnp.logical_and(dp == at.dp, high == at.z_high)

        def slice_start(j):
            device, here = slice_at(j)
            for k in range(n_pieces):
                src = x_ref.at[j, :, pl.ds(k * tokens, tokens)]
                dst = a_all.at[pl.ds(j * width + k * columns, columns), two]

                @pl.when(here)
                def _():
                    pltpu.make_async_copy(src, dst, slice_recv.at[j]).start()

                @pl.when(jnp.logical_not(here))
                def _():
                    pltpu.make_async_remote_copy(src, dst, slice_send.at[j], slice_recv.at[j], device, MESH).start()

        def slice_finish(j):
            _, here = slice_at(j)

            @pl.when(jnp.logical_not(here))
            def _():
                wait(x_ref.at[j], slice_send.at[j])

        n_chunks = length // 2 // depth
        per = depth // tokens
        er = 2 * group
        edge_rows = lambda b: pl.ds(pl.multiple_of(b * er, 16), er)
        def slot_at(i):
            return slots.at[pl.ds(i % n_slots * depth, depth)]

        def table_rows(c, g):
            return table_ref.at[pl.ds(pl.multiple_of(g * (length // 2) + c * depth, 16), depth)]

        order = [(offset, c) for offset in reversed(range(group)) for c in range(n_chunks)]
        def front_load(i):
            offset, c = order[i]
            return pltpu.make_async_copy(table_rows(c, at.g ^ offset), slot_at(i), table_sem.at[i % n_slots])

        def to_tokens(js, offset, kinds):
            device, g = at.peer(offset)
            rows = rows_of(at.block)
            for j in js:
                moves = []
                if "u" in kinds:
                    moves.append((m_all.at[pl.ds(j * width + offset * columns, columns), two], ub.at[j, rows], 0))
                if "e" in kinds:
                    moves.append((e_send.at[pl.ds(j * er, er)], eb.at[j, edge_rows(at.block)], 1))
                if "x" in kinds:
                    for p, i in ((0, g), (1, 2 * group - 1 - g)):
                        moves.append((
                            a_all.at[pl.ds(pl.multiple_of(j * width + i // 2 * columns, 16), columns),
                                     pl.ds(pl.multiple_of(2 * tokens + i % 2 * half, 128), half)],
                            xb.at[j, rows, parts[p]], 2))
                for src, dst, kind in moves:
                    if offset:
                        pltpu.make_async_remote_copy(
                            src, dst, tok_send.at[j, kind], tok_recv.at[j, kind], device, MESH).start()
                    else:
                        pltpu.make_async_copy(src, dst, tok_recv.at[j, kind]).start()

        def front_prefetch():
            for i in range(n_slots):
                front_load(i).start()

        def front_pass(js, first):
            m = len(js) * columns
            for offset in range(1, group):
                to_tokens(js[:first], offset, "x")
            for i, j in enumerate(js):
                edge = jnp.zeros((er, columns), F32)
                for k in range(n_pieces // 2):
                    k2 = k + n_pieces // 2
                    low = a_all[j * width + k * columns : j * width + (k + 1) * columns, 2 * tokens : 3 * tokens]
                    high = a_all[j * width + k2 * columns : j * width + (k2 + 1) * columns, 2 * tokens : 3 * tokens]
                    edge = edge + dot(edge_v[:, k * tokens : (k + 1) * tokens], low, 1, 1)
                    edge = edge + dot(edge_v[:, k2 * tokens : (k2 + 1) * tokens], high, 1, 1)
                    low, high = low.astype(F32), high.astype(F32)
                    rows = pl.ds(k * m + i * columns, columns)
                    nl[rows, two] = (low + high).astype(BF)
                    gl[rows, two] = (low - high).astype(BF)
                e_send[j * er : (j + 1) * er, 0:columns] = edge.astype(BF)
            for n, (offset, c) in enumerate(order):
                if c == 0:
                    even = jnp.zeros((m, half), F32)
                    odd = jnp.zeros((m, half), F32)
                front_load(n).wait()
                slot = slot_at(n)
                for s_ in range(per):
                    k = c * per + s_
                    rows = pl.ds(s_ * tokens, tokens)
                    even = even + dot(nl[k * m : (k + 1) * m, two], slot[rows, A], 1, 0)
                    odd = odd + dot(gl[k * m : (k + 1) * m, two], slot[rows, B], 1, 0)
                if n + n_slots < len(order):
                    front_load(n + n_slots).start()
                if c == n_chunks - 1:
                    for i, j in enumerate(js):
                        rows = pl.ds(j * width + offset * columns, columns)
                        mine = slice(i * columns, (i + 1) * columns)
                        m_all[rows, 2 * tokens : 2 * tokens + half] = even[mine].astype(BF)
                        m_all[rows, 2 * tokens + half : 3 * tokens] = odd[mine].astype(BF)
                    to_tokens(js[:first], offset, "ue" if offset else "uex")

        def later_tokens(j):
            for offset in reversed(range(group)):
                to_tokens([j], offset, "uex")

        def tokens_arrived(j):
            wait(ub.at[j], tok_recv.at[j, 0])
            wait(eb.at[j], tok_recv.at[j, 1])
            wait(xb.at[j], tok_recv.at[j, 2])

        def tokens_sent(j):
            rest = pl.ds(0, width - columns)
            wait(ub.at[j, rest], tok_send.at[j, 0])
            wait(eb.at[j, pl.ds(0, (n_tensor - 1) * er)], tok_send.at[j, 1])
            wait(xb.at[j, rest], tok_send.at[j, 2])

        bt = units // n_tensor
        hb, qb = bt // 2, bt // 4
        slices = at.slices
        core, x = at.dp % 2, at.dp // 2 % 2
        flip = lambda bit: (at.dp ^ bit, at.tensor)
        core_peer, x_peer, y_peer = flip(1), flip(2), (at.dp, at.tensor ^ 1)
        z_peer = lambda offset: (at.dp, (at.z ^ offset) * 2 + at.y)
        w_refs, w_bufs = (win_ref, wout_ref), (win, wout)

        far = [(o, p) for o in range(slices) for p in range(2) if o or p]

        def piece(z, p, cc, xx):
            start = (z * 2 + (at.y ^ p)) * bt + cc * hb + xx * qb
            return pl.ds(pl.multiple_of(start, 16), qb)

        def pass_on(level, arr, rows, key, device):
            ref = w_bufs[arr].at[rows]
            pltpu.make_async_remote_copy(
                ref, ref, gather_send.at[level, arr], gather_recv.at[level, arr, key], device, MESH).start()

        def arrive(level, arr, rows, key):
            wait(w_bufs[arr].at[rows], gather_recv.at[level, arr, key])

        ways = [(1, at.z < slices - 1), (-1, at.z > 0)]

        def neighbour(way):
            return (at.dp, (at.z + way) * 2 + at.y)

        def gather_start(arr):
            mine = pl.ds(pl.multiple_of(core * hb + x * qb, 16), qb)
            for way, there in ways:
                @pl.when(there)
                def _():
                    pltpu.make_async_remote_copy(
                        w_refs[arr].at[mine], w_bufs[arr].at[piece(at.z, 0, core, x)],
                        gather_send.at[0, arr], gather_recv.at[0, arr, at.z], neighbour(way), MESH).start()
            pltpu.make_async_remote_copy(
                w_refs[arr].at[mine], w_bufs[arr].at[piece(at.z, 0, core, x)],
                gather_send.at[1, arr], gather_recv.at[1, arr, at.z], y_peer, MESH).start()
            pltpu.make_async_copy(
                w_refs[arr], w_bufs[arr].at[pl.ds(pl.multiple_of(at.tensor * bt, 16), bt)], load.at[arr]).start()

        def gather_two():
            for step in range(1, slices):
                for arr, (way, there) in [(arr, w) for arr in range(2) for w in ways]:
                    z = at.z - way * step

                    @pl.when((z >= 0) & (z < slices))
                    def _():
                        rows = piece(z, 0, core, x)
                        arrive(0, arr, rows, z)

                        @pl.when(there)
                        def _():
                            pass_on(0, arr, rows, z, neighbour(way))

                        pass_on(1, arr, rows, z, y_peer)
                        pass_on(2, arr, rows, 2 * z, x_peer)
                        pass_on(3, arr, rows, 4 * z, core_peer)

        def gather_three(arr):
            for o in range(slices):
                z = at.z ^ o
                rows = piece(z, 1, core, x)
                arrive(1, arr, rows, z)
                pass_on(2, arr, rows, 2 * z + 1, x_peer)
                pass_on(3, arr, rows, 4 * z + 2, core_peer)

        def gather_four(arr):
            for o, p in far:
                z = at.z ^ o
                rows = piece(z, p, core, 1 - x)
                arrive(2, arr, rows, 2 * z + p)
                pass_on(3, arr, rows, 2 * (2 * z + p) + 1, core_peer)

        def gather_last(arr):
            pltpu.make_async_copy(
                w_refs[arr], w_bufs[arr].at[pl.ds(pl.multiple_of(at.tensor * bt, 16), bt)], load.at[arr]).wait()
            for o, p in far:
                z = at.z ^ o
                for q in range(2):
                    arrive(3, arr, piece(z, p, 1 - core, 1 - x if q else x), 2 * (2 * z + p) + q)

        def gather_sent():
            for arr in range(2):
                g = w_bufs[arr]
                for step in range(slices):
                    for way, there in ways:
                        z = at.z - way * step

                        @pl.when((z >= 0) & (z < slices) & there)
                        def _():
                            wait(g.at[pl.ds(0, qb)], gather_send.at[0, arr])
                for level, quarters in ((1, slices), (2, len(far)), (3, 2 * len(far))):
                    wait(g.at[pl.ds(0, quarters * qb)], gather_send.at[level, arr])

        def vectors_start():
            rows_ref[...] = jnp.zeros_like(rows_ref)
            for i, ref in enumerate(
                (b_in_ref, b_out_ref, gain_one_ref, shift_one_ref, gain_two_ref, shift_two_ref, valid_ref)):
                rows_ref[i : i + 1, 0 : ref.shape[1]] = ref[...].astype(F32)
            pltpu.make_async_copy(rows_ref, vrows.at[pl.ds(pl.multiple_of(at.tensor * 8, 8), 8)], vec_recv.at[0]).start()
            pltpu.make_async_copy(rows_ref, drows.at[pl.ds(pl.multiple_of(at.dp * 8, 8), 8)], vec_recv.at[1]).start()
            for offset in range(1, n_tensor):
                pltpu.make_async_remote_copy(
                    rows_ref, vrows.at[pl.ds(pl.multiple_of(at.tensor * 8, 8), 8)],
                    vec_send.at[0], vec_recv.at[0], (at.dp, at.tensor ^ offset), MESH).start()
            for offset in range(1, n_dp):
                pltpu.make_async_remote_copy(
                    rows_ref, drows.at[pl.ds(pl.multiple_of(at.dp * 8, 8), 8)],
                    vec_send.at[1], vec_recv.at[1], (at.dp ^ offset, at.tensor), MESH).start()

        def vectors_arrived():
            wait(vrows.at[pl.ds(0, 8 * n_tensor)], vec_recv.at[0])
            wait(drows, vec_recv.at[1])
            wait(vrows.at[pl.ds(0, 8 * (n_tensor - 1))], vec_send.at[0])
            wait(drows.at[pl.ds(0, 8 * (n_dp - 1))], vec_send.at[1])
            turned = vrows[...].T
            for t in range(n_tensor):
                b_in_v[t * bt : (t + 1) * bt, :] = turned[0:bt, 8 * t : 8 * t + 1]
                vec[t * columns : (t + 1) * columns, :] = turned[0:columns, 8 * t + 1 : 8 * t + 6]

        gather_start(0)
        gather_start(1)
        slice_start(0)
        tables = [
            pltpu.make_async_copy(src, dst, load.at[2 + i])
            for i, (src, dst) in enumerate(((edge_ref, edge_v), (cos_ref, cos), (sin_ref, sin)))
        ]
        for move in tables:
            move.start()
        vectors_start()
        front_prefetch()

        place0 = lax.broadcasted_iota(jnp.int32, (tokens, half), 0)
        k1 = lax.broadcasted_iota(jnp.int32, (tokens, half), 1)
        place = lambda k, shift: k // 2 + k % 2 * half + shift * (half // 2)
        one_hot = lambda hit: jnp.where(hit, 1.0, 0.0).astype(BF)
        for shift in range(2):
            perm[:, shift * half : (shift + 1) * half] = one_hot(place0 == place(k1, shift))
            perm[:, (2 + shift) * half : (3 + shift) * half] = one_hot(
                (place0 == place(half - k1, shift)) & (k1 > 0))
        turn0 = lax.broadcasted_iota(jnp.int32, (half, half), 0)
        turn1 = lax.broadcasted_iota(jnp.int32, (half, half), 1)
        turn = one_hot(turn0 + turn1 == half)
        edge0 = lax.broadcasted_iota(jnp.int32, (2 * group, half), 0)
        edge1 = lax.broadcasted_iota(jnp.int32, (2 * group, half), 1)
        pick_u = one_hot((edge0 == 2 * at.g) & (edge1 == 0))
        pick_v = one_hot((edge0 == 2 * at.g + 1) & (edge1 == 0))
        e_send[...] = jnp.zeros_like(e_send)
        A, B = parts
        block = 256
        step = 32

        def over(rows, size, body, carry=None, unroll=2):
            def inner(i, c):
                r = pl.ds(pl.multiple_of(i * size, size), size)
                return body(r, c)
            return lax.fori_loop(0, rows // size, inner, carry, unroll=unroll)

        def fold(v):
            return jnp.sum(v.reshape(v.shape[0] // 8, 8, v.shape[1]), axis=0)

        def lane_fold(v):
            return sum(v[:, k * 128 : (k + 1) * 128] for k in range(v.shape[1] // 128))

        zeros8 = jnp.zeros((8, tokens), F32)

        def mean_of(total):
            return jnp.sum(total, axis=0, keepdims=True) / width

        def statistics(ref):
            total = over(width, step, lambda r, c: c + fold(ref[r, :]), zeros8)
            center = mean_of(total)
            def spread(r, c):
                off = ref[r, :] - center
                return c + fold(off * off)
            var = mean_of(over(width, step, spread, zeros8))
            return center, lax.rsqrt(var + EPSILON)

        bacc[...] = jnp.zeros_like(bacc)
        vacc[...] = jnp.zeros_like(vacc)

        def forward_mix(j):
            tokens_arrived(j)
            for b in range(n_tensor):
                r = pl.ds(b * columns, columns)
                e = eb[j, b * er : (b + 1) * er, 0:columns]
                all_four = dot(ub[j, r, :], perm[...], 1, 0)
                ub[j, r, :] = all_four[:, : 2 * half].astype(BF)
                tile[r, A] = (all_four[:, 2 * half : 3 * half] + dot(e, pick_u, 0, 0)).astype(BF)
                tile[r, B] = (all_four[:, 3 * half :] + dot(e, pick_v, 0, 0)).astype(BF)
            def mixed(r, c):
                f1[r, A] = xb[j, r, A].astype(F32) + mix_scale * (
                    dot(cos[r, :], ub[j, :, A], 1, 0) - dot(sin[r, :], ub[j, :, B], 1, 0))
                f1[r, B] = xb[j, r, B].astype(F32) + mix_scale * (
                    dot(cos[r, :], tile[:, A], 1, 0) + dot(sin[r, :], tile[:, B], 1, 0))
                return c
            over(width, block, mixed, 0, unroll=1)
            center, inverse = statistics(f1)
            def scale(r, c):
                h = (f1[r, :] - center) * inverse
                f1[r, :] = h
                n = h * vec[r, 1:2] + vec[r, 2:3]
                f2[r, :] = n
                nl[r, own(j)] = n.astype(BF)
                return c
            over(width, step, scale, 0)
            return inverse

        c0 = math.sqrt(2.0 / math.pi)
        c1 = c0 * 0.044715

        def forward_mlp(j):
            def inner(r, c):
                v = dot(win[r, :], nl[:, own(j)], 1, 0) + b_in_v[r, :]
                v2 = v * v
                p = 0.5 + 0.5 * jnp.tanh(v * (c0 + c1 * v2))
                a = v * p
                a_all[r, own(j)] = a.astype(BF)
                m_all[r, own(j)] = (p + a * (1.0 - p) * (2.0 * c0 + 6.0 * c1 * v2)).astype(BF)
                return c
            over(units, block, inner, 0, unroll=1)
            def outer(r, c):
                f2[r, :] = f2[r, :] + dot(wout[:, r], a_all[:, own(j)], 0, 0) + vec[r, 0:1]
                return c
            for k in range(width // block):
                outer(pl.ds(k * block, block), 0)

        def second_norm(j):
            center, inverse = statistics(f2)
            flag = drows[pl.ds(pl.multiple_of(at.dp_from(j) * 8, 8), 8), 0:128][6:7, j : j + 1]
            def result(r, c):
                h = (f2[r, :] - center) * inverse
                f2[r, :] = h
                ab[j, r, :] = (h * vec[r, 3:4] + vec[r, 4:5]).astype(BF)
                return c
            over(width, step, result, 0)
            act_start(j)
            wait(cb.at[pl.ds(j * width, width)], cot_recv.at[j])
            def sums(r, c):
                go = cb[pl.ds(pl.multiple_of(j * width + r.start, 16), r.size), :].astype(F32) * flag
                h = f2[r, :]
                goh = go * h
                vacc[3, r, :] += lane_fold(goh)
                vacc[4, r, :] += lane_fold(go)
                gh = go * vec[r, 3:4]
                return c[0] + fold(gh), c[1] + fold(gh * h)
            m1, m2 = over(width, step, sums, (zeros8, zeros8))
            m1, m2 = mean_of(m1), mean_of(m2)
            def back(r, c):
                gh = cb[pl.ds(pl.multiple_of(j * width + r.start, 16), r.size), :].astype(F32) * flag * vec[r, 3:4]
                gs = inverse * (gh - m1 - f2[r, :] * m2)
                vacc[0, r, :] += lane_fold(gs)
                f3[r, :] = gs
                gl[r, own(j)] = gs.astype(BF)
                return c
            over(width, step, back, 0)

        def backward_inner(j):
            def inner(r, c):
                gi = dot(wout[r, :], gl[:, own(j)], 1, 0) * m_all[r, own(j)].astype(F32)
                bacc[r, :] += lane_fold(gi)
                m_all[r, own(j)] = gi.astype(BF)
                return c
            over(units, block, inner, 0, unroll=1)

        def backward_outer(j):
            for k in range(width // block):
                r = pl.ds(k * block, block)
                f3[r, :] = f3[r, :] + dot(win[:, r], m_all[:, own(j)], 0, 0)

        def first_back(j, inverse):
            def sums(r, c):
                gn = f3[r, :]
                h = f1[r, :]
                gnh = gn * h
                vacc[1, r, :] += lane_fold(gnh)
                vacc[2, r, :] += lane_fold(gn)
                gh = gn * vec[r, 1:2]
                return c[0] + fold(gh), c[1] + fold(gh * h)
            m1, m2 = over(width, step, sums, (zeros8, zeros8))
            m1, m2 = mean_of(m1), mean_of(m2)
            def back(r, c):
                gf = inverse * (f3[r, :] * vec[r, 1:2] - m1 - f1[r, :] * m2)
                xb[j, r, :] = gf.astype(BF)
                tile[r, :] = (gf * mix_scale).astype(BF)
                return c
            over(width, step, back, 0)
            def fold_pairs(r, c):
                a = tile[r, A].astype(F32)
                b = tile[r, B]
                t = dot(b, turn, 1, 0)
                ub[j, r, A] = (t + a).astype(BF)
                ub[j, r, B] = (t - a).astype(BF)
                return c
            over(width, block, fold_pairs, 0, unroll=1)
            edge = dot(pick_u + pick_v, tile[:, B], 1, 1).astype(BF)
            is_cos = lax.broadcasted_iota(jnp.int32, (er, columns), 0) % 2 == 0
            for b in range(n_tensor):
                r = pl.ds(b * columns, columns)
                eb[j, b * er : (b + 1) * er, 0:columns] = jnp.where(
                    is_cos, dot(edge, cos[r, :], 1, 1), dot(edge, sin[r, :], 1, 1)).astype(BF)
            for k in range(width // block):
                r = pl.ds(k * block, block)
                tile[r, A] = dot(cos[r, :], ub[j, :, A], 1, 0).astype(BF)
                tile[r, B] = dot(sin[r, :], ub[j, :, B], 1, 0).astype(BF)
            for k in range(width // block):
                r = pl.ds(k * block, block)
                ub[j, r, :] = dot(tile[r, :], perm[:, : 2 * half], 1, 1).astype(BF)
            for move in col_moves(j):
                move.start()

        grads = (wout, win)
        if seqs * tokens >= 2 * width:
            land = lambda rows, arr: a_all.at[rows, pl.ds(arr * width, width)]
        else:
            land = lambda rows, arr: spare.at[rows, pl.ds(arr * width, width)]
        at2 = n_tensor * hb
        at3 = at2 + slices * hb
        at4 = at3 + slices * qb
        at5 = at4 + (slices - 1) * qb
        land1 = lambda arr, k: land(pl.ds(pl.multiple_of(k * hb, 16), hb), arr)
        land3 = lambda arr, k: land(pl.ds(at3 + k * qb, qb), arr)
        land4 = lambda arr, k: land(pl.ds(at4 + k * qb, qb), arr)
        land5 = lambda arr: land(pl.ds(at5, qb), arr)
        def block_at(k):
            y = jnp.where(k < slices, 1 - at.y, at.y)
            return (k % slices) * 2 + y
        def rows_half(k, c):
            return pl.ds(pl.multiple_of(block_at(k) * bt + c * hb, 16), hb)
        def rows_quarter(k, xx):
            return pl.ds(pl.multiple_of(block_at(k) * bt + core * hb + xx * qb, 16), qb)

        def send(src, dst, level, arr, k, device):
            pltpu.make_async_remote_copy(
                src, dst, rs_send.at[level, arr], rs_recv.at[level, arr, k], device, MESH).start()

        def ready_signal():
            for i, device in enumerate([core_peer, x_peer, y_peer] + [z_peer(o) for o in range(1, slices)]
                                       + [flip(1 << b) for b in range(2, n_dp.bit_length() - 1)]):
                pl.semaphore_signal(ready.at[i], inc=1, device_id=device, device_id_type=MESH)

        def ready_wait(i):
            pl.semaphore_wait(ready.at[i], 1)

        def weight_grads(arr, left, right):
            def tile_step(k, c):
                r = pl.ds(pl.multiple_of(block_at(k) * bt, 16), bt)
                grads[arr][r, :] = dot(left[r, :], right[...], 1, 1).astype(BF)
                return c
            lax.fori_loop(0, n_tensor, tile_step, 0)

        def level1(arr):
            def go(k, c):
                send(grads[arr].at[rows_half(k, 1 - core)], land1(arr, k), 0, arr, k, core_peer)
                return c
            lax.fori_loop(0, n_tensor, go, 0)

        def add(arr, rows, landed, level, k):
            wait(landed, rs_recv.at[level, arr, k])
            ref = grads[arr].at[rows]
            n = ref.shape[0]
            def go(i, c):
                r = pl.ds(pl.multiple_of(i * 16, 16), 16)
                ref[r, :] = (ref[r, :].astype(F32) + landed[r, :].astype(F32)).astype(BF)
                return c
            lax.fori_loop(0, n // 16, go, 0, unroll=2)

        def y_first(arr, z):
            return arr == 1 and z >= slices // 2

        def land2_x(arr, z, own_y):
            return land(pl.ds(at2 + z * hb + (qb if own_y else 0), qb), arr)

        def land2_y(arr, z):
            return land(pl.ds(at2 + z * hb, hb), arr)

        def after1(arr):
            for k in range(n_tensor):
                z, own_y = k % slices, k >= slices
                add(arr, rows_half(k, core), land1(arr, k), 0, k)
                if not y_first(arr, z):
                    send(grads[arr].at[rows_quarter(k, 1 - x)], land2_x(arr, z, own_y), 1, arr, k, x_peer)
                elif not own_y:
                    send(grads[arr].at[rows_half(k, core)], land2_y(arr, z), 1, arr, k, y_peer)

        def after2(arr):
            for z in range(slices):
                if y_first(arr, z):
                    add(arr, rows_half(slices + z, core), land2_y(arr, z), 1, z)
                    send(grads[arr].at[rows_quarter(slices + z, 1 - x)], land3(arr, z), 2, arr, z, x_peer)
                else:
                    add(arr, rows_quarter(z, x), land2_x(arr, z, False), 1, z)
                    send(grads[arr].at[rows_quarter(z, x)], land3(arr, z), 2, arr, z, y_peer)
            for z in range(slices):
                if not y_first(arr, z):
                    add(arr, rows_quarter(slices + z, x), land2_x(arr, z, True), 1, slices + z)

        bits = [1 << b for b in range(slices.bit_length() - 1)]
        first_slot = lambda bit: slices - slices // bit

        def after3(arr):
            for z in range(slices):
                add(arr, rows_quarter(slices + z, x), land3(arr, z), 2, z)
            z_send(arr, 1)

        def z_send(arr, bit):
            for i in range(slices // (2 * bit)):
                block_z = at.z ^ (bit + 2 * bit * i)
                send(grads[arr].at[rows_quarter(slices + block_z, x)], land4(arr, first_slot(bit) + i), 3, arr,
                     first_slot(bit) + i, z_peer(bit))

        def z_add(arr, bit):
            for i in range(slices // (2 * bit)):
                add(arr, rows_quarter(slices + (at.z ^ (2 * bit * i)), x), land4(arr, first_slot(bit) + i), 3,
                    first_slot(bit) + i)

        def z_turn(arr):
            for bit in bits[:-1]:
                z_add(arr, bit)
                z_send(arr, 2 * bit)

        def after4(arr):
            mine = rows_quarter(slices + at.z, x)
            z_add(arr, bits[-1])
            for b in range(2, n_dp.bit_length() - 1):
                k = b - 2
                peer_ = flip(1 << b)
                pltpu.make_async_remote_copy(
                    grads[arr].at[mine], land5(arr), more_send.at[arr, k], more_recv.at[arr, k], peer_, MESH).start()
                wait(grads[arr].at[mine], more_send.at[arr, k])
                wait(land5(arr), more_recv.at[arr, k])
                ref = grads[arr].at[mine]
                ref[...] = (ref[...].astype(F32) + land5(arr)[...].astype(F32)).astype(BF)
                if b + 1 < n_dp.bit_length() - 1:
                    pl.semaphore_signal(more_free, inc=1, device_id=peer_, device_id_type=MESH)
                    pl.semaphore_wait(more_free, 1)
            home = pl.ds(pl.multiple_of(core * hb + x * qb, 16), qb)
            out = (gout_o, gin_o)[arr]
            pltpu.make_async_copy(grads[arr].at[mine], out.at[home], rs_recv.at[4, arr, 0]).start()
            for q in range(1, 3):
                pltpu.make_async_remote_copy(
                    grads[arr].at[mine], out.at[home], rs_send.at[4, arr], rs_recv.at[4, arr, q], flip(q), MESH).start()

        def after5(arr):
            out = (gout_o, gin_o)[arr]
            came = out.at[pl.ds(pl.multiple_of(core * hb + (1 - x) * qb, 16), qb)]
            wait(came, rs_recv.at[4, arr, 2])
            pltpu.make_async_remote_copy(came, came, rs_send.at[4, arr], rs_recv.at[4, arr, 3], core_peer, MESH).start()

        def rs_finish(arr):
            g = grads[arr]
            n = n_tensor * hb
            wait(g.at[pl.ds(0, n)], rs_send.at[0, arr])
            wait(g.at[pl.ds(0, slices * hb)], rs_send.at[1, arr])
            wait(g.at[pl.ds(0, slices * qb)], rs_send.at[2, arr])
            wait(g.at[pl.ds(0, (slices - 1) * qb)], rs_send.at[3, arr])
            wait(g.at[pl.ds(0, 3 * qb)], rs_send.at[4, arr])
            for q in (0, 1, 3):
                wait((gout_o, gin_o)[arr].at[pl.ds(0, qb)], rs_recv.at[4, arr, q])

        def table_start(i):
            c, g = i // group, i % group
            return pltpu.make_async_copy(table_rows(c, g), slot_at(i), table_sem.at[i % n_slots])

        def back_prefetch():
            for i in range(n_slots):
                table_start(i).start()

        def words_back(js, acc):
            m = len(js) * columns
            base = js[0] * width
            n_edge = len(js) * er
            some = pl.ds(js[0] * columns, m)
            some_edges = pl.ds(js[0] * er, n_edge)
            for j in js:
                col_arrived(j)
                act_sent(j)
            for g in range(group):
                pltpu.make_async_copy(gu_o.at[g, some], cb.at[pl.ds(base + g * m, m)], table_sem.at[n_slots]).start()
                pltpu.make_async_copy(
                    ge_o.at[g, some_edges], tile.at[pl.ds(g * n_edge, n_edge), pl.ds(0, 128)],
                    table_sem.at[n_slots + 1]).start()
            for j in js:
                for k in range(n_pieces):
                    pltpu.make_async_copy(
                        gf_o.at[j, :, pl.ds(k * tokens, tokens)], ab.at[j, pl.ds(k * columns, columns)],
                        table_sem.at[n_slots + 2]).start()
            wait(cb.at[pl.ds(base, group * m)], table_sem.at[n_slots])
            wait(tile.at[pl.ds(0, group * n_edge), pl.ds(0, 128)], table_sem.at[n_slots + 1])
            for j in js:
                wait(ab.at[j], table_sem.at[n_slots + 2])
            edges = tile[0:n_edge, 0:128].astype(F32)
            for g in range(1, group):
                edges = edges + tile[g * n_edge : (g + 1) * n_edge, 0:128].astype(F32)
            edges = edges.astype(BF)
            for c in range(n_chunks):
                for g in range(group):
                    i = c * group + g
                    table_start(i).wait()
                    for s_ in range(per):
                        t = slot_at(i)[pl.ds(s_ * tokens, tokens), :]
                        left = cb[base + g * m : base + (g + 1) * m, :]
                        even = dot(left[:, :half], t[:, :half], 1, 1)
                        odd = dot(left[:, half:], t[:, half:], 1, 1)
                        at_even = pl.ds(s_ * m, m)
                        at_odd = pl.ds((per + s_) * m, m)
                        if g:
                            acc[at_even, :] += even
                            acc[at_odd, :] += odd
                        else:
                            acc[at_even, :] = even
                            acc[at_odd, :] = odd
                    if i + n_slots < n_chunks * group:
                        table_start(i + n_slots).start()
                for s_ in range(per):
                    for sign in range(2):
                        k = c * per + s_ + sign * (n_pieces // 2)
                        for n, j in enumerate(js):
                            rows = pl.ds(k * columns, columns)
                            even = acc[pl.ds(s_ * m + n * columns, columns), :]
                            odd = acc[pl.ds((per + s_) * m + n * columns, columns), :]
                            edge = dot(edges[n * er : (n + 1) * er, 0:columns], edge_v[:, k * tokens : (k + 1) * tokens], 0, 0)
                            both = even - odd if sign else even + odd
                            ab[j, rows, :] = (both + edge + ab[j, rows, :].astype(F32)).astype(BF)
                            home_start(j, k)

        def home_at(j):
            dp = at.dp_from(j)
            return dp, jnp.logical_and(dp == at.dp, at.block == at.tensor)

        def home_start(j, k):
            dp, here = home_at(j)
            src = ab.at[j, pl.ds(k * columns, columns)]
            dst = gw_o.at[j, :, pl.ds(k * tokens, tokens)]

            @pl.when(here)
            def _():
                pltpu.make_async_copy(src, dst, home_recv.at[j]).start()

            @pl.when(jnp.logical_not(here))
            def _():
                pltpu.make_async_remote_copy(src, dst, home_send.at[j], home_recv.at[j], (dp, at.block), MESH).start()

        def home_finish(j):
            dp, here = home_at(j)

            @pl.when(jnp.logical_not(here))
            def _():
                wait(gw_o.at[j], home_send.at[j])

            wait(gw_o.at[j], home_recv.at[j])

        def vector_grads():
            cols = pl.ds(0, 128)
            vrows[...] = jnp.zeros_like(vrows)
            turned = jnp.zeros((wide, 128), F32)
            scratch = f1.at[pl.ds(0, wide), cols]
            scratch[...] = turned
            for t in range(n_tensor):
                scratch[0:bt, 8 * t : 8 * t + 1] = jnp.sum(bacc[t * bt : (t + 1) * bt, :], axis=1, keepdims=True)
                for i in range(5):
                    scratch[0:columns, 8 * t + 1 + i : 8 * t + 2 + i] = jnp.sum(
                        vacc[i, t * columns : (t + 1) * columns, :], axis=1, keepdims=True)
            vrows[...] = scratch[...].T
            n = 8 * n_tensor
            for offset in range(1, n_dp):
                pltpu.make_async_remote_copy(
                    vrows.at[pl.ds(0, n)], grows.at[pl.ds((offset - 1) * n, n)],
                    vg_send.at[0], vg_recv.at[0], (at.dp ^ offset, at.tensor), MESH).start()

        def vector_grads_two():
            n = 8 * n_tensor
            wait(grows.at[pl.ds(0, (n_dp - 1) * n)], vg_recv.at[0])
            wait(grows.at[pl.ds(0, (n_dp - 1) * n)], vg_send.at[0])
            total = vrows[0:n, :]
            for offset in range(1, n_dp):
                total = total + grows[(offset - 1) * n : offset * n, :]
            vrows[0:n, :] = total
            for offset in range(1, n_tensor):
                t = at.tensor ^ offset
                pltpu.make_async_remote_copy(
                    vrows.at[pl.ds(pl.multiple_of(t * 8, 8), 8)], drows2.at[pl.ds((offset - 1) * 8, 8)],
                    vg_send.at[1], vg_recv.at[1], (at.dp, t), MESH).start()

        def vector_grads_three():
            n = 8 * (n_tensor - 1)
            wait(drows2.at[pl.ds(0, n)], vg_recv.at[1])
            wait(drows2.at[pl.ds(0, n)], vg_send.at[1])
            total = vrows[pl.ds(pl.multiple_of(at.tensor * 8, 8), 8), :]
            for offset in range(1, n_tensor):
                total = total + drows2[(offset - 1) * 8 : offset * 8, :]
            vec_o[...] = total

        gather_two()
        slice_start(1)
        gather_three(0)
        gather_three(1)
        for move in tables:
            move.wait()
        vectors_arrived()
        wait(a_all.at[pl.ds(0, width), two], slice_recv.at[0])
        for j in range(2, seqs):
            slice_start(j)
        cot_start(0)
        front_pass([0], 1)
        front_prefetch()
        gather_four(0)
        for i in range(1, seqs):
            wait(a_all.at[pl.ds(i * width, width), two], slice_recv.at[i])
        front_pass(list(range(1, seqs)), 1)
        back_prefetch()
        gather_four(1)
        inverse = forward_mix(0)
        for arr in range(2):
            gather_last(arr)
        cot_start(1)
        last = seqs - 1
        for j in range(seqs):
            if j:
                inverse = forward_mix(j)
            if j == last:
                for i in range(seqs):
                    tokens_sent(i)
            forward_mlp(j)
            if 0 < j and j + 1 < seqs:
                cot_start(j + 1)
            if j == last:
                words_back([0], f3)
                back_prefetch()
            second_norm(j)
            backward_inner(j)
            if j + 2 < seqs:
                later_tokens(j + 2)
            backward_outer(j)
            first_back(j, inverse)
        gather_sent()
        weight_grads(0, a_all, gl)
        ready_signal()
        ready_wait(0)
        level1(0)
        weight_grads(1, m_all, nl)
        level1(1)
        ready_wait(1)
        after1(0)
        vector_grads()
        ready_wait(2)
        after1(1)
        for j in range(1, last):
            words_back([j], f2)
            back_prefetch()
        after2(0)
        words_back([last], f2)
        for i in range(3, 3 + slices - 1 + max(0, n_dp.bit_length() - 3)):
            ready_wait(i)
        after3(0)
        after2(1)
        z_turn(0)
        after3(1)
        z_turn(1)
        vector_grads_two()
        after4(0)
        after4(1)
        vector_grads_three()
        after5(0)
        after5(1)
        for j in range(seqs):
            slice_finish(j)
            cot_finish(j)
            col_finish(j)
            home_finish(j)
        rs_finish(0)
        rs_finish(1)


    shape = jax.ShapeDtypeStruct
    dma = pltpu.SemaphoreType.DMA
    whole_vmem = pl.BlockSpec(memory_space=pltpu.VMEM)
    depth = min(1024, length // 2)
    need_spare = seqs * tokens < 2 * width
    regular = pltpu.SemaphoreType.REGULAR
    activations, _, _, _, gw, g_in, g_out, vec_g = pl.pallas_call(
        layer_body,
        out_shape=[
            shape(words.shape, BF),
            shape((group, seqs * columns, tokens), BF),
            shape((group, seqs * 2 * group, 128), BF),
            shape((seqs, columns, length), BF),
            shape((seqs, columns, length), BF),
            shape(w_in.shape, BF),
            shape(w_in.shape, BF),
            shape((8, wide), F32),
        ],
        in_specs=[ANY] * 8 + [whole_vmem] * 7,
        out_specs=[ANY] * 7 + [whole_vmem],
        scratch_shapes=[
            pltpu.VMEM((units, width), BF),
            pltpu.VMEM((units, width), BF),
            pltpu.VMEM((width, width), BF),
            pltpu.VMEM((width, width), BF),
            pltpu.VMEM((seqs, width, tokens), BF),
            pltpu.VMEM((seqs, width, tokens), BF),
            pltpu.VMEM((seqs, n_tensor * 2 * group, 128), BF),
            pltpu.VMEM((group * seqs * columns, tokens), BF),
            pltpu.VMEM((seqs, width, tokens), BF),
            pltpu.VMEM((units, seqs * tokens), BF),
            pltpu.VMEM((units, seqs * tokens), BF),
            pltpu.VMEM((width, seqs * tokens), BF),
            pltpu.VMEM((width, seqs * tokens), BF),
            pltpu.VMEM((3 * width, tokens), F32),
            pltpu.VMEM((width, tokens), BF),
            pltpu.VMEM((2 * group, length), BF),
            pltpu.VMEM((n_slots * depth, tokens), BF),
            pltpu.VMEM((tokens, 4 * half), BF),
            pltpu.VMEM((seqs * 2 * group, 128), BF),
            pltpu.VMEM((8, wide), F32),
            pltpu.VMEM((units, 128), F32),
            pltpu.VMEM((5, width, 128), F32),
            pltpu.VMEM((units, 1), F32),
            pltpu.VMEM((width, 5), F32),
            pltpu.VMEM((128, wide), F32),
            pltpu.VMEM((8 * n_dp, wide), F32),
            pltpu.VMEM((8 * n_tensor * (n_dp - 1), wide), F32),
            pltpu.VMEM((8 * (n_tensor - 1), wide), F32),
            pltpu.VMEM((units, 2 * width) if need_spare else (16, 128), BF),
            dma((5,)),
            dma((seqs,)),
            dma((seqs,)),
            dma((seqs, 3)),
            dma((seqs, 3)),
            dma((2,)),
            dma((2,)),
            dma((4, 2)),
            dma((4, 2, 2 * n_tensor)),
            dma((seqs,)),
            dma((seqs,)),
            dma((seqs,)),
            dma((seqs,)),
            dma((seqs,)),
            dma((seqs,)),
            dma((seqs, 3)),
            dma((seqs, 3)),
            regular((3 + n_tensor // 2 + n_dp,)),
            dma((5, 2)),
            dma((5, 2, n_tensor)),
            dma((n_slots + 3,)),
            dma((seqs,)),
            dma((seqs,)),
            dma((2, n_dp)),
            dma((2, n_dp)),
            regular,
            dma((2,)),
            dma((2,)),
        ],
        compiler_params=pltpu.CompilerParams(
            collective_id=1, has_side_effects=True, vmem_limit_bytes=64 * 1024 * 1024
        ),
    )(
        words, cotangent, w_in, w_out, jnp.asarray(hid_cos), jnp.asarray(hid_sin), table, edge_table,
        *[v[None] for v in (b_in, b_out, gain_one, shift_one, gain_two, shift_two, valid)],
    )
    grad_words = gw.astype(F32)

    grad_w_in = g_in.astype(F32)
    grad_w_out = g_out.astype(F32)
    return (
        activations,
        grad_words,
        grad_w_in,
        vec_g[0, : w_in.shape[0]],
        grad_w_out,
        vec_g[1, :columns],
        vec_g[2, :columns],
        vec_g[3, :columns],
        vec_g[4, :columns],
        vec_g[5, :columns],
    )


def solution(mesh):
    spec = (
        P("dp", "tensor", None),
        P("tensor", None),
        P("tensor"),
        P("tensor", None),
        P("tensor"),
        P("tensor"),
        P("tensor"),
        P("tensor"),
        P("tensor"),
        P("dp", "tensor", None),
        P("dp"),
    )
    out = (
        P("dp", "tensor", None),
        P("dp", "tensor", None),
        P("tensor", None),
        P("tensor"),
        P("tensor", None),
        P("tensor"),
        P("tensor"),
        P("tensor"),
        P("tensor"),
        P("tensor"),
    )
    return jax.shard_map(on_device, mesh=mesh, in_specs=spec, out_specs=out, check_vma=False)
```

```python
import math

import jax
import jax.numpy as jnp
import numpy as np
from jax import lax
from jax.experimental import pallas as pl
from jax.experimental.pallas import tpu as pltpu
from jax.sharding import PartitionSpec as P

EPSILON = 1e-12
MESH = pl.DeviceIdType.MESH
BF = jnp.bfloat16
F32 = jnp.float32


def token_tables(length, group):
    half = length // (2 * group)

    def wave(n, k):
        angle = (n[:, None] * k[None, :] % length) * (2.0 * math.pi / length)
        return np.cos(angle), np.sin(angle)

    n = np.arange(length, dtype=np.int64)
    k = np.arange(length // 2).reshape(group, half)
    columns = np.stack([k[:, 0::2], k[:, 1::2]], axis=1)
    cos, sin = wave(n[: length // 2], columns.reshape(-1))
    shape = (length // 2, group, 2, 1, half // 2)
    main = np.concatenate([cos.reshape(shape), sin.reshape(shape)], axis=3)
    main = main.reshape(length // 2, group, 2 * half).transpose(1, 0, 2).reshape(-1, 2 * half)
    edge_cos, edge_sin = wave(half * (np.arange(group) + 1), n)
    edge = np.stack([edge_cos, np.where(np.abs(edge_sin) < 1e-9, 0.0, edge_sin)], axis=1)
    return main.astype(BF), edge.reshape(2 * group, length).astype(BF)


def hidden_tables(width):
    ids = np.arange(width, dtype=np.int64)
    angle = (ids[:, None] * ids[None, :] % width) * (2.0 * math.pi / width)
    return np.cos(angle).astype(BF), np.sin(angle).astype(BF)


class Place:
    def __init__(self, n_dp, n_tensor):
        self.n_dp, self.n_tensor = n_dp, n_tensor
        self.slices = n_tensor // 2
        self.low = self.slices // 2
        self.dp = lax.axis_index("dp")
        self.tensor = lax.axis_index("tensor")
        self.x, self.core = self.dp // 2, self.dp % 2
        self.z, self.y = self.tensor // 2, self.tensor % 2
        self.z_high, self.z_low = self.z // self.low, self.z % self.low
        self.g = (self.z_low * 2 + self.core) * 2 + self.y
        self.block = self.block_of(self.g)

    def block_of(self, g):
        return (g // 2 % 2 * self.low + g // 4) * 2 + g % 2

    def member(self, g, z_high):
        return (self.x * 2 + g // 2 % 2, (z_high * self.low + g // 4) * 2 + g % 2)

    def high_of(self, j):
        return self.core ^ (j % 2)

    def dp_from(self, j):
        return self.x * 2 + (self.z_high ^ (j % 2))

    def peer(self, offset):
        g = self.g ^ offset
        return self.member(g, self.z_high), g


ANY = pl.BlockSpec(memory_space=pl.ANY)


def on_device(
    words, w_in, b_in, w_out, b_out, gain_one, shift_one, gain_two, shift_two, cotangent, valid
):
    seqs, columns, length = words.shape
    width = w_in.shape[1]
    n_dp, n_tensor = lax.axis_size("dp"), lax.axis_size("tensor")
    group = n_tensor
    half = length // (2 * group)
    mix_scale = 1.0 / math.sqrt(length * width)
    table, edge_table = token_tables(length, group)
    hid_cos, hid_sin = hidden_tables(width)

    table = jnp.asarray(table)
    edge_table = jnp.asarray(edge_table)
    units = w_in.shape[0] * n_tensor
    tokens = 2 * half

    def dot(a, b, da, db):
        return lax.dot_general(a, b, (((da,), (db,)), ((), ())), preferred_element_type=F32)

    wide = 512

    n_slots = 4

    def layer_body(
        x_ref, c_ref, win_ref, wout_ref, cos_ref, sin_ref, table_ref, edge_ref,
        b_in_ref, b_out_ref, gain_one_ref, shift_one_ref, gain_two_ref, shift_two_ref, valid_ref,
        act_o, gu_o, ge_o, gf_o, gw_o, gin_o, gout_o, vec_o,
        win, wout, cos, sin, xb, ub, eb, cb, ab, a_all, m_all, nl, gl, f, tile, edge_v, slots,
        perm, e_send, rows_ref, bacc, vacc, b_in_v, vec, vrows, drows, grows, drows2, spare,
        load, slice_send, slice_recv, tok_send, tok_recv, vec_send, vec_recv, gather_send, gather_recv,
        cot_send, cot_own, cot_recv, act_send, act_own, act_recv, col_send, col_recv,
        ready, rs_send, rs_recv, table_sem, home_send, home_recv, more_send, more_recv, more_free,
        vg_send, vg_recv,
    ):
        at = Place(n_dp, n_tensor)
        barrier = pltpu.get_barrier_semaphore()
        others = n_dp * n_tensor - 1
        def greet(i, c):
            k = (at.dp * n_tensor + at.tensor + i) % (others + 1)
            pl.semaphore_signal(
                barrier, inc=1, device_id=(k // n_tensor, k % n_tensor), device_id_type=MESH)
            return c
        lax.fori_loop(1, others + 1, greet, 0)
        pl.semaphore_wait(barrier, others)

        def wait(ref, sem):
            pltpu.make_async_copy(ref, ref, sem).wait()

        def lanes(g):
            return (
                pl.ds(pl.multiple_of(g * half, 128), half),
                pl.ds(pl.multiple_of(length - (g + 1) * half, 128), half),
            )

        parts = (pl.ds(0, half), pl.ds(half, half))
        own = lambda j: pl.ds(j * tokens, tokens)
        f1, f2, f3 = [f.at[pl.ds(k * width, width)] for k in range(3)]
        rows_of = lambda b: pl.ds(pl.multiple_of(b * columns, 16), columns)

        def cot_start(j):
            high = at.high_of(j)
            for offset in range(group):
                g = at.g ^ offset
                for p in range(2):
                    src = c_ref.at[j, :, lanes(g)[p]]
                    dst = cb.at[pl.ds(pl.multiple_of(j * width + at.tensor * columns, 16), columns), parts[p]]
                    device = at.member(g, high)
                    if offset:
                        pltpu.make_async_remote_copy(src, dst, cot_send.at[j], cot_recv.at[j], device, MESH).start()
                    else:
                        @pl.when(high == at.z_high)
                        def _():
                            pltpu.make_async_copy(src, dst, cot_recv.at[j]).start()

                        @pl.when(high != at.z_high)
                        def _():
                            pltpu.make_async_remote_copy(src, dst, cot_own.at[j], cot_recv.at[j], device, MESH).start()

        def cot_finish(j):
            high = at.high_of(j)
            wait(c_ref.at[j, :, pl.ds(0, length - 2 * half)], cot_send.at[j])

            @pl.when(high != at.z_high)
            def _():
                wait(c_ref.at[j, :, pl.ds(0, 2 * half)], cot_own.at[j])

        def act_start(j):
            dp = at.dp_from(j)
            for offset in range(n_tensor):
                b = at.tensor ^ offset
                for p in range(2):
                    src = ab.at[j, rows_of(b), parts[p]]
                    dst = act_o.at[j, :, lanes(at.g)[p]]
                    if offset:
                        pltpu.make_async_remote_copy(src, dst, act_send.at[j], act_recv.at[j], (dp, b), MESH).start()
                    else:
                        @pl.when(dp == at.dp)
                        def _():
                            pltpu.make_async_copy(src, dst, act_recv.at[j]).start()

                        @pl.when(dp != at.dp)
                        def _():
                            pltpu.make_async_remote_copy(src, dst, act_own.at[j], act_recv.at[j], (dp, b), MESH).start()

        def act_sent(j):
            dp = at.dp_from(j)
            wait(ab.at[j, pl.ds(0, width - columns)], act_send.at[j])

            @pl.when(dp != at.dp)
            def _():
                wait(ab.at[j, pl.ds(0, columns)], act_own.at[j])

            wait(act_o.at[j], act_recv.at[j])

        def col_moves(j):
            for offset in range(group):
                device, g_ = at.peer(offset)
                rows = rows_of(at.block_of(g_))
                for i, (src, dst) in enumerate((
                    (ub.at[j, rows], gu_o.at[at.g, pl.ds(j * columns, columns)]),
                    (eb.at[j, pl.ds(pl.multiple_of(at.block_of(g_) * er, 16), er)], ge_o.at[at.g, pl.ds(j * er, er)]),
                    (xb.at[j, rows, parts[0]], gf_o.at[j, :, lanes(at.g)[0]]),
                    (xb.at[j, rows, parts[1]], gf_o.at[j, :, lanes(at.g)[1]]),
                )):
                    kind = min(i, 2)
                    if offset:
                        yield pltpu.make_async_remote_copy(
                            src, dst, col_send.at[j, kind], col_recv.at[j, kind], device, MESH)
                    else:
                        yield pltpu.make_async_copy(src, dst, col_recv.at[j, kind])

        def col_finish(j):
            rest = pl.ds(0, width - columns)
            wait(ub.at[j, rest], col_send.at[j, 0])
            wait(eb.at[j, pl.ds(0, (n_tensor - 1) * er)], col_send.at[j, 1])
            wait(xb.at[j, rest], col_send.at[j, 2])

        def col_arrived(j):
            wait(gu_o.at[:, pl.ds(j * columns, columns)], col_recv.at[j, 0])
            wait(ge_o.at[:, pl.ds(j * er, er)], col_recv.at[j, 1])
            wait(gf_o.at[j], col_recv.at[j, 2])

        two = own(2)
        n_pieces = length // tokens

        def slice_at(j):
            high = at.high_of(j)
            dp = at.x * 2 + at.z_high
            return (dp, (high * at.low + at.z_low) * 2 + at.y), jnp.logical_and(dp == at.dp, high == at.z_high)

        def slice_start(j):
            device, here = slice_at(j)
            for k in range(n_pieces):
                src = x_ref.at[j, :, pl.ds(k * tokens, tokens)]
                dst = a_all.at[pl.ds(j * width + k * columns, columns), two]

                @pl.when(here)
                def _():
                    pltpu.make_async_copy(src, dst, slice_recv.at[j]).start()

                @pl.when(jnp.logical_not(here))
                def _():
                    pltpu.make_async_remote_copy(src, dst, slice_send.at[j], slice_recv.at[j], device, MESH).start()

        def slice_finish(j):
            _, here = slice_at(j)

            @pl.when(jnp.logical_not(here))
            def _():
                wait(x_ref.at[j], slice_send.at[j])

        n_chunks = length // 2 // depth
        per = depth // tokens
        er = 2 * group
        edge_rows = lambda b: pl.ds(pl.multiple_of(b * er, 16), er)
        def slot_at(i):
            return slots.at[pl.ds(i % n_slots * depth, depth)]

        def table_rows(c, g):
            return table_ref.at[pl.ds(pl.multiple_of(g * (length // 2) + c * depth, 16), depth)]

        order = [(offset, c) for offset in reversed(range(group)) for c in range(n_chunks)]
        def front_load(i):
            offset, c = order[i]
            return pltpu.make_async_copy(table_rows(c, at.g ^ offset), slot_at(i), table_sem.at[i % n_slots])

        def to_tokens(js, offset, kinds):
            device, g = at.peer(offset)
            rows = rows_of(at.block)
            for j in js:
                moves = []
                if "u" in kinds:
                    moves.append((m_all.at[pl.ds(j * width + offset * columns, columns), two], ub.at[j, rows], 0))
                if "e" in kinds:
                    moves.append((e_send.at[pl.ds(j * er, er)], eb.at[j, edge_rows(at.block)], 1))
                if "x" in kinds:
                    for p, i in ((0, g), (1, 2 * group - 1 - g)):
                        moves.append((
                            a_all.at[pl.ds(pl.multiple_of(j * width + i // 2 * columns, 16), columns),
                                     pl.ds(pl.multiple_of(2 * tokens + i % 2 * half, 128), half)],
                            xb.at[j, rows, parts[p]], 2))
                for src, dst, kind in moves:
                    if offset:
                        pltpu.make_async_remote_copy(
                            src, dst, tok_send.at[j, kind], tok_recv.at[j, kind], device, MESH).start()
                    else:
                        pltpu.make_async_copy(src, dst, tok_recv.at[j, kind]).start()

        def front_prefetch():
            for i in range(n_slots):
                front_load(i).start()

        def front_pass(js, first):
            m = len(js) * columns
            for offset in range(1, group):
                to_tokens(js[:first], offset, "x")
            for i, j in enumerate(js):
                edge = jnp.zeros((er, columns), F32)
                for k in range(n_pieces // 2):
                    k2 = k + n_pieces // 2
                    low = a_all[j * width + k * columns : j * width + (k + 1) * columns, 2 * tokens : 3 * tokens]
                    high = a_all[j * width + k2 * columns : j * width + (k2 + 1) * columns, 2 * tokens : 3 * tokens]
                    edge = edge + dot(edge_v[:, k * tokens : (k + 1) * tokens], low, 1, 1)
                    edge = edge + dot(edge_v[:, k2 * tokens : (k2 + 1) * tokens], high, 1, 1)
                    low, high = low.astype(F32), high.astype(F32)
                    rows = pl.ds(k * m + i * columns, columns)
                    nl[rows, two] = (low + high).astype(BF)
                    gl[rows, two] = (low - high).astype(BF)
                e_send[j * er : (j + 1) * er, 0:columns] = edge.astype(BF)
            for n, (offset, c) in enumerate(order):
                if c == 0:
                    even = jnp.zeros((m, half), F32)
                    odd = jnp.zeros((m, half), F32)
                front_load(n).wait()
                slot = slot_at(n)
                for s_ in range(per):
                    k = c * per + s_
                    rows = pl.ds(s_ * tokens, tokens)
                    even = even + dot(nl[k * m : (k + 1) * m, two], slot[rows, A], 1, 0)
                    odd = odd + dot(gl[k * m : (k + 1) * m, two], slot[rows, B], 1, 0)
                if n + n_slots < len(order):
                    front_load(n + n_slots).start()
                if c == n_chunks - 1:
                    for i, j in enumerate(js):
                        rows = pl.ds(j * width + offset * columns, columns)
                        mine = slice(i * columns, (i + 1) * columns)
                        m_all[rows, 2 * tokens : 2 * tokens + half] = even[mine].astype(BF)
                        m_all[rows, 2 * tokens + half : 3 * tokens] = odd[mine].astype(BF)
                    to_tokens(js[:first], offset, "ue" if offset else "uex")

        def later_tokens(j):
            for offset in reversed(range(group)):
                to_tokens([j], offset, "uex")

        def tokens_arrived(j):
            wait(ub.at[j], tok_recv.at[j, 0])
            wait(eb.at[j], tok_recv.at[j, 1])
            wait(xb.at[j], tok_recv.at[j, 2])

        def tokens_sent(j):
            rest = pl.ds(0, width - columns)
            wait(ub.at[j, rest], tok_send.at[j, 0])
            wait(eb.at[j, pl.ds(0, (n_tensor - 1) * er)], tok_send.at[j, 1])
            wait(xb.at[j, rest], tok_send.at[j, 2])

        bt = units // n_tensor
        hb, qb = bt // 2, bt // 4
        slices = at.slices
        core, x = at.dp % 2, at.dp // 2 % 2
        flip = lambda bit: (at.dp ^ bit, at.tensor)
        core_peer, x_peer, y_peer = flip(1), flip(2), (at.dp, at.tensor ^ 1)
        z_peer = lambda offset: (at.dp, (at.z ^ offset) * 2 + at.y)
        w_refs, w_bufs = (win_ref, wout_ref), (win, wout)

        far = [(o, p) for o in range(slices) for p in range(2) if o or p]

        def piece(z, p, cc, xx):
            start = (z * 2 + (at.y ^ p)) * bt + cc * hb + xx * qb
            return pl.ds(pl.multiple_of(start, 16), qb)

        def pass_on(level, arr, rows, key, device):
            ref = w_bufs[arr].at[rows]
            pltpu.make_async_remote_copy(
                ref, ref, gather_send.at[level, arr], gather_recv.at[level, arr, key], device, MESH).start()

        def arrive(level, arr, rows, key):
            wait(w_bufs[arr].at[rows], gather_recv.at[level, arr, key])

        ways = [(1, at.z < slices - 1), (-1, at.z > 0)]

        def neighbour(way):
            return (at.dp, (at.z + way) * 2 + at.y)

        def gather_start(arr):
            mine = pl.ds(pl.multiple_of(core * hb + x * qb, 16), qb)
            for way, there in ways:
                @pl.when(there)
                def _():
                    pltpu.make_async_remote_copy(
                        w_refs[arr].at[mine], w_bufs[arr].at[piece(at.z, 0, core, x)],
                        gather_send.at[0, arr], gather_recv.at[0, arr, at.z], neighbour(way), MESH).start()
            pltpu.make_async_remote_copy(
                w_refs[arr].at[mine], w_bufs[arr].at[piece(at.z, 0, core, x)],
                gather_send.at[1, arr], gather_recv.at[1, arr, at.z], y_peer, MESH).start()
            pltpu.make_async_copy(
                w_refs[arr], w_bufs[arr].at[pl.ds(pl.multiple_of(at.tensor * bt, 16), bt)], load.at[arr]).start()

        def gather_two():
            for step in range(1, slices):
                for arr, (way, there) in [(arr, w) for arr in range(2) for w in ways]:
                    z = at.z - way * step

                    @pl.when((z >= 0) & (z < slices))
                    def _():
                        rows = piece(z, 0, core, x)
                        arrive(0, arr, rows, z)

                        @pl.when(there)
                        def _():
                            pass_on(0, arr, rows, z, neighbour(way))

                        pass_on(1, arr, rows, z, y_peer)
                        pass_on(2, arr, rows, 2 * z, x_peer)
                        pass_on(3, arr, rows, 4 * z, core_peer)

        def gather_three(arr):
            for o in range(slices):
                z = at.z ^ o
                rows = piece(z, 1, core, x)
                arrive(1, arr, rows, z)
                pass_on(2, arr, rows, 2 * z + 1, x_peer)
                pass_on(3, arr, rows, 4 * z + 2, core_peer)

        def gather_four(arr):
            for o, p in far:
                z = at.z ^ o
                rows = piece(z, p, core, 1 - x)
                arrive(2, arr, rows, 2 * z + p)
                pass_on(3, arr, rows, 2 * (2 * z + p) + 1, core_peer)

        def gather_last(arr):
            pltpu.make_async_copy(
                w_refs[arr], w_bufs[arr].at[pl.ds(pl.multiple_of(at.tensor * bt, 16), bt)], load.at[arr]).wait()
            for o, p in far:
                z = at.z ^ o
                for q in range(2):
                    arrive(3, arr, piece(z, p, 1 - core, 1 - x if q else x), 2 * (2 * z + p) + q)

        def gather_sent():
            for arr in range(2):
                g = w_bufs[arr]
                for step in range(slices):
                    for way, there in ways:
                        z = at.z - way * step

                        @pl.when((z >= 0) & (z < slices) & there)
                        def _():
                            wait(g.at[pl.ds(0, qb)], gather_send.at[0, arr])
                for level, quarters in ((1, slices), (2, len(far)), (3, 2 * len(far))):
                    wait(g.at[pl.ds(0, quarters * qb)], gather_send.at[level, arr])

        def vectors_start():
            rows_ref[...] = jnp.zeros_like(rows_ref)
            for i, ref in enumerate(
                (b_in_ref, b_out_ref, gain_one_ref, shift_one_ref, gain_two_ref, shift_two_ref, valid_ref)):
                rows_ref[i : i + 1, 0 : ref.shape[1]] = ref[...].astype(F32)
            pltpu.make_async_copy(rows_ref, vrows.at[pl.ds(pl.multiple_of(at.tensor * 8, 8), 8)], vec_recv.at[0]).start()
            pltpu.make_async_copy(rows_ref, drows.at[pl.ds(pl.multiple_of(at.dp * 8, 8), 8)], vec_recv.at[1]).start()
            for offset in range(1, n_tensor):
                pltpu.make_async_remote_copy(
                    rows_ref, vrows.at[pl.ds(pl.multiple_of(at.tensor * 8, 8), 8)],
                    vec_send.at[0], vec_recv.at[0], (at.dp, at.tensor ^ offset), MESH).start()
            for offset in range(1, n_dp):
                pltpu.make_async_remote_copy(
                    rows_ref, drows.at[pl.ds(pl.multiple_of(at.dp * 8, 8), 8)],
                    vec_send.at[1], vec_recv.at[1], (at.dp ^ offset, at.tensor), MESH).start()

        def vectors_arrived():
            wait(vrows.at[pl.ds(0, 8 * n_tensor)], vec_recv.at[0])
            wait(drows, vec_recv.at[1])
            wait(vrows.at[pl.ds(0, 8 * (n_tensor - 1))], vec_send.at[0])
            wait(drows.at[pl.ds(0, 8 * (n_dp - 1))], vec_send.at[1])
            turned = vrows[...].T
            for t in range(n_tensor):
                b_in_v[t * bt : (t + 1) * bt, :] = turned[0:bt, 8 * t : 8 * t + 1]
                vec[t * columns : (t + 1) * columns, :] = turned[0:columns, 8 * t + 1 : 8 * t + 6]

        gather_start(0)
        gather_start(1)
        slice_start(0)
        tables = [
            pltpu.make_async_copy(src, dst, load.at[2 + i])
            for i, (src, dst) in enumerate(((edge_ref, edge_v), (cos_ref, cos), (sin_ref, sin)))
        ]
        for move in tables:
            move.start()
        vectors_start()
        front_prefetch()

        place0 = lax.broadcasted_iota(jnp.int32, (tokens, half), 0)
        k1 = lax.broadcasted_iota(jnp.int32, (tokens, half), 1)
        place = lambda k, shift: k // 2 + k % 2 * half + shift * (half // 2)
        one_hot = lambda hit: jnp.where(hit, 1.0, 0.0).astype(BF)
        for shift in range(2):
            perm[:, shift * half : (shift + 1) * half] = one_hot(place0 == place(k1, shift))
            perm[:, (2 + shift) * half : (3 + shift) * half] = one_hot(
                (place0 == place(half - k1, shift)) & (k1 > 0))
        turn0 = lax.broadcasted_iota(jnp.int32, (half, half), 0)
        turn1 = lax.broadcasted_iota(jnp.int32, (half, half), 1)
        turn = one_hot(turn0 + turn1 == half)
        edge0 = lax.broadcasted_iota(jnp.int32, (2 * group, half), 0)
        edge1 = lax.broadcasted_iota(jnp.int32, (2 * group, half), 1)
        pick_u = one_hot((edge0 == 2 * at.g) & (edge1 == 0))
        pick_v = one_hot((edge0 == 2 * at.g + 1) & (edge1 == 0))
        e_send[...] = jnp.zeros_like(e_send)
        A, B = parts
        block = 256
        step = 32

        def over(rows, size, body, carry=None, unroll=2):
            def inner(i, c):
                r = pl.ds(pl.multiple_of(i * size, size), size)
                return body(r, c)
            return lax.fori_loop(0, rows // size, inner, carry, unroll=unroll)

        def fold(v):
            return jnp.sum(v.reshape(v.shape[0] // 8, 8, v.shape[1]), axis=0)

        def lane_fold(v):
            return sum(v[:, k * 128 : (k + 1) * 128] for k in range(v.shape[1] // 128))

        zeros8 = jnp.zeros((8, tokens), F32)

        def mean_of(total):
            return jnp.sum(total, axis=0, keepdims=True) / width

        def statistics(ref):
            total = over(width, step, lambda r, c: c + fold(ref[r, :]), zeros8)
            center = mean_of(total)
            def spread(r, c):
                off = ref[r, :] - center
                return c + fold(off * off)
            var = mean_of(over(width, step, spread, zeros8))
            return center, lax.rsqrt(var + EPSILON)

        bacc[...] = jnp.zeros_like(bacc)
        vacc[...] = jnp.zeros_like(vacc)

        def forward_mix(j):
            tokens_arrived(j)
            for b in range(n_tensor):
                r = pl.ds(b * columns, columns)
                e = eb[j, b * er : (b + 1) * er, 0:columns]
                all_four = dot(ub[j, r, :], perm[...], 1, 0)
                ub[j, r, :] = all_four[:, : 2 * half].astype(BF)
                tile[r, A] = (all_four[:, 2 * half : 3 * half] + dot(e, pick_u, 0, 0)).astype(BF)
                tile[r, B] = (all_four[:, 3 * half :] + dot(e, pick_v, 0, 0)).astype(BF)
            def mixed(r, c):
                f1[r, A] = xb[j, r, A].astype(F32) + mix_scale * (
                    dot(cos[r, :], ub[j, :, A], 1, 0) - dot(sin[r, :], ub[j, :, B], 1, 0))
                f1[r, B] = xb[j, r, B].astype(F32) + mix_scale * (
                    dot(cos[r, :], tile[:, A], 1, 0) + dot(sin[r, :], tile[:, B], 1, 0))
                return c
            over(width, block, mixed, 0, unroll=1)
            center, inverse = statistics(f1)
            def scale(r, c):
                h = (f1[r, :] - center) * inverse
                f1[r, :] = h
                n = h * vec[r, 1:2] + vec[r, 2:3]
                f2[r, :] = n
                nl[r, own(j)] = n.astype(BF)
                return c
            over(width, step, scale, 0)
            return inverse

        c0 = math.sqrt(2.0 / math.pi)
        c1 = c0 * 0.044715

        def forward_mlp(j):
            def inner(r, c):
                v = dot(win[r, :], nl[:, own(j)], 1, 0) + b_in_v[r, :]
                v2 = v * v
                p = 0.5 + 0.5 * jnp.tanh(v * (c0 + c1 * v2))
                a = v * p
                a_all[r, own(j)] = a.astype(BF)
                m_all[r, own(j)] = (p + a * (1.0 - p) * (2.0 * c0 + 6.0 * c1 * v2)).astype(BF)
                return c
            over(units, block, inner, 0, unroll=1)
            def outer(r, c):
                f2[r, :] = f2[r, :] + dot(wout[:, r], a_all[:, own(j)], 0, 0) + vec[r, 0:1]
                return c
            for k in range(width // block):
                outer(pl.ds(k * block, block), 0)

        def second_norm(j):
            center, inverse = statistics(f2)
            flag = drows[pl.ds(pl.multiple_of(at.dp_from(j) * 8, 8), 8), 0:128][6:7, j : j + 1]
            def result(r, c):
                h = (f2[r, :] - center) * inverse
                f2[r, :] = h
                ab[j, r, :] = (h * vec[r, 3:4] + vec[r, 4:5]).astype(BF)
                return c
            over(width, step, result, 0)
            act_start(j)
            wait(cb.at[pl.ds(j * width, width)], cot_recv.at[j])
            def sums(r, c):
                go = cb[pl.ds(pl.multiple_of(j * width + r.start, 16), r.size), :].astype(F32) * flag
                h = f2[r, :]
                goh = go * h
                vacc[3, r, :] += lane_fold(goh)
                vacc[4, r, :] += lane_fold(go)
                gh = go * vec[r, 3:4]
                return c[0] + fold(gh), c[1] + fold(gh * h)
            m1, m2 = over(width, step, sums, (zeros8, zeros8))
            m1, m2 = mean_of(m1), mean_of(m2)
            def back(r, c):
                gh = cb[pl.ds(pl.multiple_of(j * width + r.start, 16), r.size), :].astype(F32) * flag * vec[r, 3:4]
                gs = inverse * (gh - m1 - f2[r, :] * m2)
                vacc[0, r, :] += lane_fold(gs)
                f3[r, :] = gs
                gl[r, own(j)] = gs.astype(BF)
                return c
            over(width, step, back, 0)

        def backward_inner(j):
            def inner(r, c):
                gi = dot(wout[r, :], gl[:, own(j)], 1, 0) * m_all[r, own(j)].astype(F32)
                bacc[r, :] += lane_fold(gi)
                m_all[r, own(j)] = gi.astype(BF)
                return c
            over(units, block, inner, 0, unroll=1)

        def backward_outer(j):
            for k in range(width // block):
                r = pl.ds(k * block, block)
                f3[r, :] = f3[r, :] + dot(win[:, r], m_all[:, own(j)], 0, 0)

        def first_back(j, inverse):
            def sums(r, c):
                gn = f3[r, :]
                h = f1[r, :]
                gnh = gn * h
                vacc[1, r, :] += lane_fold(gnh)
                vacc[2, r, :] += lane_fold(gn)
                gh = gn * vec[r, 1:2]
                return c[0] + fold(gh), c[1] + fold(gh * h)
            m1, m2 = over(width, step, sums, (zeros8, zeros8))
            m1, m2 = mean_of(m1), mean_of(m2)
            def back(r, c):
                gf = inverse * (f3[r, :] * vec[r, 1:2] - m1 - f1[r, :] * m2)
                xb[j, r, :] = gf.astype(BF)
                tile[r, :] = (gf * mix_scale).astype(BF)
                return c
            over(width, step, back, 0)
            def fold_pairs(r, c):
                a = tile[r, A].astype(F32)
                b = tile[r, B]
                t = dot(b, turn, 1, 0)
                ub[j, r, A] = (t + a).astype(BF)
                ub[j, r, B] = (t - a).astype(BF)
                return c
            over(width, block, fold_pairs, 0, unroll=1)
            edge = dot(pick_u + pick_v, tile[:, B], 1, 1).astype(BF)
            is_cos = lax.broadcasted_iota(jnp.int32, (er, columns), 0) % 2 == 0
            for b in range(n_tensor):
                r = pl.ds(b * columns, columns)
                eb[j, b * er : (b + 1) * er, 0:columns] = jnp.where(
                    is_cos, dot(edge, cos[r, :], 1, 1), dot(edge, sin[r, :], 1, 1)).astype(BF)
            for k in range(width // block):
                r = pl.ds(k * block, block)
                tile[r, A] = dot(cos[r, :], ub[j, :, A], 1, 0).astype(BF)
                tile[r, B] = dot(sin[r, :], ub[j, :, B], 1, 0).astype(BF)
            for k in range(width // block):
                r = pl.ds(k * block, block)
                ub[j, r, :] = dot(tile[r, :], perm[:, : 2 * half], 1, 1).astype(BF)
            for move in col_moves(j):
                move.start()

        grads = (wout, win)
        if seqs * tokens >= 2 * width:
            land = lambda rows, arr: a_all.at[rows, pl.ds(arr * width, width)]
        else:
            land = lambda rows, arr: spare.at[rows, pl.ds(arr * width, width)]
        at2 = n_tensor * hb
        at3 = at2 + slices * hb
        at4 = at3 + slices * qb
        at5 = at4 + (slices - 1) * qb
        land1 = lambda arr, k: land(pl.ds(pl.multiple_of(k * hb, 16), hb), arr)
        land3 = lambda arr, k: land(pl.ds(at3 + k * qb, qb), arr)
        land4 = lambda arr, k: land(pl.ds(at4 + k * qb, qb), arr)
        land5 = lambda arr: land(pl.ds(at5, qb), arr)
        def block_at(k):
            y = jnp.where(k < slices, 1 - at.y, at.y)
            return (k % slices) * 2 + y
        def rows_half(k, c):
            return pl.ds(pl.multiple_of(block_at(k) * bt + c * hb, 16), hb)
        def rows_quarter(k, xx):
            return pl.ds(pl.multiple_of(block_at(k) * bt + core * hb + xx * qb, 16), qb)

        def send(src, dst, level, arr, k, device):
            pltpu.make_async_remote_copy(
                src, dst, rs_send.at[level, arr], rs_recv.at[level, arr, k], device, MESH).start()

        def ready_signal():
            for i, device in enumerate([core_peer, x_peer, y_peer] + [z_peer(o) for o in range(1, slices)]
                                       + [flip(1 << b) for b in range(2, n_dp.bit_length() - 1)]):
                pl.semaphore_signal(ready.at[i], inc=1, device_id=device, device_id_type=MESH)

        def ready_wait(i):
            pl.semaphore_wait(ready.at[i], 1)

        def weight_grads(arr, left, right):
            def tile_step(k, c):
                r = pl.ds(pl.multiple_of(block_at(k) * bt, 16), bt)
                grads[arr][r, :] = dot(left[r, :], right[...], 1, 1).astype(BF)
                return c
            lax.fori_loop(0, n_tensor, tile_step, 0)

        def level1(arr):
            def go(k, c):
                send(grads[arr].at[rows_half(k, 1 - core)], land1(arr, k), 0, arr, k, core_peer)
                return c
            lax.fori_loop(0, n_tensor, go, 0)

        def add(arr, rows, landed, level, k):
            wait(landed, rs_recv.at[level, arr, k])
            ref = grads[arr].at[rows]
            n = ref.shape[0]
            def go(i, c):
                r = pl.ds(pl.multiple_of(i * 16, 16), 16)
                ref[r, :] = (ref[r, :].astype(F32) + landed[r, :].astype(F32)).astype(BF)
                return c
            lax.fori_loop(0, n // 16, go, 0, unroll=2)

        def y_first(arr, z):
            return arr == 1 and z >= slices // 2

        def land2_x(arr, z, own_y):
            return land(pl.ds(at2 + z * hb + (qb if own_y else 0), qb), arr)

        def land2_y(arr, z):
            return land(pl.ds(at2 + z * hb, hb), arr)

        def after1(arr):
            for k in range(n_tensor):
                z, own_y = k % slices, k >= slices
                add(arr, rows_half(k, core), land1(arr, k), 0, k)
                if not y_first(arr, z):
                    send(grads[arr].at[rows_quarter(k, 1 - x)], land2_x(arr, z, own_y), 1, arr, k, x_peer)
                elif not own_y:
                    send(grads[arr].at[rows_half(k, core)], land2_y(arr, z), 1, arr, k, y_peer)

        def after2(arr):
            for z in range(slices):
                if y_first(arr, z):
                    add(arr, rows_half(slices + z, core), land2_y(arr, z), 1, z)
                    send(grads[arr].at[rows_quarter(slices + z, 1 - x)], land3(arr, z), 2, arr, z, x_peer)
                else:
                    add(arr, rows_quarter(z, x), land2_x(arr, z, False), 1, z)
                    send(grads[arr].at[rows_quarter(z, x)], land3(arr, z), 2, arr, z, y_peer)
            for z in range(slices):
                if not y_first(arr, z):
                    add(arr, rows_quarter(slices + z, x), land2_x(arr, z, True), 1, slices + z)

        bits = [1 << b for b in range(slices.bit_length() - 1)]
        first_slot = lambda bit: slices - slices // bit

        def after3(arr):
            for z in range(slices):
                add(arr, rows_quarter(slices + z, x), land3(arr, z), 2, z)
            z_send(arr, 1)

        def z_send(arr, bit):
            for i in range(slices // (2 * bit)):
                block_z = at.z ^ (bit + 2 * bit * i)
                send(grads[arr].at[rows_quarter(slices + block_z, x)], land4(arr, first_slot(bit) + i), 3, arr,
                     first_slot(bit) + i, z_peer(bit))

        def z_add(arr, bit):
            for i in range(slices // (2 * bit)):
                add(arr, rows_quarter(slices + (at.z ^ (2 * bit * i)), x), land4(arr, first_slot(bit) + i), 3,
                    first_slot(bit) + i)

        def z_turn(arr):
            for bit in bits[:-1]:
                z_add(arr, bit)
                z_send(arr, 2 * bit)

        def after4(arr):
            mine = rows_quarter(slices + at.z, x)
            z_add(arr, bits[-1])
            for b in range(2, n_dp.bit_length() - 1):
                k = b - 2
                peer_ = flip(1 << b)
                pltpu.make_async_remote_copy(
                    grads[arr].at[mine], land5(arr), more_send.at[arr, k], more_recv.at[arr, k], peer_, MESH).start()
                wait(grads[arr].at[mine], more_send.at[arr, k])
                wait(land5(arr), more_recv.at[arr, k])
                ref = grads[arr].at[mine]
                ref[...] = (ref[...].astype(F32) + land5(arr)[...].astype(F32)).astype(BF)
                if b + 1 < n_dp.bit_length() - 1:
                    pl.semaphore_signal(more_free, inc=1, device_id=peer_, device_id_type=MESH)
                    pl.semaphore_wait(more_free, 1)
            home = pl.ds(pl.multiple_of(core * hb + x * qb, 16), qb)
            out = (gout_o, gin_o)[arr]
            pltpu.make_async_copy(grads[arr].at[mine], out.at[home], rs_recv.at[4, arr, 0]).start()
            for q in range(1, 3):
                pltpu.make_async_remote_copy(
                    grads[arr].at[mine], out.at[home], rs_send.at[4, arr], rs_recv.at[4, arr, q], flip(q), MESH).start()

        def after5(arr):
            out = (gout_o, gin_o)[arr]
            came = out.at[pl.ds(pl.multiple_of(core * hb + (1 - x) * qb, 16), qb)]
            wait(came, rs_recv.at[4, arr, 2])
            pltpu.make_async_remote_copy(came, came, rs_send.at[4, arr], rs_recv.at[4, arr, 3], core_peer, MESH).start()

        def rs_finish(arr):
            g = grads[arr]
            n = n_tensor * hb
            wait(g.at[pl.ds(0, n)], rs_send.at[0, arr])
            wait(g.at[pl.ds(0, slices * hb)], rs_send.at[1, arr])
            wait(g.at[pl.ds(0, slices * qb)], rs_send.at[2, arr])
            wait(g.at[pl.ds(0, (slices - 1) * qb)], rs_send.at[3, arr])
            wait(g.at[pl.ds(0, 3 * qb)], rs_send.at[4, arr])
            for q in (0, 1, 3):
                wait((gout_o, gin_o)[arr].at[pl.ds(0, qb)], rs_recv.at[4, arr, q])

        def table_start(i):
            c, g = i // group, i % group
            return pltpu.make_async_copy(table_rows(c, g), slot_at(i), table_sem.at[i % n_slots])

        def back_prefetch():
            for i in range(n_slots):
                table_start(i).start()

        def words_back(js, acc):
            m = len(js) * columns
            base = js[0] * width
            n_edge = len(js) * er
            some = pl.ds(js[0] * columns, m)
            some_edges = pl.ds(js[0] * er, n_edge)
            for j in js:
                col_arrived(j)
                act_sent(j)
            for g in range(group):
                pltpu.make_async_copy(gu_o.at[g, some], cb.at[pl.ds(base + g * m, m)], table_sem.at[n_slots]).start()
                pltpu.make_async_copy(
                    ge_o.at[g, some_edges], tile.at[pl.ds(g * n_edge, n_edge), pl.ds(0, 128)],
                    table_sem.at[n_slots + 1]).start()
            for j in js:
                for k in range(n_pieces):
                    pltpu.make_async_copy(
                        gf_o.at[j, :, pl.ds(k * tokens, tokens)], ab.at[j, pl.ds(k * columns, columns)],
                        table_sem.at[n_slots + 2]).start()
            wait(cb.at[pl.ds(base, group * m)], table_sem.at[n_slots])
            wait(tile.at[pl.ds(0, group * n_edge), pl.ds(0, 128)], table_sem.at[n_slots + 1])
            for j in js:
                wait(ab.at[j], table_sem.at[n_slots + 2])
            edges = tile[0:n_edge, 0:128].astype(F32)
            for g in range(1, group):
                edges = edges + tile[g * n_edge : (g + 1) * n_edge, 0:128].astype(F32)
            edges = edges.astype(BF)
            for c in range(n_chunks):
                for g in range(group):
                    i = c * group + g
                    table_start(i).wait()
                    for s_ in range(per):
                        t = slot_at(i)[pl.ds(s_ * tokens, tokens), :]
                        left = cb[base + g * m : base + (g + 1) * m, :]
                        even = dot(left[:, :half], t[:, :half], 1, 1)
                        odd = dot(left[:, half:], t[:, half:], 1, 1)
                        at_even = pl.ds(s_ * m, m)
                        at_odd = pl.ds((per + s_) * m, m)
                        if g:
                            acc[at_even, :] += even
                            acc[at_odd, :] += odd
                        else:
                            acc[at_even, :] = even
                            acc[at_odd, :] = odd
                    if i + n_slots < n_chunks * group:
                        table_start(i + n_slots).start()
                for s_ in range(per):
                    for sign in range(2):
                        k = c * per + s_ + sign * (n_pieces // 2)
                        for n, j in enumerate(js):
                            rows = pl.ds(k * columns, columns)
                            even = acc[pl.ds(s_ * m + n * columns, columns), :]
                            odd = acc[pl.ds((per + s_) * m + n * columns, columns), :]
                            edge = dot(edges[n * er : (n + 1) * er, 0:columns], edge_v[:, k * tokens : (k + 1) * tokens], 0, 0)
                            both = even - odd if sign else even + odd
                            ab[j, rows, :] = (both + edge + ab[j, rows, :].astype(F32)).astype(BF)
                            home_start(j, k)

        def home_at(j):
            dp = at.dp_from(j)
            return dp, jnp.logical_and(dp == at.dp, at.block == at.tensor)

        def home_start(j, k):
            dp, here = home_at(j)
            src = ab.at[j, pl.ds(k * columns, columns)]
            dst = gw_o.at[j, :, pl.ds(k * tokens, tokens)]

            @pl.when(here)
            def _():
                pltpu.make_async_copy(src, dst, home_recv.at[j]).start()

            @pl.when(jnp.logical_not(here))
            def _():
                pltpu.make_async_remote_copy(src, dst, home_send.at[j], home_recv.at[j], (dp, at.block), MESH).start()

        def home_finish(j):
            dp, here = home_at(j)

            @pl.when(jnp.logical_not(here))
            def _():
                wait(gw_o.at[j], home_send.at[j])

            wait(gw_o.at[j], home_recv.at[j])

        def vector_grads():
            cols = pl.ds(0, 128)
            vrows[...] = jnp.zeros_like(vrows)
            turned = jnp.zeros((wide, 128), F32)
            scratch = f1.at[pl.ds(0, wide), cols]
            scratch[...] = turned
            for t in range(n_tensor):
                scratch[0:bt, 8 * t : 8 * t + 1] = jnp.sum(bacc[t * bt : (t + 1) * bt, :], axis=1, keepdims=True)
                for i in range(5):
                    scratch[0:columns, 8 * t + 1 + i : 8 * t + 2 + i] = jnp.sum(
                        vacc[i, t * columns : (t + 1) * columns, :], axis=1, keepdims=True)
            vrows[...] = scratch[...].T
            n = 8 * n_tensor
            for offset in range(1, n_dp):
                pltpu.make_async_remote_copy(
                    vrows.at[pl.ds(0, n)], grows.at[pl.ds((offset - 1) * n, n)],
                    vg_send.at[0], vg_recv.at[0], (at.dp ^ offset, at.tensor), MESH).start()

        def vector_grads_two():
            n = 8 * n_tensor
            wait(grows.at[pl.ds(0, (n_dp - 1) * n)], vg_recv.at[0])
            wait(grows.at[pl.ds(0, (n_dp - 1) * n)], vg_send.at[0])
            total = vrows[0:n, :]
            for offset in range(1, n_dp):
                total = total + grows[(offset - 1) * n : offset * n, :]
            vrows[0:n, :] = total
            for offset in range(1, n_tensor):
                t = at.tensor ^ offset
                pltpu.make_async_remote_copy(
                    vrows.at[pl.ds(pl.multiple_of(t * 8, 8), 8)], drows2.at[pl.ds((offset - 1) * 8, 8)],
                    vg_send.at[1], vg_recv.at[1], (at.dp, t), MESH).start()

        def vector_grads_three():
            n = 8 * (n_tensor - 1)
            wait(drows2.at[pl.ds(0, n)], vg_recv.at[1])
            wait(drows2.at[pl.ds(0, n)], vg_send.at[1])
            total = vrows[pl.ds(pl.multiple_of(at.tensor * 8, 8), 8), :]
            for offset in range(1, n_tensor):
                total = total + drows2[(offset - 1) * 8 : offset * 8, :]
            vec_o[...] = total

        gather_two()
        slice_start(1)
        for move in tables:
            move.wait()
        wait(a_all.at[pl.ds(0, width), two], slice_recv.at[0])
        for j in range(2, seqs):
            slice_start(j)
        cot_start(0)
        front_pass([0], 1)
        front_prefetch()
        gather_three(0)
        gather_three(1)
        vectors_arrived()
        gather_four(0)
        for i in range(1, seqs):
            wait(a_all.at[pl.ds(i * width, width), two], slice_recv.at[i])
        front_pass(list(range(1, seqs)), 1)
        back_prefetch()
        gather_four(1)
        inverse = forward_mix(0)
        for arr in range(2):
            gather_last(arr)
        cot_start(1)
        last = seqs - 1
        for j in range(seqs):
            if j:
                inverse = forward_mix(j)
            if j == last:
                for i in range(seqs):
                    tokens_sent(i)
            forward_mlp(j)
            if 0 < j and j + 1 < seqs:
                cot_start(j + 1)
            if j == last:
                words_back([0], f3)
                back_prefetch()
            second_norm(j)
            backward_inner(j)
            if j + 2 < seqs:
                later_tokens(j + 2)
            backward_outer(j)
            first_back(j, inverse)
        gather_sent()
        weight_grads(0, a_all, gl)
        ready_signal()
        ready_wait(0)
        level1(0)
        weight_grads(1, m_all, nl)
        level1(1)
        ready_wait(1)
        after1(0)
        vector_grads()
        ready_wait(2)
        after1(1)
        for j in range(1, last):
            words_back([j], f2)
            back_prefetch()
        after2(0)
        words_back([last], f2)
        for i in range(3, 3 + slices - 1 + max(0, n_dp.bit_length() - 3)):
            ready_wait(i)
        after3(0)
        after2(1)
        z_turn(0)
        after3(1)
        z_turn(1)
        vector_grads_two()
        after4(0)
        after4(1)
        vector_grads_three()
        after5(0)
        after5(1)
        for j in range(seqs):
            slice_finish(j)
            cot_finish(j)
            col_finish(j)
            home_finish(j)
        rs_finish(0)
        rs_finish(1)


    shape = jax.ShapeDtypeStruct
    dma = pltpu.SemaphoreType.DMA
    whole_vmem = pl.BlockSpec(memory_space=pltpu.VMEM)
    depth = min(1024, length // 2)
    need_spare = seqs * tokens < 2 * width
    regular = pltpu.SemaphoreType.REGULAR
    activations, _, _, _, gw, g_in, g_out, vec_g = pl.pallas_call(
        layer_body,
        out_shape=[
            shape(words.shape, BF),
            shape((group, seqs * columns, tokens), BF),
            shape((group, seqs * 2 * group, 128), BF),
            shape((seqs, columns, length), BF),
            shape((seqs, columns, length), BF),
            shape(w_in.shape, BF),
            shape(w_in.shape, BF),
            shape((8, wide), F32),
        ],
        in_specs=[ANY] * 8 + [whole_vmem] * 7,
        out_specs=[ANY] * 7 + [whole_vmem],
        scratch_shapes=[
            pltpu.VMEM((units, width), BF),
            pltpu.VMEM((units, width), BF),
            pltpu.VMEM((width, width), BF),
            pltpu.VMEM((width, width), BF),
            pltpu.VMEM((seqs, width, tokens), BF),
            pltpu.VMEM((seqs, width, tokens), BF),
            pltpu.VMEM((seqs, n_tensor * 2 * group, 128), BF),
            pltpu.VMEM((group * seqs * columns, tokens), BF),
            pltpu.VMEM((seqs, width, tokens), BF),
            pltpu.VMEM((units, seqs * tokens), BF),
            pltpu.VMEM((units, seqs * tokens), BF),
            pltpu.VMEM((width, seqs * tokens), BF),
            pltpu.VMEM((width, seqs * tokens), BF),
            pltpu.VMEM((3 * width, tokens), F32),
            pltpu.VMEM((width, tokens), BF),
            pltpu.VMEM((2 * group, length), BF),
            pltpu.VMEM((n_slots * depth, tokens), BF),
            pltpu.VMEM((tokens, 4 * half), BF),
            pltpu.VMEM((seqs * 2 * group, 128), BF),
            pltpu.VMEM((8, wide), F32),
            pltpu.VMEM((units, 128), F32),
            pltpu.VMEM((5, width, 128), F32),
            pltpu.VMEM((units, 1), F32),
            pltpu.VMEM((width, 5), F32),
            pltpu.VMEM((128, wide), F32),
            pltpu.VMEM((8 * n_dp, wide), F32),
            pltpu.VMEM((8 * n_tensor * (n_dp - 1), wide), F32),
            pltpu.VMEM((8 * (n_tensor - 1), wide), F32),
            pltpu.VMEM((units, 2 * width) if need_spare else (16, 128), BF),
            dma((5,)),
            dma((seqs,)),
            dma((seqs,)),
            dma((seqs, 3)),
            dma((seqs, 3)),
            dma((2,)),
            dma((2,)),
            dma((4, 2)),
            dma((4, 2, 2 * n_tensor)),
            dma((seqs,)),
            dma((seqs,)),
            dma((seqs,)),
            dma((seqs,)),
            dma((seqs,)),
            dma((seqs,)),
            dma((seqs, 3)),
            dma((seqs, 3)),
            regular((3 + n_tensor // 2 + n_dp,)),
            dma((5, 2)),
            dma((5, 2, n_tensor)),
            dma((n_slots + 3,)),
            dma((seqs,)),
            dma((seqs,)),
            dma((2, n_dp)),
            dma((2, n_dp)),
            regular,
            dma((2,)),
            dma((2,)),
        ],
        compiler_params=pltpu.CompilerParams(
            collective_id=1, has_side_effects=True, vmem_limit_bytes=64 * 1024 * 1024
        ),
    )(
        words, cotangent, w_in, w_out, jnp.asarray(hid_cos), jnp.asarray(hid_sin), table, edge_table,
        *[v[None] for v in (b_in, b_out, gain_one, shift_one, gain_two, shift_two, valid)],
    )
    grad_words = gw.astype(F32)

    grad_w_in = g_in.astype(F32)
    grad_w_out = g_out.astype(F32)
    return (
        activations,
        grad_words,
        grad_w_in,
        vec_g[0, : w_in.shape[0]],
        grad_w_out,
        vec_g[1, :columns],
        vec_g[2, :columns],
        vec_g[3, :columns],
        vec_g[4, :columns],
        vec_g[5, :columns],
    )


def solution(mesh):
    spec = (
        P("dp", "tensor", None),
        P("tensor", None),
        P("tensor"),
        P("tensor", None),
        P("tensor"),
        P("tensor"),
        P("tensor"),
        P("tensor"),
        P("tensor"),
        P("dp", "tensor", None),
        P("dp"),
    )
    out = (
        P("dp", "tensor", None),
        P("dp", "tensor", None),
        P("tensor", None),
        P("tensor"),
        P("tensor", None),
        P("tensor"),
        P("tensor"),
        P("tensor"),
        P("tensor"),
        P("tensor"),
    )
    return jax.shard_map(on_device, mesh=mesh, in_specs=spec, out_specs=out, check_vma=False)
```
